256 devices in a mesh: angle: 2 (over y_hi), grid: 2 (over y_lo), slab: 64 (over x, z, core).
Axes of the slice: x: 4, y: 4 (y_hi: 2, y_lo: 2; y = y_hi * 2 + y_lo), z: 8, core: 2. Of those that a mesh axis runs over, the one named last changes fastest.
Arguments:
- efield: float32 [2, 6, 192, 24, 384], P('grid', 'angle', 'slab'), parts along dimension 1, may hold values from -6 to 6
- hfield: float32 [2, 6, 192, 24, 384], P('grid', 'angle', 'slab'), parts along dimension 1, may hold values from -6 to 6
- polar: float32 [2, 6, 192, 24, 384], P('grid', 'angle', 'slab'), parts along dimension 1, may hold values from -3 to 3
- current: float32 [2, 6, 192, 24, 384], P('grid', 'angle', 'slab'), parts along dimension 1, may hold values from -3 to 3
- material: int32 [2, 192, 24, 384], P('grid', 'slab'), may hold values from 0 to 3
- box_offset: int32 [2], replicated, may hold values from 0 to 256, as said below
Outputs:
- efield_final: float32 [2, 6, 192, 24, 384], P('grid', 'angle', 'slab'), parts along dimension 1
- hfield_final: float32 [2, 6, 192, 24, 384], P('grid', 'angle', 'slab'), parts along dimension 1
- polar_final: float32 [2, 6, 192, 24, 384], P('grid', 'angle', 'slab'), parts along dimension 1
- current_final: float32 [2, 6, 192, 24, 384], P('grid', 'angle', 'slab'), parts along dimension 1
The draws below stay inside these ranges and needn't reach their ends.
There are 2 independent parts, one for each index of `angle`. The reference program is written for one: setup_inputs(seed, part) draws one part's arguments, and reference() takes and returns one part's arrays. A program takes and returns all parts, laid end to end along the dimension named above; an argument that names none is the same for every part. Nothing has to cross between parts.
Inputs may be any that keep to these rules, and one draw needn't show every extreme that they name: `box_offset`: entry 0 lies in 0 to 16; entry 1 is 256, so that the box lies inside the coarse grid and reaches its last z cells.
All inputs are finite; a program needn't handle non-finite values.
Results may differ from the reference program's by a relative error of at most 0.0001.
Values sent between devices are 32-bit elements; how exact they have to be, the bound alone decides.
A program may use at most 64 MiB of HBM per device.

```python
import jax
import jax.numpy as jnp
from jax import lax

CX = 3
CY = 24
CZ = 384
STEPS = 3
NX = 192
N_SLAB = 64


def draw_box_offset(key, part):
    key = jax.random.fold_in(key, 11)
    corner_y = jax.random.randint(key, (), 0, CY - CY // 3 + 1)
    corner_z = jnp.int32(CZ - CZ // 3)
    return jnp.stack([corner_y.astype(jnp.int32), corner_z]).astype(jnp.int32)


def plant(drawn, stream_key, least, largest):
    longest = drawn.shape.index(max(drawn.shape))
    spots = []
    for shift in (0, 1):
        where = [jax.random.randint(jax.random.fold_in(stream_key, axis), (), 0, length) for axis, length in enumerate(drawn.shape)]
        where[longest] = (where[longest] + shift) % drawn.shape[longest]
        spots.append(tuple(where))
    return drawn.at[spots[0]].set(least).at[spots[1]].set(largest)


def block_levels(rng, extent, pieces, smallest, top_value):
    def one(axis_at, blocks):
        draws = jax.random.uniform(jax.random.fold_in(jax.random.fold_in(rng, 6), axis_at), (blocks,), jnp.float32, smallest / len(pieces), top_value / len(pieces))
        return jnp.repeat(jnp.exp(draws), extent[axis_at] // blocks).reshape((-1,) + (1,) * (len(extent) - axis_at - 1))

    factor_of = one(*pieces[0])
    for cut in pieces[1:]:
        factor_of = factor_of * one(*cut)
    return factor_of


def centred(key, shape, scale, bound, split=(), kind=jnp.bfloat16):
    result = scale * jax.random.normal(key, shape, jnp.float32)
    if split:
        result = result * block_levels(key, shape, split, -0.22, 0.18)
    return jnp.clip(result, -bound, bound).astype(kind)


def setup_inputs(seed: int = 0, part: int = 0) -> dict:
    keys = jax.random.split(jax.random.key(seed), 7)
    part_keys = jax.random.split(jax.random.fold_in(keys[6], part), 7)
    return {
        "efield": centred(part_keys[0], (2, 3, NX, CY, CZ), 1.0, 6.0, ((0, 2), (2, 64)), jnp.float32),
        "hfield": centred(part_keys[1], (2, 3, NX, CY, CZ), 1.0, 6.0, ((0, 2), (2, 64)), jnp.float32),
        "polar": centred(part_keys[2], (2, 3, NX, CY, CZ), 0.5, 3.0, ((0, 2), (2, 64)), jnp.float32),
        "current": centred(part_keys[3], (2, 3, NX, CY, CZ), 0.5, 3.0, ((0, 2), (2, 64)), jnp.float32),
        "material": plant(jax.random.randint(keys[4], (2, NX, CY, CZ), 0, 4), jax.random.fold_in(keys[4], 1), 0, 3).astype(jnp.int32),
        "box_offset": draw_box_offset(jax.random.fold_in(keys[6], 71), part),
    }


PERMITTIVITY = (1.0, 1.5, 1.2, 2.0)
STRENGTH = (0.4, 0.9, 0.3, 1.1)
RESONANCE = (0.6, 0.5, 0.8, 0.3)
DAMPING_RATE = (0.3, 0.2, 0.05, 0.4)
COURANT = 0.5
STEP_COARSE = 0.5
STEP_FINE = STEP_COARSE / 3.0


def lookup(material, values_table):
    values = jnp.zeros(material.shape, jnp.float32)
    for material_id in range(4):
        values = values + jnp.where(material == material_id, jnp.float32(values_table[material_id]), jnp.float32(0.0))
    return values


def coefficients(material):
    return (lookup(material, PERMITTIVITY), lookup(material, STRENGTH), lookup(material, RESONANCE), lookup(material, DAMPING_RATE))


def shifted_down(field, dimension):
    widths = [(0, 0)] * field.ndim
    widths[dimension] = (1, 0)
    return lax.slice_in_dim(jnp.pad(field, widths), 0, field.shape[dimension], axis=dimension)


def shifted_up(field, dimension):
    widths = [(0, 0)] * field.ndim
    widths[dimension] = (0, 1)
    return lax.slice_in_dim(jnp.pad(field, widths), 1, field.shape[dimension] + 1, axis=dimension)


def advance(fields, material_terms, curl_scale, step_size):
    efield, hfield, polar, current = fields
    permittivity, strength, resonance, damping = material_terms
    hfield_x, hfield_y, hfield_z = hfield[0], hfield[1], hfield[2]
    curl_h = jnp.stack([(hfield_z - shifted_down(hfield_z, 1)) - (hfield_y - shifted_down(hfield_y, 2)),
                        (hfield_x - shifted_down(hfield_x, 2)) - (hfield_z - shifted_down(hfield_z, 0)),
                        (hfield_y - shifted_down(hfield_y, 0)) - (hfield_x - shifted_down(hfield_x, 1))])
    current = current + step_size * (-damping * current - resonance * polar + strength * resonance * efield)
    polar = polar + step_size * current
    efield = efield + (curl_scale * curl_h - step_size * current) / permittivity
    efield_x, efield_y, efield_z = efield[0], efield[1], efield[2]
    curl_e = jnp.stack([(shifted_up(efield_z, 1) - efield_z) - (shifted_up(efield_y, 2) - efield_y),
                        (shifted_up(efield_x, 2) - efield_x) - (shifted_up(efield_z, 0) - efield_z),
                        (shifted_up(efield_y, 0) - efield_y) - (shifted_up(efield_x, 1) - efield_x)])
    hfield = hfield - curl_scale * curl_e
    return efield, hfield, polar, current


def upsample(section):
    components, length_x, length_y, length_z = section.shape
    expanded = jnp.broadcast_to(section[:, :, None, :, None, :, None], (components, length_x, 3, length_y, 3, length_z, 3))
    return expanded.reshape(components, 3 * length_x, 3 * length_y, 3 * length_z)


def restrict(field):
    components, length_x, length_y, length_z = field.shape
    return jnp.mean(field.reshape(components, length_x // 3, 3, length_y // 3, 3, length_z // 3, 3), axis=(2, 4, 6))


def reference(efield, hfield, polar, current, material, box_offset):
    plane_fine = CX // 3
    box_x = N_SLAB * plane_fine
    box_y = CY // 3
    box_z = CZ // 3
    start_x = (N_SLAB // 8) * CX
    anchor = jnp.int32(0)
    corner_y = box_offset[0].astype(jnp.int32)
    corner_z = box_offset[1].astype(jnp.int32)
    corner = (anchor, jnp.int32(start_x), corner_y, corner_z)
    coarse_terms = coefficients(material[0])
    fine_terms = coefficients(material[1])
    coarse = (efield[0], hfield[0], polar[0], current[0])
    fine_state = (efield[1], hfield[1], polar[1], current[1])
    position_x = jnp.arange(NX, dtype=jnp.int32)[:, None, None]
    position_y = jnp.arange(CY, dtype=jnp.int32)[None, :, None]
    position_z = jnp.arange(CZ, dtype=jnp.int32)[None, None, :]
    rim_cells = ((position_x == 0) | (position_x == NX - 1) | (position_y == 0) | (position_y == CY - 1)
                 | (position_z == 0) | (position_z == CZ - 1))
    inside = ((position_x >= start_x + 1) & (position_x <= start_x + box_x - 2)
              & (position_y >= corner_y + 1) & (position_y <= corner_y + box_y - 2)
              & (position_z >= corner_z + 1) & (position_z <= corner_z + box_z - 2))

    def section(field):
        return lax.dynamic_slice(field, corner, (3, box_x, box_y, box_z))

    previous = section(coarse[0])
    latest = previous
    for step_index in range(STEPS):
        for sub_index in range(3):
            if sub_index == 0:
                coarse = advance(coarse, coarse_terms, COURANT, STEP_COARSE)
                latest = section(coarse[0])
            fine_state = advance(fine_state, fine_terms, COURANT, STEP_FINE)
            weight = (sub_index + 1) / 3.0
            boundary = upsample(previous + weight * (latest - previous))
            fine_state = (jnp.where(rim_cells, boundary, fine_state[0]),) + fine_state[1:]
        previous = latest
        placed = lax.dynamic_update_slice(jnp.zeros_like(coarse[0]), restrict(fine_state[0]), corner)
        coarse = (jnp.where(inside, placed, coarse[0]),) + coarse[1:]
    return (jnp.stack([coarse[0], fine_state[0]]), jnp.stack([coarse[1], fine_state[1]]),
            jnp.stack([coarse[2], fine_state[2]]), jnp.stack([coarse[3], fine_state[3]]))
```

```python
import functools

import jax
import jax.numpy as jnp
from jax import lax
from jax.experimental import pallas as pl
from jax.experimental.pallas import tpu as pltpu
from jax.sharding import PartitionSpec as P

STEPS = 3
SUBS = 3
PERMITTIVITY = (1.0, 1.5, 1.2, 2.0)
STRENGTH = (0.4, 0.9, 0.3, 1.1)
RESONANCE = (0.6, 0.5, 0.8, 0.3)
DAMPING_RATE = (0.3, 0.2, 0.05, 0.4)
COURANT = 0.5
STEP_COARSE = 0.5
STEP_FINE = STEP_COARSE / 3.0
PLANES = 3
MESH = pl.DeviceIdType.MESH
EXACT = lax.Precision.HIGHEST


def tables(step):
    rows = zip(PERMITTIVITY, STRENGTH, RESONANCE, DAMPING_RATE)
    return [
        (1.0 - step * d, -step * r, step * s * r, COURANT / e, step / e) for e, s, r, d in rows
    ]


def pick(material, values):
    out = jnp.full(material.shape, values[0], jnp.float32)
    for index in range(1, 4):
        out = jnp.where(material == index, jnp.float32(values[index]), out)
    return out


def iota(shape, dim):
    return lax.broadcasted_iota(jnp.int32, shape, dim)


def down_y(u):
    return jnp.where(iota(u.shape, 0) == 0, 0.0, pltpu.roll(u, 1, 0))


def up_y(u):
    last = u.shape[0] - 1
    return jnp.where(iota(u.shape, 0) == last, 0.0, pltpu.roll(u, last, 0))


def down_z(u):
    return jnp.where(iota(u.shape, 1) == 0, 0.0, pltpu.roll(u, 1, 1))


def up_z(u):
    last = u.shape[1] - 1
    return jnp.where(iota(u.shape, 1) == last, 0.0, pltpu.roll(u, last, 1))


def kernel(
    n_slab, width, depth,
    off_ref, e_in, h_in, p_in, j_in, m_in,
    e_out, h_out, p_out, j_out,
    E, H, Q, J, M, CO, C3, m_right, T,
    h_send, h_recv, b_send, b_recv,
    sec_send, sec_recv, up_prev, up_last, mean_send, mean_recv,
    load_sem, out_sem, m_send_sem, m_recv_sem,
    hs_sem, hr_sem, bs_sem, br_sem, ss_sem, sr_sem, ms_sem, mr_sem,
):
    slab = lax.axis_index("slab")
    level = lax.axis_index("grid")
    box_y, box_z = width // 3, depth // 3
    first_slab = n_slab // 8
    is_fine = level == 1
    is_coarse = level == 0
    has_left = slab > 0
    has_right = slab < n_slab - 1
    partner_slab = first_slab + slab // 3
    partner_plane = slab % 3
    fine_at = [3 * (slab - first_slab) + p for p in range(PLANES)]
    in_box = [(f >= 0) & (f < n_slab) for f in fine_at]
    on_box = [is_coarse & b for b in in_box]

    fields = ((e_in, E, e_out), (h_in, H, h_out), (p_in, Q, p_out), (j_in, J, j_out))
    loads = [
        [pltpu.make_async_copy(src.at[0, :, p], dst.at[p], load_sem.at[k, p]) for p in range(PLANES)]
        for k, (src, dst, _) in enumerate(fields)
    ]
    load_m = pltpu.make_async_copy(m_in.at[0], M, load_sem.at[4, 0])

    barrier = pltpu.get_barrier_semaphore()

    def greet(condition, target):
        @pl.when(condition)
        def _():
            pl.semaphore_signal(barrier, inc=1, device_id=target, device_id_type=MESH)

    greet(has_left, {"slab": slab - 1})
    greet(has_right, {"slab": slab + 1})
    greet(is_fine, {"grid": 0, "slab": partner_slab})
    for p in range(PLANES):
        greet(on_box[p], {"grid": 1, "slab": fine_at[p]})

    load_m.start()
    for p in range(PLANES):
        for k in range(4):
            loads[k][p].start()

    greeted = has_left.astype(jnp.int32) + has_right.astype(jnp.int32) + is_fine.astype(jnp.int32)
    for p in range(PLANES):
        greeted = greeted + on_box[p].astype(jnp.int32)

    def remote(src, dst, send, recv, target):
        return pltpu.make_async_remote_copy(
            src_ref=src, dst_ref=dst, send_sem=send, recv_sem=recv, device_id=target, device_id_type=MESH
        )

    def h_copy(slot):
        return remote(h_send.at[slot], h_recv.at[slot], hs_sem.at[slot], hr_sem.at[slot], {"slab": slab + 1})

    def b_copy(slot):
        return remote(b_send.at[slot, 0:2], b_recv.at[slot], bs_sem.at[slot], br_sem.at[slot], {"slab": slab - 1})

    m_copy = remote(m_in.at[0, 0], m_right, m_send_sem, m_recv_sem, {"slab": slab - 1})

    def section_copy(index, p):
        return remote(
            sec_send.at[index, p], sec_recv.at[index], ss_sem.at[index, p], sr_sem.at[index],
            {"grid": 1, "slab": fine_at[p]},
        )

    def section_arrival(index):
        return remote(
            sec_send.at[index, 0], sec_recv.at[index], ss_sem.at[index, 0], sr_sem.at[index],
            {"grid": 0, "slab": partner_slab},
        )

    def mean_copy(index):
        return remote(
            mean_send.at[index], mean_recv.at[index, partner_plane], ms_sem.at[index],
            mr_sem.at[index, partner_plane], {"grid": 0, "slab": partner_slab},
        )

    def mean_arrival(index, p):
        return remote(
            mean_send.at[index], mean_recv.at[index, p], ms_sem.at[index], mr_sem.at[index, p],
            {"grid": 1, "slab": fine_at[p]},
        )

    def oscillate(p):
        a_j, a_p, a_e = CO[0, p], CO[1, p], CO[2, p]
        for c in range(3):
            current = a_j * J[p, c] + a_p * Q[p, c] + a_e * E[p, c]
            J[p, c] = current

    def move(p, step):
        for c in range(3):
            Q[p, c] = Q[p, c] + step * J[p, c]

    def electric(p):
        k_c, k_j = CO[3, p], CO[4, p]
        h_x, h_y, h_z = H[p, 0], H[p, 1], H[p, 2]
        e_x = E[p, 0] - k_j * J[p, 0] + k_c * ((h_z - down_y(h_z)) - (h_y - down_z(h_y)))
        b_y = E[p, 1] - k_j * J[p, 1] + k_c * ((h_x - down_z(h_x)) - h_z)
        b_z = E[p, 2] - k_j * J[p, 2] + k_c * (h_y - (h_x - down_y(h_x)))
        return e_x, b_y, b_z

    def electric_whole(p):
        e_x, b_y, b_z = electric(p)
        k_c = CO[3, p]
        E[p, 0] = e_x
        E[p, 1] = b_y + k_c * H[p - 1, 2]
        E[p, 2] = b_z - k_c * H[p - 1, 1]

    def magnetic(p):
        e_x, e_y, e_z = E[p, 0], E[p, 1], E[p, 2]
        h_x = H[p, 0] - COURANT * ((up_y(e_z) - e_z) - (up_z(e_y) - e_y))
        g_y = H[p, 1] - COURANT * ((up_z(e_x) - e_x) + e_z)
        g_z = H[p, 2] + COURANT * (e_y + (up_y(e_x) - e_x))
        return h_x, g_y, g_z

    def magnetic_whole(p):
        h_x, g_y, g_z = magnetic(p)
        H[p, 0] = h_x
        H[p, 1] = g_y + COURANT * E[p + 1, 2]
        H[p, 2] = g_z - COURANT * E[p + 1, 1]

    def set_coefficients(step):
        load_m.wait()
        values = tables(step)
        for p in range(PLANES):
            material = M[p]
            for k in range(5):
                CO[k, p] = pick(material, [row[k] for row in values])

    def begin(step, first):
        set_coefficients(step)
        for k in range(4):
            loads[k][0].wait()
        loads[1][2].wait()
        first()
        oscillate(0)
        move(0, step)
        e_x, b_y, b_z = electric(0)
        b_send[0, 0], b_send[0, 1], b_send[0, 2] = b_y, b_z, e_x
        h_send[0, 0], h_send[0, 1] = H[2, 1], H[2, 2]

        @pl.when(jnp.logical_not(has_left))
        def _():
            h_recv[...] = jnp.zeros_like(h_recv)

        @pl.when(jnp.logical_not(has_right))
        def _():
            b_recv[...] = jnp.zeros_like(b_recv)
            m_right[...] = jnp.zeros_like(m_right)

        pl.semaphore_wait(barrier, greeted)

        @pl.when(has_right)
        def _():
            h_copy(0).start()

        @pl.when(has_left)
        def _():
            b_copy(0).start()
            m_copy.start()

    def rest_of_loads(skip):
        for k in range(4):
            for p in range(1, PLANES):
                if (k, p) != (1, 2) and k not in skip:
                    loads[k][p].wait()

    def learn_right():
        @pl.when(has_right)
        def _():
            m_copy.wait_recv()

        @pl.when(has_left)
        def _():
            m_copy.wait_send()

        scale = pick(m_right[...], [COURANT / e for e in PERMITTIVITY])
        C3[...] = scale * has_right.astype(jnp.float32)

    def hear_left(slot):
        @pl.when(has_left)
        def _():
            h_copy(slot).wait_recv()

    def hear_right(slot):
        @pl.when(has_right)
        def _():
            b_copy(slot).wait_recv()

    def sent(slot):
        @pl.when(has_right)
        def _():
            h_copy(slot).wait_send()

        @pl.when(has_left)
        def _():
            b_copy(slot).wait_send()

    def last_plane(slot):
        h_x, g_y, g_z = magnetic(2)
        e_y = b_recv[slot, 0] + C3[...] * h_send[slot, 1]
        e_z = b_recv[slot, 1] - C3[...] * h_send[slot, 0]
        H[2, 0] = h_x
        H[2, 1] = g_y + COURANT * e_z
        H[2, 2] = g_z - COURANT * e_y

    def first_plane(slot):
        k_c = CO[3, 0]
        E[0, 0] = b_send[slot, 2]
        E[0, 1] = b_send[slot, 0] + k_c * h_recv[slot, 1]
        E[0, 2] = b_send[slot, 1] - k_c * h_recv[slot, 0]

    def tell_right(slot):
        h_send[slot, 0], h_send[slot, 1] = H[2, 1], H[2, 2]

        @pl.when(has_right)
        def _():
            h_copy(slot).start()

    def tell_left(slot, step):
        oscillate(0)
        move(0, step)
        e_x, b_y, b_z = electric(0)
        b_send[slot, 0], b_send[slot, 1], b_send[slot, 2] = b_y, b_z, e_x

        @pl.when(has_left)
        def _():
            b_copy(slot).start()

    def rim(p):
        row, column = iota((width, depth), 0), iota((width, depth), 1)
        edge = (row == 0) | (row == width - 1) | (column == 0) | (column == depth - 1)
        if p == 0:
            edge = edge | (slab == 0)
        if p == PLANES - 1:
            edge = edge | (slab == n_slab - 1)
        return edge

    def upsampled(index):
        section = sec_recv[index].reshape(3 * box_y, box_z)
        spread_z = (iota((box_z, depth), 1) // 3 == iota((box_z, depth), 0)).astype(jnp.float32)
        spread_y = (iota((3 * width, 3 * box_y), 0) // 3 == iota((3 * width, 3 * box_y), 1)).astype(jnp.float32)
        wide = jnp.dot(section, spread_z, precision=EXACT, preferred_element_type=jnp.float32)
        return jnp.dot(spread_y, wide, precision=EXACT, preferred_element_type=jnp.float32)

    def average():
        total = [E[0, c] + E[1, c] + E[2, c] for c in range(3)]
        total = jnp.concatenate(total, axis=0)
        fold_z = (iota((depth, box_z), 0) // 3 == iota((depth, box_z), 1)).astype(jnp.float32)
        fold_y = (iota((3 * box_y, 3 * width), 1) // 3 == iota((3 * box_y, 3 * width), 0)).astype(jnp.float32)
        rows = jnp.dot(fold_y, total, precision=EXACT, preferred_element_type=jnp.float32)
        both = jnp.dot(rows, fold_z, precision=EXACT, preferred_element_type=jnp.float32)
        return both * jnp.float32(1.0 / 27.0)

    def write(k):
        for p in range(PLANES):
            pltpu.make_async_copy(fields[k][1].at[p], fields[k][2].at[0, :, p], out_sem.at[k, p]).start()

    def written():
        for k in range(4):
            for p in range(PLANES):
                pltpu.make_async_copy(fields[k][1].at[p], fields[k][2].at[0, :, p], out_sem.at[k, p]).wait()

    @pl.when(is_fine)
    def _():
        begin(STEP_FINE, lambda: None)
        rest_of_loads(())
        total_subs = STEPS * SUBS

        def sub_step(m, carry):
            step_index = m // SUBS
            sub_index = m % SUBS
            slot = m % 2
            for p in (1, 2):
                oscillate(p)
                move(p, STEP_FINE)
            electric_whole(2)
            electric_whole(1)
            magnetic_whole(1)

            @pl.when(m == 0)
            def _():
                learn_right()

            hear_right(slot)
            last_plane(slot)

            @pl.when(m < total_subs - 1)
            def _():
                tell_right(1 - slot)

            hear_left(slot)
            first_plane(slot)
            magnetic_whole(0)
            sent(slot)

            @pl.when(m == 0)
            def _():
                section_arrival(0).wait_recv()
                up_last[...] = upsampled(0).reshape(up_last.shape)

            @pl.when(sub_index == 0)
            def _():
                up_prev[...] = up_last[...]
                section_arrival(step_index + 1).wait_recv()
                up_last[...] = upsampled(step_index + 1).reshape(up_last.shape)

            weight = (sub_index + 1).astype(jnp.float32) * jnp.float32(1.0 / 3.0)
            for c in range(3):
                before = up_prev[c]
                boundary = before + weight * (up_last[c] - before)
                for p in range(PLANES):
                    E[p, c] = jnp.where(rim(p), boundary, E[p, c])

            @pl.when(m < total_subs - 1)
            def _():
                tell_left(1 - slot, STEP_FINE)

            @pl.when(sub_index == SUBS - 1)
            def _():
                averaged = average()

                mean_send[step_index] = averaged.reshape(3, box_y, box_z)
                mean_copy(step_index).start()

            return carry

        lax.fori_loop(0, total_subs, sub_step, 0)
        for k in range(4):
            write(k)
        for index in range(STEPS):
            mean_copy(index).wait_send()
        written()

    @pl.when(is_coarse)
    def _():
        corner_y = off_ref[0]

        def take_section(index, source):
            for p in range(PLANES):
                for c in range(3):
                    slice_z = source[p, c, :, depth - box_z : depth]
                    sec_send[index, p, c] = pltpu.roll(slice_z, width - corner_y, 0)[:box_y]

        def send_section(index):
            for p in range(PLANES):

                @pl.when(in_box[p])
                def _(p=p):
                    section_copy(index, p).start()

        def first():
            for p in range(1, PLANES):
                loads[0][p].wait()
            take_section(0, E)

        def place(index):
            row, column = iota((width, box_z), 0), iota((width, box_z), 1)
            interior = (row >= corner_y + 1) & (row <= corner_y + box_y - 2) & (column >= 1) & (column <= box_z - 2)
            for p in range(PLANES):

                @pl.when(in_box[p])
                def _(p=p):
                    mean_arrival(index, p).wait_recv()
                    inside = interior & (fine_at[p] >= 1) & (fine_at[p] <= n_slab - 2)
                    for c in range(3):
                        mean = mean_recv[index, p, c]
                        tall = jnp.concatenate([mean] * (width // box_y), axis=0)
                        placed = pltpu.roll(tall, corner_y, 0)
                        kept = E[p, c, :, depth - box_z : depth]
                        E[p, c, :, depth - box_z : depth] = jnp.where(inside, placed, kept)

        def foresee(slot):
            for p in range(PLANES):
                a_j, a_p, a_e, k_c, k_j = (CO[k, p] for k in range(5))
                h_x, h_y, h_z = H[p, 0], H[p, 1], H[p, 2]
                if p == 0:
                    y_back, z_back = h_recv[slot, 0], h_recv[slot, 1]
                else:
                    y_back, z_back = H[p - 1, 1], H[p - 1, 2]
                curls = (
                    (h_z - down_y(h_z)) - (h_y - down_z(h_y)),
                    (h_x - down_z(h_x)) - (h_z - z_back),
                    (h_y - y_back) - (h_x - down_y(h_x)),
                )
                for c in range(3):
                    current = a_j * J[p, c] + a_p * Q[p, c] + a_e * E[p, c]
                    T[p, c] = E[p, c] - k_j * current + k_c * curls[c]

        begin(STEP_COARSE, first)
        send_section(0)
        rest_of_loads((0,))

        def step(n, carry):
            slot = n % 2
            for p in (1, 2):
                oscillate(p)
                move(p, STEP_COARSE)
            electric_whole(2)
            electric_whole(1)
            magnetic_whole(1)

            @pl.when(n == 0)
            def _():
                learn_right()
                hear_left(0)

            first_plane(slot)

            @pl.when(n == 0)
            def _():
                take_section(1, E)
                send_section(1)

            magnetic_whole(0)
            hear_right(slot)
            last_plane(slot)
            sent(slot)

            @pl.when(n < STEPS - 1)
            def _():
                tell_right(1 - slot)
                hear_left(1 - slot)
                foresee(1 - slot)
                take_section(n + 2, T)
                send_section(n + 2)

            place(n)

            @pl.when(n < STEPS - 1)
            def _():
                tell_left(1 - slot, STEP_COARSE)

            return carry

        lax.fori_loop(0, STEPS, step, 0)
        for k in range(4):
            write(k)
        for index in range(STEPS + 1):
            for p in range(PLANES):

                @pl.when(in_box[p])
                def _(index=index, p=p):
                    section_copy(index, p).wait_send()

        written()


def on_device(n_slab, efield, hfield, polar, current, material, box_offset):
    planes, width, depth = efield.shape[2:]
    box_y, box_z = width // 3, depth // 3
    plane = (width, depth)
    f32 = jnp.float32
    dma = pltpu.SemaphoreType.DMA
    scratch = [
        pltpu.VMEM((planes, 3) + plane, f32),
        pltpu.VMEM((planes, 3) + plane, f32),
        pltpu.VMEM((planes, 3) + plane, f32),
        pltpu.VMEM((planes, 3) + plane, f32),
        pltpu.VMEM((planes,) + plane, jnp.int32),
        pltpu.VMEM((5, planes) + plane, f32),
        pltpu.VMEM(plane, f32),
        pltpu.VMEM(plane, jnp.int32),
        pltpu.VMEM((planes, 3) + plane, f32),
        pltpu.VMEM((2, 2) + plane, f32),
        pltpu.VMEM((2, 2) + plane, f32),
        pltpu.VMEM((2, 3) + plane, f32),
        pltpu.VMEM((2, 2) + plane, f32),
        pltpu.VMEM((STEPS + 1, planes, 3, box_y, box_z), f32),
        pltpu.VMEM((STEPS + 1, 3, box_y, box_z), f32),
        pltpu.VMEM((3,) + plane, f32),
        pltpu.VMEM((3,) + plane, f32),
        pltpu.VMEM((STEPS, 3, box_y, box_z), f32),
        pltpu.VMEM((STEPS, planes, 3, box_y, box_z), f32),
        dma((5, planes)),
        dma((4, planes)),
        dma,
        dma,
        dma((2,)),
        dma((2,)),
        dma((2,)),
        dma((2,)),
        dma((STEPS + 1, planes)),
        dma((STEPS + 1,)),
        dma((STEPS,)),
        dma((STEPS, planes)),
    ]
    whole = pl.BlockSpec(memory_space=pl.ANY)
    return pl.pallas_call(
        functools.partial(kernel, n_slab, width, depth),
        out_shape=[jax.ShapeDtypeStruct(efield.shape, f32)] * 4,
        in_specs=[pl.BlockSpec(memory_space=pltpu.SMEM)] + [whole] * 5,
        out_specs=[whole] * 4,
        scratch_shapes=scratch,
        compiler_params=pltpu.CompilerParams(
            collective_id=1, has_side_effects=True, vmem_limit_bytes=32 * 1024 * 1024
        ),
    )(box_offset, efield, hfield, polar, current, material)


def solution(mesh):
    field = P("grid", "angle", "slab", None, None)
    return jax.shard_map(
        functools.partial(on_device, mesh.shape["slab"]),
        mesh=mesh,
        in_specs=(field, field, field, field, P("grid", "slab", None, None), P()),
        out_specs=(field, field, field, field),
        check_vma=False,
    )
```

```python
import functools

import jax
import jax.numpy as jnp
from jax import lax
from jax.experimental import pallas as pl
from jax.experimental.pallas import tpu as pltpu
from jax.sharding import PartitionSpec as P

STEPS = 3
SUBS = 3
PERMITTIVITY = (1.0, 1.5, 1.2, 2.0)
STRENGTH = (0.4, 0.9, 0.3, 1.1)
RESONANCE = (0.6, 0.5, 0.8, 0.3)
DAMPING_RATE = (0.3, 0.2, 0.05, 0.4)
COURANT = 0.5
STEP_COARSE = 0.5
STEP_FINE = STEP_COARSE / 3.0
PLANES = 3
MESH = pl.DeviceIdType.MESH
EXACT = lax.Precision.HIGHEST


def tables(step):
    rows = zip(PERMITTIVITY, STRENGTH, RESONANCE, DAMPING_RATE)
    return [
        (1.0 - step * d, -step * r, step * s * r, COURANT / e, step / e) for e, s, r, d in rows
    ]


def pick(material, values):
    out = jnp.full(material.shape, values[0], jnp.float32)
    for index in range(1, 4):
        out = jnp.where(material == index, jnp.float32(values[index]), out)
    return out


def iota(shape, dim):
    return lax.broadcasted_iota(jnp.int32, shape, dim)


def down_y(u):
    return jnp.where(iota(u.shape, 0) == 0, 0.0, pltpu.roll(u, 1, 0))


def up_y(u):
    last = u.shape[0] - 1
    return jnp.where(iota(u.shape, 0) == last, 0.0, pltpu.roll(u, last, 0))


def down_z(u):
    return jnp.where(iota(u.shape, 1) == 0, 0.0, pltpu.roll(u, 1, 1))


def up_z(u):
    last = u.shape[1] - 1
    return jnp.where(iota(u.shape, 1) == last, 0.0, pltpu.roll(u, last, 1))


def curl_h(h, back=None):
    x, y, z = h
    c_x = (z - down_y(z)) - (y - down_z(y))
    c_y, c_z = -z, y
    if x is not None:
        c_y, c_z = (x - down_z(x)) - z, y - (x - down_y(x))
    if back is not None:
        c_y, c_z = c_y + back[1], c_z - back[0]
    return c_x, c_y, c_z


def curl_e(e, ahead=None):
    x, y, z = e
    c_x = (up_y(z) - z) - (up_z(y) - y)
    c_y, c_z = z, -y
    if x is not None:
        c_y, c_z = (up_z(x) - x) + z, -y - (up_y(x) - x)
    if ahead is not None:
        c_y, c_z = c_y - ahead[1], c_z + ahead[0]
    return c_x, c_y, c_z


def kernel(
    n_slab, width, depth,
    off_ref, e_in, h_in, p_in, j_in, m_in,
    e_out, h_out, p_out, j_out,
    E, H, Q, J, TE, TH, TQ, TJ, M, CO, m_left, m_right, CL, CR,
    AE, AH, AQ, AJ, A1, BE, BH,
    h_send, h_recv, b_send, b_recv,
    sec_send, sec_recv, table_send, table_recv, near_send, near_recv,
    up_prev, up_last, mean_send, mean_recv, f_send, f_recv,
    load_sem, out_sem, m_sem,
    hs_sem, hr_sem, bs_sem, br_sem, ss_sem, sr_sem, ts_sem, tr_sem, ns_sem, nr_sem,
    ms_sem, mr_sem, fs_sem, fr_sem,
):
    slab = lax.axis_index("slab")
    level = lax.axis_index("grid")
    box_y, box_z = width // 3, depth // 3
    first_slab = n_slab // 8
    is_fine = level == 1
    is_coarse = level == 0
    has_left = slab > 0
    has_right = slab < n_slab - 1
    partner_slab = first_slab + slab // 3
    partner_plane = slab % 3
    borrows = partner_plane == 0
    fine_at = [3 * (slab - first_slab) + p for p in range(PLANES + 1)]
    in_box = [(f >= 0) & (f < n_slab) for f in fine_at]

    fields = ((e_in, E, e_out), (h_in, H, h_out), (p_in, Q, p_out), (j_in, J, j_out))
    loads = [
        [pltpu.make_async_copy(src.at[0, :, p], dst.at[p], load_sem.at[k, p]) for p in range(PLANES)]
        for k, (src, dst, _) in enumerate(fields)
    ]
    load_m = pltpu.make_async_copy(m_in.at[0], M, load_sem.at[4, 0])

    barrier = pltpu.get_barrier_semaphore()

    def greet(condition, target):
        @pl.when(condition)
        def _():
            pl.semaphore_signal(barrier, inc=1, device_id=target, device_id_type=MESH)

    def count(*conditions):
        return sum(c.astype(jnp.int32) for c in conditions)

    greet(is_fine, {"grid": 0, "slab": partner_slab})
    greet(is_fine & borrows, {"grid": 0, "slab": partner_slab - 1})
    greet(has_left, {"slab": slab - 1})
    greet(has_right, {"slab": slab + 1})

    load_m.start()
    for p in range(PLANES):
        for k in range(4):
            loads[k][p].start()

    def remote(src, dst, send, recv, target):
        return pltpu.make_async_remote_copy(
            src_ref=src, dst_ref=dst, send_sem=send, recv_sem=recv, device_id=target, device_id_type=MESH
        )

    left, right = {"slab": slab - 1}, {"slab": slab + 1}

    def h_copy(slot):
        return remote(h_send.at[slot], h_recv.at[slot], hs_sem.at[slot], hr_sem.at[slot], right)

    def b_copy(slot):
        return remote(b_send.at[slot, 0:2], b_recv.at[slot], bs_sem.at[slot], br_sem.at[slot], left)

    m_to_left = remote(m_in.at[0, 0:2], m_right, m_sem.at[0], m_sem.at[1], left)
    m_to_right = remote(m_in.at[0, 2], m_left, m_sem.at[2], m_sem.at[3], right)

    def section_copy(index, p):
        return remote(
            sec_send.at[index, p], sec_recv.at[index], ss_sem.at[index, p], sr_sem.at[index],
            {"grid": 1, "slab": fine_at[p]},
        )

    def table_copy(p):
        return remote(
            table_send.at[p], table_recv, ts_sem.at[p], tr_sem, {"grid": 1, "slab": fine_at[p]}
        )

    def near_copy(index):
        return remote(
            near_send.at[index], near_recv.at[index], ns_sem.at[index], nr_sem.at[index],
            {"grid": 1, "slab": fine_at[PLANES]},
        )

    def mean_copy(index):
        return remote(
            mean_send.at[index], mean_recv.at[index, partner_plane], ms_sem.at[index],
            mr_sem.at[index, partner_plane], {"grid": 0, "slab": partner_slab},
        )

    def mean_arrival(index, p):
        return remote(
            mean_send.at[index], mean_recv.at[index, p], ms_sem.at[index], mr_sem.at[index, p],
            {"grid": 1, "slab": fine_at[p]},
        )

    def f_copy(side):
        return remote(f_send, f_recv.at[side], fs_sem.at[side], fr_sem.at[side], right if side == 0 else left)

    def go(condition, *copies):
        @pl.when(condition)
        def _():
            for copy in copies:
                copy.start()

    def heard(condition, *copies):
        @pl.when(condition)
        def _():
            for copy in copies:
                copy.wait_recv()

    def sent(condition, *copies):
        @pl.when(condition)
        def _():
            for copy in copies:
                copy.wait_send()

    def get(ref, *index):
        return tuple(ref[(*index, c)] for c in range(3))

    def put(ref, index, values):
        for c, value in enumerate(values):
            if value is not None:
                ref[(*index, c)] = value

    def oscillate(p, step, state):
        e, _, q, j = state
        a_j, a_p, a_e = CO[0, p], CO[1, p], CO[2, p]
        for c in range(3):
            current = a_j * j[p, c] + a_p * q[p, c] + a_e * e[p, c]
            j[p, c] = current
            q[p, c] = q[p, c] + step * current

    def electric(p, state, back=None):
        e, h, _, j = state
        k_c, k_j = CO[3, p], CO[4, p]
        curl = curl_h(get(h, p), back)
        return tuple(e[p, c] - k_j * j[p, c] + k_c * curl[c] for c in range(3))

    def electric_whole(p, state):
        put(state[0], (p,), electric(p, state, (state[1][p - 1, 1], state[1][p - 1, 2])))

    def magnetic(p, state, ahead=None):
        e, h, _, _ = state
        curl = curl_e(get(e, p), ahead)
        return tuple(h[p, c] - COURANT * curl[c] for c in range(3))

    def magnetic_whole(p, state):
        put(state[1], (p,), magnetic(p, state, (state[0][p + 1, 1], state[0][p + 1, 2])))

    def set_coefficients(step):
        load_m.wait()
        values = tables(step)
        for p in range(PLANES):
            material = M[p]
            for k in range(5):
                CO[k, p] = pick(material, [row[k] for row in values])

    def learn_neighbours(step):
        heard(has_right, m_to_left)
        heard(has_left, m_to_right)
        sent(has_left, m_to_left)
        sent(has_right, m_to_right)
        values = tables(step)
        near, far = m_right[0], m_right[1]
        is_there = has_right.astype(jnp.float32)
        for k in range(5):
            scale = is_there if k == 3 else 1.0
            CR[k] = pick(near, [row[k] for row in values]) * scale
        CR[5] = pick(far, [row[3] for row in values]) * is_there
        CL[...] = pick(m_left[...], [row[3] for row in values]) * has_left.astype(jnp.float32)

    def prepare():
        @pl.when(jnp.logical_not(has_left))
        def _():
            h_recv[...] = jnp.zeros_like(h_recv)
            m_left[...] = jnp.zeros_like(m_left)

        @pl.when(jnp.logical_not(has_right))
        def _():
            b_recv[...] = jnp.zeros_like(b_recv)
            m_right[...] = jnp.zeros_like(m_right)

    def tell_right(slot, y, z):
        h_send[slot, 0], h_send[slot, 1] = y, z
        go(has_right, h_copy(slot))

    def set_b(slot, b):
        b_send[slot, 0], b_send[slot, 1], b_send[slot, 2] = b[1], b[2], b[0]

    def tell_left(slot, b):
        set_b(slot, b)
        go(has_left, b_copy(slot))

    def wait_loads(*which):
        for k, p in which:
            loads[k][p].wait()

    def write(k):
        for p in range(PLANES):
            pltpu.make_async_copy(fields[k][1].at[p], fields[k][2].at[0, :, p], out_sem.at[k, p]).start()

    def written():
        for k in range(4):
            for p in range(PLANES):
                pltpu.make_async_copy(fields[k][1].at[p], fields[k][2].at[0, :, p], out_sem.at[k, p]).wait()

    true = (E, H, Q, J)

    @pl.when(is_fine)
    def _():
        step = STEP_FINE
        row, column = iota((width, depth), 0), iota((width, depth), 1)
        edge = (row == 0) | (row == width - 1) | (column == 0) | (column == depth - 1)
        rims = [edge | (slab == 0), edge, edge | (slab == n_slab - 1)]
        small_row, small_column = iota((box_y, box_z), 0), iota((box_y, box_z), 1)
        f_cells = (
            (small_row >= 1) & (small_row <= box_y - 2) & (small_column >= 1) & (small_column <= box_z - 2)
            & (slab >= 1) & (slab <= n_slab - 2)
        )

        def upsampled(section):
            section = section.reshape(3 * box_y, box_z)
            spread_z = (iota((box_z, depth), 1) // 3 == iota((box_z, depth), 0)).astype(jnp.float32)
            spread_y = (iota((3 * width, 3 * box_y), 0) // 3 == iota((3 * width, 3 * box_y), 1)).astype(jnp.float32)
            wide = jnp.dot(section, spread_z, precision=EXACT, preferred_element_type=jnp.float32)
            tall = jnp.dot(spread_y, wide, precision=EXACT, preferred_element_type=jnp.float32)
            return tall.reshape(3, width, depth)

        def average():
            total = jnp.concatenate([E[0, c] + E[1, c] + E[2, c] for c in range(3)], axis=0)
            fold_z = (iota((depth, box_z), 0) // 3 == iota((depth, box_z), 1)).astype(jnp.float32)
            fold_y = (iota((3 * box_y, 3 * width), 1) // 3 == iota((3 * box_y, 3 * width), 0)).astype(jnp.float32)
            rows = jnp.dot(fold_y, total, precision=EXACT, preferred_element_type=jnp.float32)
            both = jnp.dot(rows, fold_z, precision=EXACT, preferred_element_type=jnp.float32)
            return (both * jnp.float32(1.0 / 27.0)).reshape(3, box_y, box_z)

        def boundary(sub):
            weight = jnp.float32((sub + 1) / 3.0)
            return [up_prev[c] + weight * (up_last[c] - up_prev[c]) for c in range(3)]

        def inject(ref, index, p, values):
            for c in range(3):
                ref[(*index, c)] = jnp.where(rims[p], values[c], ref[(*index, c)])

        def open_block(first_slot):
            oscillate(0, step, true)
            e = electric(0, true)
            put(AE, (), e)
            tell_left(first_slot, e)

        set_coefficients(step)
        wait_loads((0, 0), (1, 0), (2, 0), (3, 0), (1, 2))
        prepare()

        @pl.when(jnp.logical_not(borrows))
        def _():
            near_recv[...] = jnp.zeros_like(near_recv)

        @pl.when(jnp.logical_not(has_left))
        def _():
            f_recv[0] = jnp.zeros_like(f_recv[0])

        @pl.when(jnp.logical_not(has_right))
        def _():
            f_recv[1] = jnp.zeros_like(f_recv[1])

        pl.semaphore_wait(barrier, count(has_left, has_right))
        tell_right(0, H[2, 1], H[2, 2])
        open_block(0)
        go(has_left, m_to_left)
        go(has_right, m_to_right)
        wait_loads(*[(k, p) for k in range(4) for p in (1, 2) if (k, p) != (1, 2)])

        def latest(index):
            heard(True, section_copy(index, 0))
            heard(borrows, near_copy(index))
            k_c = table_recv[3]
            base = sec_recv[index]
            return (
                base[0],
                base[1] + k_c * near_recv[index, 1],
                base[2] - k_c * near_recv[index, 0],
            )

        def feedback_response():
            heard(has_left, f_copy(0))
            heard(has_right, f_copy(1))
            here, before, after = f_send, f_recv.at[0], f_recv.at[1]
            curl = curl_e((here[0], here[1], here[2]), (after[1], after[2]))
            back_x = (up_z(before[0]) - before[0], up_y(before[0]) - before[0])
            back_y = back_x[0] - (here[2] - before[2])
            back_z = (here[1] - before[1]) - back_x[1]
            twice = curl_h(curl, (back_y, back_z))
            return [-COURANT * table_recv[3] * t for t in twice]

        def block(b, carry):
            s0 = 3 * b
            for p in (1, 2):
                oscillate(p, step, true)
            electric_whole(2, true)
            electric_whole(1, true)
            h = magnetic(2, true)
            put(BH, (), h)
            tell_right(s0 + 1, h[1], h[2])
            magnetic_whole(1, true)
            curl = curl_e(get(AE), (E[1, 1], E[1, 2]))
            put(AH, (), [H[0, c] - COURANT * curl[c] for c in range(3)])

            @pl.when(b == 0)
            def _():
                heard(True, table_copy(0))
                up_last[...] = upsampled(table_recv[0:3])

            up_prev[...] = up_last[...]
            arrived = latest(b)

            @pl.when(b < STEPS - 1)
            def _():
                up_last[...] = upsampled(jnp.stack(arrived))

            @pl.when(b == STEPS - 1)
            def _():
                extra = feedback_response()
                up_last[...] = upsampled(jnp.stack([a + e for a, e in zip(arrived, extra)]))

            values = boundary(0)
            inject(AE, (), 0, values)
            inject(E, (1,), 1, values)
            inject(E, (2,), 2, values)
            a_j, a_p, a_e, k_c, k_j = (CO[k, 0] for k in range(5))
            for c in range(3):
                current = a_j * J[0, c] + a_p * Q[0, c] + a_e * AE[c]
                AJ[c] = current
                AQ[c] = Q[0, c] + step * current
            curl = curl_h(get(AH))
            e_0 = tuple(AE[c] - k_j * AJ[c] + k_c * curl[c] for c in range(3))
            put(AE, (), e_0)
            tell_left(s0 + 1, e_0)
            for p in (1, 2):
                oscillate(p, step, true)
            curl = curl_h(get(BH), (H[1, 1], H[1, 2]))
            e_2 = tuple(E[2, c] - CO[4, 2] * J[2, c] + CO[3, 2] * curl[c] for c in range(3))
            put(BE, (), e_2)
            curl = curl_e(e_2)
            h = tuple(BH[c] - COURANT * curl[c] for c in range(3))
            put(BH, (), h)
            tell_right(s0 + 2, h[1], h[2])
            curl = curl_h(get(H, 1), (AH[1], AH[2]))
            e_1 = tuple(E[1, c] - CO[4, 1] * J[1, c] + CO[3, 1] * curl[c] for c in range(3))
            put(A1, (), e_1)
            curl = curl_e(get(AE), (A1[1], A1[2]))
            put(AH, (), [AH[c] - COURANT * curl[c] for c in range(3)])
            values = boundary(1)
            inject(AE, (), 0, values)
            for c in range(3):
                current = a_j * AJ[c] + a_p * AQ[c] + a_e * AE[c]
                AJ[c] = current
                AQ[c] = AQ[c] + step * current
            curl = curl_h(get(AH))
            e_0 = tuple(AE[c] - k_j * AJ[c] + k_c * curl[c] for c in range(3))
            put(AE, (), e_0)
            tell_left(s0 + 2, e_0)

            @pl.when(b == 0)
            def _():
                learn_neighbours(step)

            def face(coefficients, k_near, k_back, there, h_own, e_own, hear):
                a_j, a_p, a_e, k_c, k_j = coefficients
                side = COURANT * there.astype(jnp.float32)

                def kept(u):
                    return jnp.where(edge, 0.0, u)

                hear(0)
                h_y, h_z = h_own(0)
                e_y, e_z = e_own(0)
                d_y, d_z = k_c * h_z, -k_c * h_y
                e_y, e_z = e_y + d_y, e_z + d_z
                l_y, l_z = side * e_z, -side * e_y
                d_h = tuple(-COURANT * u for u in curl_e((None, d_y, d_z)))
                d_y, d_z = kept(d_y), kept(d_z)
                j_y, j_z = a_e * d_y, a_e * d_z
                p_y, p_z = step * j_y, step * j_z
                hear(1)
                h_y, h_z = h_own(1)
                e_y, e_z = e_own(1)
                h_y, h_z = h_y + l_y, h_z + l_z
                curl = curl_h(d_h, (h_y, h_z))
                d_x = k_c * curl[0]
                d_y = d_y - k_j * j_y + k_c * curl[1]
                d_z = d_z - k_j * j_z + k_c * curl[2]
                e_y, e_z = e_y + d_y, e_z + d_z
                l_e = tuple(k_back * u for u in curl_h((None, l_y, l_z)))
                curl = curl_e(l_e)
                l_h = (
                    -COURANT * curl[0],
                    l_y - COURANT * curl[1] + side * e_z,
                    l_z - COURANT * curl[2] - side * e_y,
                )
                f_y, f_z = k_near * d_h[2], -k_near * d_h[1]
                curl = curl_e((d_x, d_y, d_z), (f_y, f_z))
                d_h = tuple(d_h[c] - COURANT * curl[c] for c in range(3))
                d_e = kept(d_x), kept(d_y), kept(d_z)
                d_j = (a_e * d_e[0], a_j * j_y + a_p * p_y + a_e * d_e[1], a_j * j_z + a_p * p_z + a_e * d_e[2])
                d_p = (step * d_j[0], p_y + step * d_j[1], p_z + step * d_j[2])
                curl = curl_h(d_h, (l_h[1], l_h[2]))
                d_e = tuple(d_e[c] - k_j * d_j[c] + k_c * curl[c] for c in range(3))
                return d_e, d_j, d_p, d_h, (f_y, f_z), l_e, l_h

            def hear_left(m):
                heard(has_left, h_copy(s0 + m))

            def hear_right(m):
                heard(has_right, b_copy(s0 + m))

            d_e, _, _, _, _, l_e, l_h = face(
                [CR[k] for k in range(5)], CR[5], CO[3, 2], has_right,
                lambda m: (h_send[s0 + m, 0], h_send[s0 + m, 1]),
                lambda m: (b_recv[s0 + m, 0], b_recv[s0 + m, 1]),
                hear_right,
            )
            k_c = CR[3]
            next_y = d_e[1] + k_c * h_send[s0 + 2, 1]
            next_z = d_e[2] - k_c * h_send[s0 + 2, 0]
            put(H, (2,), [BH[c] + l_h[c] for c in range(3)])
            put(E, (2,), [BE[c] + l_e[c] for c in range(3)])
            d_e, d_j, d_p, d_h, near, _, _ = face(
                [CO[k, 0] for k in range(5)], CO[3, 1], CL[...], has_left,
                lambda m: (h_recv[s0 + m, 0], h_recv[s0 + m, 1]),
                lambda m: (b_send[s0 + m, 0], b_send[s0 + m, 1]),
                hear_left,
            )
            put(H, (0,), [AH[c] + d_h[c] for c in range(3)])
            put(J, (0,), [AJ[c] + d_j[c] for c in range(3)])
            put(Q, (0,), [AQ[c] + d_p[c] for c in range(3)])
            put(AE, (), [AE[c] + d_e[c] for c in range(3)])
            put(E, (1,), [A1[0], A1[1] + near[0], A1[2] + near[1]])

            magnetic_whole(1, true)
            values = boundary(1)
            for p in (1, 2):
                inject(E, (p,), p, values)
                oscillate(p, step, true)
            electric_whole(2, true)
            electric_whole(1, true)
            magnetic_whole(1, true)
            values = boundary(2)

            hear_right(2)
            put(H, (2,), magnetic(2, true, (next_y + b_recv[s0 + 2, 0], next_z + b_recv[s0 + 2, 1])))

            @pl.when(b < STEPS - 1)
            def _():
                tell_right(s0 + 3, H[2, 1], H[2, 2])

            hear_left(2)
            k_c = CO[3, 0]
            E[0, 0] = AE[0]
            E[0, 1] = AE[1] + k_c * h_recv[s0 + 2, 1]
            E[0, 2] = AE[2] - k_c * h_recv[s0 + 2, 0]
            magnetic_whole(0, true)
            inject(E, (0,), 0, values)

            @pl.when(b < STEPS - 1)
            def _():
                open_block(s0 + 3)

            inject(E, (1,), 1, values)
            inject(E, (2,), 2, values)
            mean = average()
            mean_send[b] = mean
            mean_copy(b).start()

            @pl.when(b == 0)
            def _():
                g = table_recv[4]
                for c in range(3):
                    f_send[c] = jnp.where(f_cells, g * mean[c], 0.0)
                go(has_right, f_copy(0))
                go(has_left, f_copy(1))

            return carry

        lax.fori_loop(0, STEPS, block, 0)
        for k in range(4):
            write(k)
        for slot in range(STEPS * SUBS):
            sent(has_right, h_copy(slot))
            sent(has_left, b_copy(slot))
        sent(has_right, f_copy(0))
        sent(has_left, f_copy(1))
        for index in range(STEPS):
            mean_copy(index).wait_send()
        written()

    @pl.when(is_coarse)
    def _():
        step = STEP_COARSE
        corner_y = off_ref[0]
        guess = (TE, TH, TQ, TJ)

        def cut(value):
            return pltpu.roll(value[:, depth - box_z : depth], width - corner_y, 0)[:box_y]

        row, column = iota((width, box_z), 0), iota((width, box_z), 1)
        interior = (row >= corner_y + 1) & (row <= corner_y + box_y - 2) & (column >= 1) & (column <= box_z - 2)

        def inside(p):
            return interior & (fine_at[p] >= 1) & (fine_at[p] <= n_slab - 2)

        def place(index):
            for p in range(PLANES):

                @pl.when(in_box[p])
                def _(p=p):
                    mean_arrival(index, p).wait_recv()
                    for c in range(3):
                        tall = jnp.concatenate([mean_recv[index, p, c]] * (width // box_y), axis=0)
                        placed = pltpu.roll(tall, corner_y, 0)
                        kept = E[p, c, :, depth - box_z : depth]
                        E[p, c, :, depth - box_z : depth] = jnp.where(inside(p), placed, kept)

        def take(index, p, values):
            for c in range(3):
                sec_send[index, p, c] = cut(values[c])

        def take_near(index, state):
            for c in range(2):
                near_send[index, c] = cut(state[1][2, 1 + c])

        def send(index):
            for p in range(PLANES):
                go(in_box[p], section_copy(index, p))
            go(in_box[PLANES], near_copy(index))

        def first_half(state, slot_h, slot_b):
            e, h, _, _ = state
            for p in (1, 2):
                oscillate(p, step, state)
            electric_whole(2, state)
            electric_whole(1, state)
            k_c = CO[3, 0]
            e[0, 0] = b_send[slot_b, 2]
            e[0, 1] = b_send[slot_b, 0] + k_c * h_recv[slot_h, 1]
            e[0, 2] = b_send[slot_b, 1] - k_c * h_recv[slot_h, 0]
            magnetic_whole(1, state)
            magnetic_whole(0, state)

        def second_half(state, slot_h, slot_b):
            heard(has_right, b_copy(slot_b))
            k_c = CR[3]
            ahead = (
                b_recv[slot_b, 0] + k_c * h_send[slot_h, 1],
                b_recv[slot_b, 1] - k_c * h_send[slot_h, 0],
            )
            put(state[1], (2,), magnetic(2, state, ahead))

        set_coefficients(step)
        wait_loads(*[(k, p) for k in range(4) for p in range(PLANES)])
        for p in range(PLANES):
            for c in range(3):
                table_send[p, c] = cut(E[p, c])
            table_send[p, 3] = cut(CO[3, p])
            table_send[p, 4] = 1.0 - cut(CO[4, p]) * cut(CO[2, p])
        h_send[0, 0], h_send[0, 1] = H[2, 1], H[2, 2]
        take_near(0, true)
        for p in range(PLANES):
            oscillate(p, step, true)
        start = electric(0, true)
        set_b(0, start)
        take(0, 0, start)
        electric_whole(2, true)
        electric_whole(1, true)
        for p in (1, 2):
            take(0, p, get(E, p))
        prepare()
        pl.semaphore_wait(barrier, count(has_left, has_right, *in_box))
        for p in range(PLANES):
            go(in_box[p], table_copy(p), section_copy(0, p))
        go(in_box[PLANES], near_copy(0))
        go(has_right, h_copy(0), m_to_right)
        go(has_left, b_copy(0), m_to_left)

        magnetic_whole(1, true)
        learn_neighbours(step)
        heard(has_left, h_copy(0))
        k_c = CO[3, 0]
        E[0, 0] = start[0]
        E[0, 1] = b_send[0, 0] + k_c * h_recv[0, 1]
        E[0, 2] = b_send[0, 1] - k_c * h_recv[0, 0]
        magnetic_whole(0, true)
        second_half(true, 0, 0)
        tell_right(1, H[2, 1], H[2, 2])

        take_near(1, true)
        for p in range(PLANES):
            for c in range(3):
                value = E[p, c]
                TE[p, c] = value
                kept = value[:, depth - box_z : depth]
                TE[p, c, :, depth - box_z : depth] = jnp.where(inside(p) & in_box[p], 0.0, kept)
                TH[p, c] = H[p, c]
                TQ[p, c] = Q[p, c]
                TJ[p, c] = J[p, c]
        oscillate(0, step, guess)
        start = electric(0, guess)
        tell_left(1, start)
        take(1, 0, start)
        for p in (1, 2):
            oscillate(p, step, guess)
        electric_whole(2, guess)
        electric_whole(1, guess)
        for p in (1, 2):
            take(1, p, get(TE, p))
        send(1)
        heard(has_left, h_copy(1))
        k_c = CO[3, 0]
        TE[0, 0] = b_send[1, 2]
        TE[0, 1] = b_send[1, 0] + k_c * h_recv[1, 1]
        TE[0, 2] = b_send[1, 1] - k_c * h_recv[1, 0]
        magnetic_whole(1, guess)
        magnetic_whole(0, guess)
        second_half(guess, 1, 1)
        take_near(2, guess)
        for p in range(PLANES):
            oscillate(p, step, guess)
            back = None if p == 0 else (TH[p - 1, 1], TH[p - 1, 2])
            take(2, p, electric(p, guess, back))
        send(2)

        place(0)
        oscillate(0, step, true)
        tell_left(2, electric(0, true))
        first_half(true, 1, 2)
        second_half(true, 1, 2)
        tell_right(2, H[2, 1], H[2, 2])
        place(1)
        oscillate(0, step, true)
        tell_left(3, electric(0, true))
        heard(has_left, h_copy(2))
        first_half(true, 2, 3)
        write(2)
        write(3)
        second_half(true, 2, 3)
        write(1)
        place(2)
        write(0)
        for slot in range(3):
            sent(has_right, h_copy(slot))
        for slot in range(4):
            sent(has_left, b_copy(slot))
        for p in range(PLANES):
            sent(in_box[p], table_copy(p), *[section_copy(index, p) for index in range(STEPS)])
        sent(in_box[PLANES], *[near_copy(index) for index in range(STEPS)])
        written()


def hand_over(*refs):
    for source, target in zip(refs[:4], refs[4:]):
        target[...] = source[...]


def on_device(n_slab, efield, hfield, polar, current, material, box_offset):
    planes, width, depth = efield.shape[2:]
    box = (width // 3, depth // 3)
    plane = (width, depth)
    f32 = jnp.float32
    dma = pltpu.SemaphoreType.DMA
    slots = STEPS * SUBS

    def room(*shape, dtype=f32):
        return pltpu.VMEM(shape, dtype)

    state = room(planes, 3, *plane)
    triple = room(3, *plane)
    scratch = [state] * 8 + [
        room(planes, *plane, dtype=jnp.int32),
        room(5, planes, *plane),
        room(*plane, dtype=jnp.int32),
        room(2, *plane, dtype=jnp.int32),
        room(*plane),
        room(6, *plane),
    ]
    scratch += [triple] * 7
    scratch += [room(slots, 2, *plane), room(slots, 2, *plane), room(slots, 3, *plane), room(slots, 2, *plane)]
    scratch += [
        room(STEPS, planes, 3, *box),
        room(STEPS, 3, *box),
        room(planes, 5, *box),
        room(5, *box),
        room(STEPS, 2, *box),
        room(STEPS, 2, *box),
        triple,
        triple,
        room(STEPS, 3, *box),
        room(STEPS, planes, 3, *box),
        room(3, *box),
        room(2, 3, *box),
    ]
    scratch += [dma((5, planes)), dma((4, planes)), dma((4,))]
    scratch += [dma((slots,))] * 4
    scratch += [dma((STEPS, planes)), dma((STEPS,)), dma((planes,)), dma, dma((STEPS,)), dma((STEPS,))]
    scratch += [dma((STEPS,)), dma((STEPS, planes)), dma((2,)), dma((2,))]
    whole = pl.BlockSpec(memory_space=pl.ANY)
    fields = [jax.ShapeDtypeStruct(efield.shape, f32)] * 4
    state = pl.pallas_call(
        functools.partial(kernel, n_slab, width, depth),
        out_shape=fields,
        in_specs=[pl.BlockSpec(memory_space=pltpu.SMEM)] + [whole] * 5,
        out_specs=[whole] * 4,
        scratch_shapes=scratch,
        compiler_params=pltpu.CompilerParams(
            collective_id=1, has_side_effects=True, vmem_limit_bytes=60 * 1024 * 1024
        ),
    )(box_offset, efield, hfield, polar, current, material)
    return pl.pallas_call(
        hand_over,
        out_shape=fields,
        in_specs=[pl.BlockSpec(memory_space=pltpu.VMEM)] * 4,
        out_specs=[pl.BlockSpec(memory_space=pltpu.VMEM)] * 4,
    )(*state)


def solution(mesh):
    field = P("grid", "angle", "slab", None, None)
    return jax.shard_map(
        functools.partial(on_device, mesh.shape["slab"]),
        mesh=mesh,
        in_specs=(field, field, field, field, P("grid", "slab", None, None), P()),
        out_specs=(field, field, field, field),
        check_vma=False,
    )
```

```python
import functools

import jax
import jax.numpy as jnp
from jax import lax
from jax.experimental import pallas as pl
from jax.experimental.pallas import tpu as pltpu
from jax.sharding import PartitionSpec as P

STEPS = 3
SUBS = 3
PERMITTIVITY = (1.0, 1.5, 1.2, 2.0)
STRENGTH = (0.4, 0.9, 0.3, 1.1)
RESONANCE = (0.6, 0.5, 0.8, 0.3)
DAMPING_RATE = (0.3, 0.2, 0.05, 0.4)
COURANT = 0.5
STEP_COARSE = 0.5
STEP_FINE = STEP_COARSE / 3.0
PLANES = 3
MESH = pl.DeviceIdType.MESH
EXACT = lax.Precision.HIGHEST


def tables(step):
    rows = zip(PERMITTIVITY, STRENGTH, RESONANCE, DAMPING_RATE)
    return [
        (1.0 - step * d, -step * r, step * s * r, COURANT / e, step / e) for e, s, r, d in rows
    ]


def pick(material, values):
    out = jnp.full(material.shape, values[0], jnp.float32)
    for index in range(1, 4):
        out = jnp.where(material == index, jnp.float32(values[index]), out)
    return out


def iota(shape, dim):
    return lax.broadcasted_iota(jnp.int32, shape, dim)


def down_y(u):
    return jnp.where(iota(u.shape, 0) == 0, 0.0, pltpu.roll(u, 1, 0))


def up_y(u):
    last = u.shape[0] - 1
    return jnp.where(iota(u.shape, 0) == last, 0.0, pltpu.roll(u, last, 0))


def down_z(u):
    return jnp.where(iota(u.shape, 1) == 0, 0.0, pltpu.roll(u, 1, 1))


def up_z(u):
    last = u.shape[1] - 1
    return jnp.where(iota(u.shape, 1) == last, 0.0, pltpu.roll(u, last, 1))


def curl_h(h, back=None):
    x, y, z = h
    c_x = (z - down_y(z)) - (y - down_z(y))
    c_y, c_z = -z, y
    if x is not None:
        c_y, c_z = (x - down_z(x)) - z, y - (x - down_y(x))
    if back is not None:
        c_y, c_z = c_y + back[1], c_z - back[0]
    return c_x, c_y, c_z


def curl_e(e, ahead=None):
    x, y, z = e
    c_x = (up_y(z) - z) - (up_z(y) - y)
    c_y, c_z = z, -y
    if x is not None:
        c_y, c_z = (up_z(x) - x) + z, -y - (up_y(x) - x)
    if ahead is not None:
        c_y, c_z = c_y - ahead[1], c_z + ahead[0]
    return c_x, c_y, c_z


def kernel(
    n_slab, width, depth,
    off_in, e_in, h_in, p_in, j_in, m_in,
    e_out, h_out, p_out, j_out, mean_out,
    off_ref, E, H, Q, J, TE, TH, TQ, TJ, M, CO, m_left, m_right, CL, CR,
    AE, AH, AQ, AJ, A1, BE, BH, partial,
    h_send, h_recv, b_send, b_recv,
    sec_send, sec_recv, table_send, table_recv, near_send, near_recv,
    up_prev, up_last, mean_send, mean_recv, f_send, f_recv,
    off_sem, load_sem, out_sem, m_sem,
    hs_sem, hr_sem, bs_sem, br_sem, ss_sem, sr_sem, ts_sem, tr_sem, ns_sem, nr_sem,
    ms_sem, mr_sem, fs_sem, fr_sem,
):
    slab = lax.axis_index("slab")
    level = lax.axis_index("grid")
    box_y, box_z = width // 3, depth // 3
    first_slab = n_slab // 8
    is_fine = level == 1
    is_coarse = level == 0
    has_left = slab > 0
    has_right = slab < n_slab - 1
    partner_slab = first_slab + slab // 3
    partner_plane = slab % 3
    borrows = partner_plane == 0
    fine_at = [3 * (slab - first_slab) + p for p in range(PLANES + 1)]
    in_box = [(f >= 0) & (f < n_slab) for f in fine_at]

    fields = ((e_in, E, e_out), (h_in, H, h_out), (p_in, Q, p_out), (j_in, J, j_out))
    loads = [
        [pltpu.make_async_copy(src.at[0, :, p], dst.at[p], load_sem.at[k, p]) for p in range(PLANES)]
        for k, (src, dst, _) in enumerate(fields)
    ]
    load_m = pltpu.make_async_copy(m_in.at[0], M, load_sem.at[4, 0])

    barrier = pltpu.get_barrier_semaphore()

    def greet(condition, target):
        @pl.when(condition)
        def _():
            pl.semaphore_signal(barrier, inc=1, device_id=target, device_id_type=MESH)

    def count(*conditions):
        return sum(c.astype(jnp.int32) for c in conditions)

    greet(is_fine, {"grid": 0, "slab": partner_slab})
    greet(is_fine & borrows, {"grid": 0, "slab": partner_slab - 1})
    greet(has_left, {"slab": slab - 1})
    greet(has_right, {"slab": slab + 1})

    load_m.start()
    for p in range(PLANES):
        for k in range(4):
            loads[k][p].start()

    def remote(src, dst, send, recv, target):
        return pltpu.make_async_remote_copy(
            src_ref=src, dst_ref=dst, send_sem=send, recv_sem=recv, device_id=target, device_id_type=MESH
        )

    left, right = {"slab": slab - 1}, {"slab": slab + 1}

    def h_copy(slot):
        return remote(h_send.at[slot], h_recv.at[slot], hs_sem.at[slot], hr_sem.at[slot], right)

    def b_copy(slot):
        return remote(b_send.at[slot, 0:2], b_recv.at[slot], bs_sem.at[slot], br_sem.at[slot], left)

    m_to_left = remote(m_in.at[0, 0:2], m_right, m_sem.at[0], m_sem.at[1], left)
    m_to_right = remote(m_in.at[0, 2], m_left, m_sem.at[2], m_sem.at[3], right)

    def section_copy(index, p):
        return remote(
            sec_send.at[index, p], sec_recv.at[index], ss_sem.at[index, p], sr_sem.at[index],
            {"grid": 1, "slab": fine_at[p]},
        )

    def table_copy(p):
        return remote(
            table_send.at[p], table_recv, ts_sem.at[p], tr_sem, {"grid": 1, "slab": fine_at[p]}
        )

    def near_copy(index):
        return remote(
            near_send.at[index], near_recv.at[index], ns_sem.at[index], nr_sem.at[index],
            {"grid": 1, "slab": fine_at[PLANES]},
        )

    def mean_copy(index):
        room = mean_out if index == STEPS - 1 else mean_recv.at[index]
        return remote(
            mean_send.at[index], room.at[partner_plane], ms_sem.at[index],
            mr_sem.at[index, partner_plane], {"grid": 0, "slab": partner_slab},
        )

    def mean_arrival(index, p):
        room = mean_out if index == STEPS - 1 else mean_recv.at[index]
        return remote(
            mean_send.at[index], room.at[p], ms_sem.at[index], mr_sem.at[index, p],
            {"grid": 1, "slab": fine_at[p]},
        )

    def f_copy(side):
        return remote(f_send, f_recv.at[side], fs_sem.at[side], fr_sem.at[side], right if side == 0 else left)

    def go(condition, *copies):
        @pl.when(condition)
        def _():
            for copy in copies:
                copy.start()

    def heard(condition, *copies):
        @pl.when(condition)
        def _():
            for copy in copies:
                copy.wait_recv()

    def sent(condition, *copies):
        @pl.when(condition)
        def _():
            for copy in copies:
                copy.wait_send()

    def get(ref, *index):
        return tuple(ref[(*index, c)] for c in range(3))

    def put(ref, index, values):
        for c, value in enumerate(values):
            if value is not None:
                ref[(*index, c)] = value

    def oscillate(p, step, state):
        e, _, q, j = state
        a_j, a_p, a_e = CO[0, p], CO[1, p], CO[2, p]
        for c in range(3):
            current = a_j * j[p, c] + a_p * q[p, c] + a_e * e[p, c]
            j[p, c] = current
            q[p, c] = q[p, c] + step * current

    def electric(p, state, back=None):
        e, h, _, j = state
        k_c, k_j = CO[3, p], CO[4, p]
        curl = curl_h(get(h, p), back)
        return tuple(e[p, c] - k_j * j[p, c] + k_c * curl[c] for c in range(3))

    def electric_whole(p, state):
        put(state[0], (p,), electric(p, state, (state[1][p - 1, 1], state[1][p - 1, 2])))

    def magnetic(p, state, ahead=None):
        e, h, _, _ = state
        curl = curl_e(get(e, p), ahead)
        return tuple(h[p, c] - COURANT * curl[c] for c in range(3))

    def magnetic_whole(p, state):
        put(state[1], (p,), magnetic(p, state, (state[0][p + 1, 1], state[0][p + 1, 2])))

    def set_coefficients(step):
        load_m.wait()
        values = tables(step)
        for p in range(PLANES):
            material = M[p]
            for k in range(5):
                CO[k, p] = pick(material, [row[k] for row in values])

    def learn_neighbours(step):
        heard(has_right, m_to_left)
        heard(has_left, m_to_right)
        sent(has_left, m_to_left)
        sent(has_right, m_to_right)
        values = tables(step)
        near, far = m_right[0], m_right[1]
        is_there = has_right.astype(jnp.float32)
        for k in range(5):
            scale = is_there if k == 3 else 1.0
            CR[k] = pick(near, [row[k] for row in values]) * scale
        CR[5] = pick(far, [row[3] for row in values]) * is_there
        CL[...] = pick(m_left[...], [row[3] for row in values]) * has_left.astype(jnp.float32)

    def prepare():
        @pl.when(jnp.logical_not(has_left))
        def _():
            h_recv[...] = jnp.zeros_like(h_recv)
            m_left[...] = jnp.zeros_like(m_left)

        @pl.when(jnp.logical_not(has_right))
        def _():
            b_recv[...] = jnp.zeros_like(b_recv)
            m_right[...] = jnp.zeros_like(m_right)

    def tell_right(slot, y, z):
        h_send[slot, 0], h_send[slot, 1] = y, z
        go(has_right, h_copy(slot))

    def set_b(slot, b):
        b_send[slot, 0], b_send[slot, 1], b_send[slot, 2] = b[1], b[2], b[0]

    def tell_left(slot, b):
        set_b(slot, b)
        go(has_left, b_copy(slot))

    def wait_loads(*which):
        for k, p in which:
            loads[k][p].wait()

    def write(k):
        for p in range(PLANES):
            pltpu.make_async_copy(fields[k][1].at[p], fields[k][2].at[0, :, p], out_sem.at[k, p]).start()

    def written():
        for k in range(4):
            for p in range(PLANES):
                pltpu.make_async_copy(fields[k][1].at[p], fields[k][2].at[0, :, p], out_sem.at[k, p]).wait()

    true = (E, H, Q, J)

    @pl.when(is_fine)
    def _():
        step = STEP_FINE
        row, column = iota((width, depth), 0), iota((width, depth), 1)
        edge = (row == 0) | (row == width - 1) | (column == 0) | (column == depth - 1)
        rims = [edge | (slab == 0), edge, edge | (slab == n_slab - 1)]
        small_row, small_column = iota((box_y, box_z), 0), iota((box_y, box_z), 1)
        f_cells = (
            (small_row >= 1) & (small_row <= box_y - 2) & (small_column >= 1) & (small_column <= box_z - 2)
            & (slab >= 1) & (slab <= n_slab - 2)
        )

        def groups(few, many, many_dim):
            shape = (few, many) if many_dim == 1 else (many, few)
            same = iota(shape, many_dim) // 3 == iota(shape, 1 - many_dim)
            return jnp.where(same, 1.0, 0.0).astype(jnp.bfloat16)

        def times(wide, matrix):
            return sum(jnp.dot(t, matrix, preferred_element_type=jnp.float32) for t in terms(wide))

        def times_left(matrix, wide):
            return sum(jnp.dot(matrix, t, preferred_element_type=jnp.float32) for t in terms(wide))

        def terms(value):
            out = []
            for _ in range(3):
                out.append(value.astype(jnp.bfloat16))
                value = value - out[-1].astype(jnp.float32)
            return out

        def upsampled(section):
            section = section.reshape(3 * box_y, box_z)
            wide = times(section, groups(box_z, depth, 1))
            return times_left(groups(3 * box_y, 3 * width, 0), wide).reshape(3, width, depth)

        def average():
            total = jnp.concatenate([E[0, c] + partial[c] for c in range(3)], axis=0)
            rows = times_left(groups(3 * box_y, 3 * width, 1), total)
            both = times(rows, groups(box_z, depth, 0))
            return (both * jnp.float32(1.0 / 27.0)).reshape(3, box_y, box_z)

        def boundary(sub):
            weight = jnp.float32((sub + 1) / 3.0)
            return [up_prev[c] + weight * (up_last[c] - up_prev[c]) for c in range(3)]

        def inject(ref, index, p, values):
            for c in range(3):
                ref[(*index, c)] = jnp.where(rims[p], values[c], ref[(*index, c)])

        def open_block(first_slot):
            oscillate(0, step, true)
            e = electric(0, true)
            put(AE, (), e)
            tell_left(first_slot, e)

        set_coefficients(step)
        wait_loads((0, 0), (1, 0), (2, 0), (3, 0), (1, 2))
        prepare()

        @pl.when(jnp.logical_not(borrows))
        def _():
            near_recv[...] = jnp.zeros_like(near_recv)

        @pl.when(jnp.logical_not(has_left))
        def _():
            f_recv[0] = jnp.zeros_like(f_recv[0])

        @pl.when(jnp.logical_not(has_right))
        def _():
            f_recv[1] = jnp.zeros_like(f_recv[1])

        pl.semaphore_wait(barrier, count(has_left, has_right))
        tell_right(0, H[2, 1], H[2, 2])
        open_block(0)
        go(has_left, m_to_left)
        go(has_right, m_to_right)
        wait_loads(*[(k, p) for k in range(4) for p in (1, 2) if (k, p) != (1, 2)])

        def latest(index):
            heard(True, section_copy(index, 0))
            heard(borrows, near_copy(index))
            k_c = table_recv[3]
            base = sec_recv[index]
            return (
                base[0],
                base[1] + k_c * near_recv[index, 1],
                base[2] - k_c * near_recv[index, 0],
            )

        def feedback_response():
            heard(has_left, f_copy(0))
            heard(has_right, f_copy(1))
            here, before, after = f_send, f_recv.at[0], f_recv.at[1]
            curl = curl_e((here[0], here[1], here[2]), (after[1], after[2]))
            back_x = (up_z(before[0]) - before[0], up_y(before[0]) - before[0])
            back_y = back_x[0] - (here[2] - before[2])
            back_z = (here[1] - before[1]) - back_x[1]
            twice = curl_h(curl, (back_y, back_z))
            return [-COURANT * table_recv[3] * t for t in twice]

        def block(b, carry):
            s0 = 3 * b
            for p in (1, 2):
                oscillate(p, step, true)
            electric_whole(2, true)
            electric_whole(1, true)
            h = magnetic(2, true)
            put(BH, (), h)
            tell_right(s0 + 1, h[1], h[2])
            magnetic_whole(1, true)
            curl = curl_e(get(AE), (E[1, 1], E[1, 2]))
            put(AH, (), [H[0, c] - COURANT * curl[c] for c in range(3)])

            @pl.when(b == 0)
            def _():
                heard(True, table_copy(0))
                up_last[...] = upsampled(table_recv[0:3])

            up_prev[...] = up_last[...]
            arrived = latest(b)

            @pl.when(b < STEPS - 1)
            def _():
                up_last[...] = upsampled(jnp.stack(arrived))

            @pl.when(b == STEPS - 1)
            def _():
                extra = feedback_response()
                up_last[...] = upsampled(jnp.stack([a + e for a, e in zip(arrived, extra)]))

            values = boundary(0)
            inject(AE, (), 0, values)
            inject(E, (1,), 1, values)
            inject(E, (2,), 2, values)
            a_j, a_p, a_e, k_c, k_j = (CO[k, 0] for k in range(5))
            for c in range(3):
                current = a_j * J[0, c] + a_p * Q[0, c] + a_e * AE[c]
                AJ[c] = current
                AQ[c] = Q[0, c] + step * current
            curl = curl_h(get(AH))
            e_0 = tuple(AE[c] - k_j * AJ[c] + k_c * curl[c] for c in range(3))
            put(AE, (), e_0)
            tell_left(s0 + 1, e_0)
            for p in (1, 2):
                oscillate(p, step, true)
            curl = curl_h(get(BH), (H[1, 1], H[1, 2]))
            e_2 = tuple(E[2, c] - CO[4, 2] * J[2, c] + CO[3, 2] * curl[c] for c in range(3))
            put(BE, (), e_2)
            curl = curl_e(e_2)
            h = tuple(BH[c] - COURANT * curl[c] for c in range(3))
            put(BH, (), h)
            tell_right(s0 + 2, h[1], h[2])
            curl = curl_h(get(H, 1), (AH[1], AH[2]))
            e_1 = tuple(E[1, c] - CO[4, 1] * J[1, c] + CO[3, 1] * curl[c] for c in range(3))
            put(A1, (), e_1)
            curl = curl_e(get(AE), (A1[1], A1[2]))
            put(AH, (), [AH[c] - COURANT * curl[c] for c in range(3)])
            values = boundary(1)
            inject(AE, (), 0, values)
            for c in range(3):
                current = a_j * AJ[c] + a_p * AQ[c] + a_e * AE[c]
                AJ[c] = current
                AQ[c] = AQ[c] + step * current
            curl = curl_h(get(AH))
            e_0 = tuple(AE[c] - k_j * AJ[c] + k_c * curl[c] for c in range(3))
            put(AE, (), e_0)
            tell_left(s0 + 2, e_0)

            @pl.when(b == 0)
            def _():
                learn_neighbours(step)

            def face(coefficients, k_near, k_back, there, h_own, e_own, hear):
                a_j, a_p, a_e, k_c, k_j = coefficients
                side = COURANT * there.astype(jnp.float32)

                def kept(u):
                    return jnp.where(edge, 0.0, u)

                hear(0)
                h_y, h_z = h_own(0)
                e_y, e_z = e_own(0)
                d_y, d_z = k_c * h_z, -k_c * h_y
                e_y, e_z = e_y + d_y, e_z + d_z
                l_y, l_z = side * e_z, -side * e_y
                d_h = tuple(-COURANT * u for u in curl_e((None, d_y, d_z)))
                d_y, d_z = kept(d_y), kept(d_z)
                j_y, j_z = a_e * d_y, a_e * d_z
                p_y, p_z = step * j_y, step * j_z
                hear(1)
                h_y, h_z = h_own(1)
                e_y, e_z = e_own(1)
                h_y, h_z = h_y + l_y, h_z + l_z
                curl = curl_h(d_h, (h_y, h_z))
                d_x = k_c * curl[0]
                d_y = d_y - k_j * j_y + k_c * curl[1]
                d_z = d_z - k_j * j_z + k_c * curl[2]
                e_y, e_z = e_y + d_y, e_z + d_z
                l_e = tuple(k_back * u for u in curl_h((None, l_y, l_z)))
                curl = curl_e(l_e)
                l_h = (
                    -COURANT * curl[0],
                    l_y - COURANT * curl[1] + side * e_z,
                    l_z - COURANT * curl[2] - side * e_y,
                )
                f_y, f_z = k_near * d_h[2], -k_near * d_h[1]
                curl = curl_e((d_x, d_y, d_z), (f_y, f_z))
                d_h = tuple(d_h[c] - COURANT * curl[c] for c in range(3))
                d_e = kept(d_x), kept(d_y), kept(d_z)
                d_j = (a_e * d_e[0], a_j * j_y + a_p * p_y + a_e * d_e[1], a_j * j_z + a_p * p_z + a_e * d_e[2])
                d_p = (step * d_j[0], p_y + step * d_j[1], p_z + step * d_j[2])
                curl = curl_h(d_h, (l_h[1], l_h[2]))
                d_e = tuple(d_e[c] - k_j * d_j[c] + k_c * curl[c] for c in range(3))
                return d_e, d_j, d_p, d_h, (f_y, f_z), l_e, l_h

            def hear_left(m):
                heard(has_left, h_copy(s0 + m))

            def hear_right(m):
                heard(has_right, b_copy(s0 + m))

            d_e, _, _, _, _, l_e, l_h = face(
                [CR[k] for k in range(5)], CR[5], CO[3, 2], has_right,
                lambda m: (h_send[s0 + m, 0], h_send[s0 + m, 1]),
                lambda m: (b_recv[s0 + m, 0], b_recv[s0 + m, 1]),
                hear_right,
            )
            k_c = CR[3]
            next_y = d_e[1] + k_c * h_send[s0 + 2, 1]
            next_z = d_e[2] - k_c * h_send[s0 + 2, 0]
            put(H, (2,), [BH[c] + l_h[c] for c in range(3)])
            put(E, (2,), [BE[c] + l_e[c] for c in range(3)])
            d_e, d_j, d_p, d_h, near, _, _ = face(
                [CO[k, 0] for k in range(5)], CO[3, 1], CL[...], has_left,
                lambda m: (h_recv[s0 + m, 0], h_recv[s0 + m, 1]),
                lambda m: (b_send[s0 + m, 0], b_send[s0 + m, 1]),
                hear_left,
            )
            put(H, (0,), [AH[c] + d_h[c] for c in range(3)])
            put(J, (0,), [AJ[c] + d_j[c] for c in range(3)])
            put(Q, (0,), [AQ[c] + d_p[c] for c in range(3)])
            put(AE, (), [AE[c] + d_e[c] for c in range(3)])
            put(E, (1,), [A1[0], A1[1] + near[0], A1[2] + near[1]])

            magnetic_whole(1, true)
            values = boundary(1)
            for p in (1, 2):
                inject(E, (p,), p, values)
                oscillate(p, step, true)
            electric_whole(2, true)
            electric_whole(1, true)
            magnetic_whole(1, true)
            values = boundary(2)
            put(H, (2,), magnetic(2, true))
            near_y, near_z = E[1, 1], E[1, 2]
            for p in (1, 2):
                inject(E, (p,), p, values)
            for c in range(3):
                partial[c] = E[1, c] + E[2, c]

            def close_right():
                hear_right(2)
                H[2, 1] = H[2, 1] + COURANT * (next_z + b_recv[s0 + 2, 1])
                H[2, 2] = H[2, 2] - COURANT * (next_y + b_recv[s0 + 2, 0])

            @pl.when(b < STEPS - 1)
            def _():
                close_right()
                tell_right(s0 + 3, H[2, 1], H[2, 2])

            hear_left(2)
            k_c = CO[3, 0]
            E[0, 0] = AE[0]
            E[0, 1] = AE[1] + k_c * h_recv[s0 + 2, 1]
            E[0, 2] = AE[2] - k_c * h_recv[s0 + 2, 0]
            put(H, (0,), magnetic(0, true, (near_y, near_z)))
            inject(E, (0,), 0, values)

            @pl.when(b < STEPS - 1)
            def _():
                open_block(s0 + 3)

            mean = average()
            mean_send[b] = mean
            for index in range(STEPS):

                @pl.when(b == index)
                def _(index=index):
                    mean_copy(index).start()

            pl.when(b == STEPS - 1)(close_right)

            @pl.when(b == 0)
            def _():
                g = table_recv[4]
                for c in range(3):
                    f_send[c] = jnp.where(f_cells, g * mean[c], 0.0)
                go(has_right, f_copy(0))
                go(has_left, f_copy(1))

            return carry

        lax.fori_loop(0, STEPS, block, 0)
        for k in range(4):
            write(k)
        for slot in range(STEPS * SUBS):
            sent(has_right, h_copy(slot))
            sent(has_left, b_copy(slot))
        sent(has_right, f_copy(0))
        sent(has_left, f_copy(1))
        for index in range(STEPS):
            mean_copy(index).wait_send()
        written()

    @pl.when(is_coarse)
    def _():
        step = STEP_COARSE
        load_off = pltpu.make_async_copy(off_in, off_ref, off_sem)
        load_off.start()
        load_off.wait()
        corner_y = off_ref[0]
        guess = (TE, TH, TQ, TJ)

        def cut(value):
            return pltpu.roll(value[:, depth - box_z : depth], width - corner_y, 0)[:box_y]

        row, column = iota((width, box_z), 0), iota((width, box_z), 1)
        interior = (row >= corner_y + 1) & (row <= corner_y + box_y - 2) & (column >= 1) & (column <= box_z - 2)

        def inside(p):
            return interior & (fine_at[p] >= 1) & (fine_at[p] <= n_slab - 2)

        def place(index):
            for p in range(PLANES):

                @pl.when(in_box[p])
                def _(p=p):
                    mean_arrival(index, p).wait_recv()
                    for c in range(3):
                        tall = jnp.concatenate([mean_recv[index, p, c]] * (width // box_y), axis=0)
                        placed = pltpu.roll(tall, corner_y, 0)
                        kept = E[p, c, :, depth - box_z : depth]
                        E[p, c, :, depth - box_z : depth] = jnp.where(inside(p), placed, kept)

        def take(index, p, values):
            for c in range(3):
                sec_send[index, p, c] = cut(values[c])

        def take_near(index, state):
            for c in range(2):
                near_send[index, c] = cut(state[1][2, 1 + c])

        def send(index):
            for p in range(PLANES):
                go(in_box[p], section_copy(index, p))
            go(in_box[PLANES], near_copy(index))

        def first_half(state, slot_h, slot_b):
            e, h, _, _ = state
            for p in (1, 2):
                oscillate(p, step, state)
            electric_whole(2, state)
            electric_whole(1, state)
            k_c = CO[3, 0]
            e[0, 0] = b_send[slot_b, 2]
            e[0, 1] = b_send[slot_b, 0] + k_c * h_recv[slot_h, 1]
            e[0, 2] = b_send[slot_b, 1] - k_c * h_recv[slot_h, 0]
            magnetic_whole(1, state)
            magnetic_whole(0, state)

        def second_half(state, slot_h, slot_b):
            heard(has_right, b_copy(slot_b))
            k_c = CR[3]
            ahead = (
                b_recv[slot_b, 0] + k_c * h_send[slot_h, 1],
                b_recv[slot_b, 1] - k_c * h_send[slot_h, 0],
            )
            put(state[1], (2,), magnetic(2, state, ahead))

        set_coefficients(step)
        wait_loads(*[(k, p) for k in range(4) for p in range(PLANES)])
        for p in range(PLANES):
            for c in range(3):
                table_send[p, c] = cut(E[p, c])
            table_send[p, 3] = cut(CO[3, p])
            table_send[p, 4] = 1.0 - cut(CO[4, p]) * cut(CO[2, p])
        h_send[0, 0], h_send[0, 1] = H[2, 1], H[2, 2]
        take_near(0, true)
        for p in range(PLANES):
            oscillate(p, step, true)
        start = electric(0, true)
        set_b(0, start)
        take(0, 0, start)
        electric_whole(2, true)
        electric_whole(1, true)
        for p in (1, 2):
            take(0, p, get(E, p))
        prepare()
        pl.semaphore_wait(barrier, count(has_left, has_right, *in_box))
        for p in range(PLANES):
            go(in_box[p], table_copy(p), section_copy(0, p))
        go(in_box[PLANES], near_copy(0))
        go(has_right, h_copy(0), m_to_right)
        go(has_left, b_copy(0), m_to_left)

        magnetic_whole(1, true)
        learn_neighbours(step)
        heard(has_left, h_copy(0))
        k_c = CO[3, 0]
        E[0, 0] = start[0]
        E[0, 1] = b_send[0, 0] + k_c * h_recv[0, 1]
        E[0, 2] = b_send[0, 1] - k_c * h_recv[0, 0]
        magnetic_whole(0, true)
        second_half(true, 0, 0)
        tell_right(1, H[2, 1], H[2, 2])

        take_near(1, true)
        for p in range(PLANES):
            for c in range(3):
                value = E[p, c]
                TE[p, c] = value
                kept = value[:, depth - box_z : depth]
                TE[p, c, :, depth - box_z : depth] = jnp.where(inside(p) & in_box[p], 0.0, kept)
                TH[p, c] = H[p, c]
                TQ[p, c] = Q[p, c]
                TJ[p, c] = J[p, c]
        oscillate(0, step, guess)
        start = electric(0, guess)
        tell_left(1, start)
        take(1, 0, start)
        for p in (1, 2):
            oscillate(p, step, guess)
        electric_whole(2, guess)
        electric_whole(1, guess)
        for p in (1, 2):
            take(1, p, get(TE, p))
        send(1)
        heard(has_left, h_copy(1))
        k_c = CO[3, 0]
        TE[0, 0] = b_send[1, 2]
        TE[0, 1] = b_send[1, 0] + k_c * h_recv[1, 1]
        TE[0, 2] = b_send[1, 1] - k_c * h_recv[1, 0]
        magnetic_whole(1, guess)
        magnetic_whole(0, guess)
        second_half(guess, 1, 1)
        take_near(2, guess)
        for p in range(PLANES):
            oscillate(p, step, guess)
            back = None if p == 0 else (TH[p - 1, 1], TH[p - 1, 2])
            take(2, p, electric(p, guess, back))
        send(2)

        place(0)
        oscillate(0, step, true)
        tell_left(2, electric(0, true))
        first_half(true, 1, 2)
        second_half(true, 1, 2)
        tell_right(2, H[2, 1], H[2, 2])
        place(1)
        oscillate(0, step, true)
        tell_left(3, electric(0, true))
        heard(has_left, h_copy(2))
        first_half(true, 2, 3)
        write(2)
        write(3)
        write(0)
        second_half(true, 2, 3)
        write(1)
        for slot in range(3):
            sent(has_right, h_copy(slot))
        for slot in range(4):
            sent(has_left, b_copy(slot))
        for p in range(PLANES):
            sent(in_box[p], table_copy(p), *[section_copy(index, p) for index in range(STEPS)])
        sent(in_box[PLANES], *[near_copy(index) for index in range(STEPS)])
        written()
        for p in range(PLANES):
            heard(in_box[p], mean_arrival(STEPS - 1, p))


def hand_over(n_slab, width, depth, off_in, mean_in, *refs):
    sources, targets = refs[:4], refs[4:8]
    off_ref, mean, held, load_sem, out_sem = refs[8:]
    loads = [pltpu.make_async_copy(sources[k].at[0], held.at[k], load_sem.at[k]) for k in range(4)]
    stores = [pltpu.make_async_copy(held.at[k], targets[k].at[0], out_sem.at[k]) for k in range(4)]
    load_off = pltpu.make_async_copy(off_in, off_ref, load_sem.at[4])
    load_mean = pltpu.make_async_copy(mean_in, mean, load_sem.at[5])
    load_off.start()
    load_mean.start()
    for load in loads:
        load.start()
    slab = lax.axis_index("slab")
    is_coarse = lax.axis_index("grid") == 0
    box_y, box_z = width // 3, depth // 3
    load_off.wait()
    load_mean.wait()
    corner_y = off_ref[0]
    row, column = iota((width, box_z), 0), iota((width, box_z), 1)
    interior = (row >= corner_y + 1) & (row <= corner_y + box_y - 2) & (column >= 1) & (column <= box_z - 2)
    loads[0].wait()
    for p in range(PLANES):
        fine = 3 * (slab - n_slab // 8) + p

        @pl.when(is_coarse & (fine >= 1) & (fine <= n_slab - 2))
        def _(p=p):
            for c in range(3):
                tall = jnp.concatenate([mean[p, c]] * (width // box_y), axis=0)
                placed = pltpu.roll(tall, corner_y, 0)
                kept = held[0, c, p, :, depth - box_z : depth]
                held[0, c, p, :, depth - box_z : depth] = jnp.where(interior, placed, kept)

    stores[0].start()
    for k in (1, 2, 3):
        loads[k].wait()
        stores[k].start()
    for store in stores:
        store.wait()


def on_device(n_slab, efield, hfield, polar, current, material, box_offset):
    planes, width, depth = efield.shape[2:]
    box = (width // 3, depth // 3)
    plane = (width, depth)
    f32 = jnp.float32
    dma = pltpu.SemaphoreType.DMA
    slots = STEPS * SUBS

    def room(*shape, dtype=f32):
        return pltpu.VMEM(shape, dtype)

    state = room(planes, 3, *plane)
    triple = room(3, *plane)
    scratch = [pltpu.SMEM((2,), jnp.int32)] + [state] * 8 + [
        room(planes, *plane, dtype=jnp.int32),
        room(5, planes, *plane),
        room(*plane, dtype=jnp.int32),
        room(2, *plane, dtype=jnp.int32),
        room(*plane),
        room(6, *plane),
    ]
    scratch += [triple] * 8
    scratch += [room(slots, 2, *plane), room(slots, 2, *plane), room(slots, 3, *plane), room(slots, 2, *plane)]
    scratch += [
        room(STEPS, planes, 3, *box),
        room(STEPS, 3, *box),
        room(planes, 5, *box),
        room(5, *box),
        room(STEPS, 2, *box),
        room(STEPS, 2, *box),
        triple,
        triple,
        room(STEPS, 3, *box),
        room(STEPS - 1, planes, 3, *box),
        room(3, *box),
        room(2, 3, *box),
    ]
    scratch += [dma, dma((5, planes)), dma((4, planes)), dma((4,))]
    scratch += [dma((slots,))] * 4
    scratch += [dma((STEPS, planes)), dma((STEPS,)), dma((planes,)), dma, dma((STEPS,)), dma((STEPS,))]
    scratch += [dma((STEPS,)), dma((STEPS, planes)), dma((2,)), dma((2,))]
    whole = pl.BlockSpec(memory_space=pl.ANY)
    fields = [jax.ShapeDtypeStruct(efield.shape, f32)] * 4
    state = pl.pallas_call(
        functools.partial(kernel, n_slab, width, depth),
        out_shape=fields + [jax.ShapeDtypeStruct((planes, 3, *box), f32)],
        in_specs=[whole] * 6,
        out_specs=[whole] * 5,
        scratch_shapes=scratch,
        compiler_params=pltpu.CompilerParams(
            collective_id=1, has_side_effects=True, vmem_limit_bytes=60 * 1024 * 1024
        ),
    )(box_offset, efield, hfield, polar, current, material)
    *state, mean = state
    return pl.pallas_call(
        functools.partial(hand_over, n_slab, width, depth),
        out_shape=fields,
        in_specs=[whole] * 6,
        out_specs=[whole] * 4,
        scratch_shapes=[
            pltpu.SMEM((2,), jnp.int32),
            room(planes, 3, *box),
            room(4, 3, planes, *plane),
            dma((6,)),
            dma((4,)),
        ],
        compiler_params=pltpu.CompilerParams(vmem_limit_bytes=60 * 1024 * 1024),
    )(box_offset, mean, *state)


def solution(mesh):
    field = P("grid", "angle", "slab", None, None)
    return jax.shard_map(
        functools.partial(on_device, mesh.shape["slab"]),
        mesh=mesh,
        in_specs=(field, field, field, field, P("grid", "slab", None, None), P()),
        out_specs=(field, field, field, field),
        check_vma=False,
    )
```

```python
import functools

import jax
import jax.numpy as jnp
from jax import lax
from jax.experimental import pallas as pl
from jax.experimental.pallas import tpu as pltpu
from jax.sharding import PartitionSpec as P

STEPS = 3
SUBS = 3
PERMITTIVITY = (1.0, 1.5, 1.2, 2.0)
STRENGTH = (0.4, 0.9, 0.3, 1.1)
RESONANCE = (0.6, 0.5, 0.8, 0.3)
DAMPING_RATE = (0.3, 0.2, 0.05, 0.4)
COURANT = 0.5
STEP_COARSE = 0.5
STEP_FINE = STEP_COARSE / 3.0
PLANES = 3
MESH = pl.DeviceIdType.MESH
EXACT = lax.Precision.HIGHEST


def tables(step):
    rows = zip(PERMITTIVITY, STRENGTH, RESONANCE, DAMPING_RATE)
    return [
        (1.0 - step * d, -step * r, step * s * r, COURANT / e, step / e) for e, s, r, d in rows
    ]


def pick(material, values):
    out = jnp.full(material.shape, values[0], jnp.float32)
    for index in range(1, 4):
        out = jnp.where(material == index, jnp.float32(values[index]), out)
    return out


def iota(shape, dim):
    return lax.broadcasted_iota(jnp.int32, shape, dim)


def down_y(u):
    return jnp.where(iota(u.shape, 0) == 0, 0.0, pltpu.roll(u, 1, 0))


def up_y(u):
    last = u.shape[0] - 1
    return jnp.where(iota(u.shape, 0) == last, 0.0, pltpu.roll(u, last, 0))


def down_z(u):
    return jnp.where(iota(u.shape, 1) == 0, 0.0, pltpu.roll(u, 1, 1))


def up_z(u):
    last = u.shape[1] - 1
    return jnp.where(iota(u.shape, 1) == last, 0.0, pltpu.roll(u, last, 1))


def curl_h(h, back=None):
    x, y, z = h
    c_x = (z - down_y(z)) - (y - down_z(y))
    c_y, c_z = -z, y
    if x is not None:
        c_y, c_z = (x - down_z(x)) - z, y - (x - down_y(x))
    if back is not None:
        c_y, c_z = c_y + back[1], c_z - back[0]
    return c_x, c_y, c_z


def curl_e(e, ahead=None):
    x, y, z = e
    c_x = (up_y(z) - z) - (up_z(y) - y)
    c_y, c_z = z, -y
    if x is not None:
        c_y, c_z = (up_z(x) - x) + z, -y - (up_y(x) - x)
    if ahead is not None:
        c_y, c_z = c_y - ahead[1], c_z + ahead[0]
    return c_x, c_y, c_z


def groups(few, many, many_dim):
    shape = (few, many) if many_dim == 1 else (many, few)
    return ones_where(iota(shape, many_dim) // 3 == iota(shape, 1 - many_dim))


def ones_where(condition):
    return jnp.where(condition, 1.0, 0.0).astype(jnp.bfloat16)


def terms(value):
    out = []
    for _ in range(3):
        out.append(value.astype(jnp.bfloat16))
        value = value - out[-1].astype(jnp.float32)
    return out


def times(wide, matrix):
    return sum(jnp.dot(t, matrix, preferred_element_type=jnp.float32) for t in terms(wide))


def times_left(matrix, wide):
    return sum(jnp.dot(matrix, t, preferred_element_type=jnp.float32) for t in terms(wide))


def times_turned(matrix, wide):
    return sum(
        lax.dot_general(matrix, t, (((1,), (1,)), ((), ())), preferred_element_type=jnp.float32)
        for t in terms(wide)
    )


def pack(sections):
    box_y, box_z = sections[0].shape
    tall = jnp.concatenate(sections, axis=0)
    shape = (8, 3 * box_y)
    row, column = iota(shape, 0), iota(shape, 1)
    ends = ones_where((row < 6) & (column == (row // 2) * box_y + (row % 2) * (box_y - 1)))
    shape = (8, box_z)
    row, column = iota(shape, 0), iota(shape, 1)
    sides = ones_where(((row == 6) & (column == 0)) | ((row == 7) & (column == box_z - 1)))
    padded = jnp.concatenate([tall, jnp.zeros((box_z - 3 * box_y, box_z), jnp.float32)], axis=0)
    return times_left(ends, tall) + times_turned(sides, padded)


def unpack(packs, width, depth):
    box_y, box_z = width // 3, depth // 3
    tall = jnp.concatenate(packs, axis=0)
    wide = times(tall, groups(box_z, depth, 1))
    shape = (3 * width, box_z)
    spread = times_turned(ones_where(iota(shape, 1) == iota(shape, 0) // 3), tall)
    row, column = iota((width, depth), 0), iota((width, depth), 1)
    planes = []
    for j in range(len(packs)):
        plane = []
        for c in range(3):
            at = 8 * j + 2 * c
            side = spread[c * width : (c + 1) * width]
            value = jnp.where(column == 0, side[:, 8 * j + 6 : 8 * j + 7], 0.0)
            value = jnp.where(column == depth - 1, side[:, 8 * j + 7 : 8 * j + 8], value)
            value = jnp.where(row == 0, wide[at : at + 1], value)
            plane.append(jnp.where(row == width - 1, wide[at + 1 : at + 2], value))
        planes.append(plane)
    return planes


def kernel(
    n_slab, width, depth,
    off_in, e_in, h_in, p_in, j_in, m_in,
    e_out, h_out, p_out, j_out, mean_out,
    off_ref, E, H, Q, J, TE, TH, TQ, TJ, M, CO, m_left, m_right, CL, CR,
    AE, AH, AQ, AJ, A1, BE, BH, partial,
    h_send, h_recv, b_send, b_recv,
    sec_send, sec_recv, table_send, table_recv, near_send, near_recv,
    U, GA, DH, DJ, DQ, DE, mean_send, mean_recv, f_send, f_recv,
    pack_send, pack_recv, kp_send, kp_recv, rim_send, rim_recv, D, d_send, d_recv,
    off_sem, load_sem, out_sem, m_sem,
    hs_sem, hr_sem, bs_sem, br_sem, ss_sem, sr_sem, ts_sem, tr_sem, ns_sem, nr_sem,
    ms_sem, mr_sem, fs_sem, fr_sem,
    ps_sem, pr_sem, ks_sem, kr_sem, es_sem, er_sem, ds_sem, dr_sem,
):
    slab = lax.axis_index("slab")
    level = lax.axis_index("grid")
    box_y, box_z = width // 3, depth // 3
    first_slab = n_slab // 8
    is_fine = level == 1
    is_coarse = level == 0
    has_left = slab > 0
    has_right = slab < n_slab - 1
    partner_slab = first_slab + slab // 3
    partner_plane = slab % 3
    outer = (slab == 0) | (slab == n_slab - 1)
    borrows = outer & (partner_plane == 0)
    seam = jnp.where(partner_plane == 0, 1, jnp.where(partner_plane == 1, 0, 2))
    has_seam = slab + seam - 1 < n_slab
    near_fines = [3 * (slab - first_slab) + k for k in range(-1, PLANES + 2)]
    listens = [(f >= 0) & (f < n_slab) for f in near_fines]
    listens[0] = listens[0] & (near_fines[1] < n_slab)
    fine_at = [3 * (slab - first_slab) + p for p in range(PLANES + 1)]
    in_box = [(f >= 0) & (f < n_slab) for f in fine_at]
    full_at = [(f == 0) | (f == n_slab - 1) for f in fine_at]

    fields = ((e_in, E, e_out), (h_in, H, h_out), (p_in, Q, p_out), (j_in, J, j_out))
    loads = [
        [pltpu.make_async_copy(src.at[0, :, p], dst.at[p], load_sem.at[k, p]) for p in range(PLANES)]
        for k, (src, dst, _) in enumerate(fields)
    ]
    load_m = pltpu.make_async_copy(m_in.at[0], M, load_sem.at[4, 0])

    barrier = pltpu.get_barrier_semaphore()

    def greet(condition, target):
        @pl.when(condition)
        def _():
            pl.semaphore_signal(barrier, inc=1, device_id=target, device_id_type=MESH)

    def count(*conditions):
        return sum(c.astype(jnp.int32) for c in conditions)

    greet(is_fine, {"grid": 0, "slab": partner_slab})
    greet(is_fine & (partner_plane < 2), {"grid": 0, "slab": partner_slab - 1})
    greet(is_fine & (partner_plane == 2) & has_right, {"grid": 0, "slab": partner_slab + 1})
    greet(has_left, {"slab": slab - 1})
    greet(has_right, {"slab": slab + 1})

    load_m.start()
    for p in range(PLANES):
        for k in range(4):
            loads[k][p].start()

    def remote(src, dst, send, recv, target):
        return pltpu.make_async_remote_copy(
            src_ref=src, dst_ref=dst, send_sem=send, recv_sem=recv, device_id=target, device_id_type=MESH
        )

    left, right = {"slab": slab - 1}, {"slab": slab + 1}

    def h_copy(slot):
        return remote(h_send.at[slot], h_recv.at[slot], hs_sem.at[slot], hr_sem.at[slot], right)

    def b_copy(slot):
        return remote(b_send.at[slot, 0:2], b_recv.at[slot], bs_sem.at[slot], br_sem.at[slot], left)

    m_to_left = remote(m_in.at[0, 0:2], m_right, m_sem.at[0], m_sem.at[1], left)
    m_to_right = remote(m_in.at[0, 2], m_left, m_sem.at[2], m_sem.at[3], right)

    def section_copy(index, p):
        return remote(
            sec_send.at[index, p], sec_recv.at[index], ss_sem.at[index, p], sr_sem.at[index],
            {"grid": 1, "slab": fine_at[p]},
        )

    def table_copy(p):
        return remote(
            table_send.at[p], table_recv, ts_sem.at[p], tr_sem, {"grid": 1, "slab": fine_at[p]}
        )

    def near_copy(index):
        return remote(
            near_send.at[index], near_recv.at[index], ns_sem.at[index], nr_sem.at[index],
            {"grid": 1, "slab": fine_at[PLANES]},
        )

    def mean_copy(index):
        room = mean_out if index == STEPS - 1 else mean_recv.at[index]
        return remote(
            mean_send.at[index], room.at[partner_plane], ms_sem.at[index],
            mr_sem.at[index, partner_plane], {"grid": 0, "slab": partner_slab},
        )

    def mean_arrival(index, p):
        room = mean_out if index == STEPS - 1 else mean_recv.at[index]
        return remote(
            mean_send.at[index], room.at[p], ms_sem.at[index], mr_sem.at[index, p],
            {"grid": 1, "slab": fine_at[p]},
        )

    def f_copy(side):
        return remote(f_send, f_recv.at[side], fs_sem.at[side], fr_sem.at[side], right if side == 0 else left)

    def pack_copy(index, p, k):
        return remote(
            pack_send.at[index, p], pack_recv.at[index, 2 - k], ps_sem.at[index, p, k], pr_sem.at[index, 2 - k],
            {"grid": 1, "slab": fine_at[p] + k - 1},
        )

    def kp_copy(k):
        return remote(kp_send, kp_recv, ks_sem.at[k], kr_sem, {"grid": 1, "slab": fine_at[0] + k - 1})

    def rim_copy(index, k):
        return remote(
            rim_send.at[index], rim_recv.at[index], es_sem.at[index, k], er_sem.at[index],
            {"grid": 1, "slab": fine_at[PLANES] + k - 1},
        )

    def d_copy(side):
        return remote(d_send, d_recv.at[side], ds_sem.at[side], dr_sem.at[side], right if side == 0 else left)

    def reaches(p, k):
        target = fine_at[p] + k - 1
        return in_box[p] & (target >= 0) & (target < n_slab)

    def go(condition, *copies):
        @pl.when(condition)
        def _():
            for copy in copies:
                copy.start()

    def heard(condition, *copies):
        @pl.when(condition)
        def _():
            for copy in copies:
                copy.wait_recv()

    def sent(condition, *copies):
        @pl.when(condition)
        def _():
            for copy in copies:
                copy.wait_send()

    def get(ref, *index):
        return tuple(ref[(*index, c)] for c in range(3))

    def put(ref, index, values):
        for c, value in enumerate(values):
            if value is not None:
                ref[(*index, c)] = value

    def oscillate(p, step, state):
        e, _, q, j = state
        a_j, a_p, a_e = CO[0, p], CO[1, p], CO[2, p]
        for c in range(3):
            current = a_j * j[p, c] + a_p * q[p, c] + a_e * e[p, c]
            j[p, c] = current
            q[p, c] = q[p, c] + step * current

    def electric(p, state, back=None):
        e, h, _, j = state
        k_c, k_j = CO[3, p], CO[4, p]
        curl = curl_h(get(h, p), back)
        return tuple(e[p, c] - k_j * j[p, c] + k_c * curl[c] for c in range(3))

    def electric_whole(p, state):
        put(state[0], (p,), electric(p, state, (state[1][p - 1, 1], state[1][p - 1, 2])))

    def magnetic(p, state, ahead=None):
        e, h, _, _ = state
        curl = curl_e(get(e, p), ahead)
        return tuple(h[p, c] - COURANT * curl[c] for c in range(3))

    def magnetic_whole(p, state):
        put(state[1], (p,), magnetic(p, state, (state[0][p + 1, 1], state[0][p + 1, 2])))

    def set_coefficients(step):
        load_m.wait()
        values = tables(step)
        for p in range(PLANES):
            material = M[p]
            for k in range(5):
                CO[k, p] = pick(material, [row[k] for row in values])

    def learn_neighbours(step):
        heard(has_right, m_to_left)
        heard(has_left, m_to_right)
        sent(has_left, m_to_left)
        sent(has_right, m_to_right)
        values = tables(step)
        near, far = m_right[0], m_right[1]
        is_there = has_right.astype(jnp.float32)
        for k in range(5):
            scale = is_there if k == 3 else 1.0
            CR[k] = pick(near, [row[k] for row in values]) * scale
        CR[5] = pick(far, [row[3] for row in values]) * is_there
        before = m_left[...]
        CL[...] = pick(before, [row[3] for row in values]) * has_left.astype(jnp.float32)
        gains = [1.0 - row[4] * row[2] for row in values]
        for q, material in enumerate((before, M[0], M[1], M[2], near, far)):
            GA[q] = pick(material, gains)

    def prepare():
        @pl.when(jnp.logical_not(has_left))
        def _():
            h_recv[...] = jnp.zeros_like(h_recv)
            m_left[...] = jnp.zeros_like(m_left)

        @pl.when(jnp.logical_not(has_right))
        def _():
            b_recv[...] = jnp.zeros_like(b_recv)
            m_right[...] = jnp.zeros_like(m_right)

    def tell_right(slot, y, z):
        h_send[slot, 0], h_send[slot, 1] = y, z
        go(has_right, h_copy(slot))

    def set_b(slot, b):
        b_send[slot, 0], b_send[slot, 1], b_send[slot, 2] = b[1], b[2], b[0]

    def tell_left(slot, b):
        set_b(slot, b)
        go(has_left, b_copy(slot))

    def wait_loads(*which):
        for k, p in which:
            loads[k][p].wait()

    def write(k):
        for p in range(PLANES):
            pltpu.make_async_copy(fields[k][1].at[p], fields[k][2].at[0, :, p], out_sem.at[k, p]).start()

    def written():
        for k in range(4):
            for p in range(PLANES):
                pltpu.make_async_copy(fields[k][1].at[p], fields[k][2].at[0, :, p], out_sem.at[k, p]).wait()

    true = (E, H, Q, J)

    @pl.when(is_fine)
    def _():
        step = STEP_FINE
        row, column = iota((width, depth), 0), iota((width, depth), 1)
        edge = (row == 0) | (row == width - 1) | (column == 0) | (column == depth - 1)
        rims = [edge | (slab == 0), edge, edge | (slab == n_slab - 1)]
        small_row, small_column = iota((box_y, box_z), 0), iota((box_y, box_z), 1)
        f_cells = (
            (small_row >= 1) & (small_row <= box_y - 2) & (small_column >= 1) & (small_column <= box_z - 2)
            & (slab >= 1) & (slab <= n_slab - 2)
        )

        def upsampled(section):
            section = section.reshape(3 * box_y, box_z)
            wide = times(section, groups(box_z, depth, 1))
            return times_left(groups(3 * box_y, 3 * width, 0), wide).reshape(3, width, depth)

        def average():
            total = jnp.concatenate([E[0, c] + partial[c] for c in range(3)], axis=0)
            rows = times_left(groups(3 * box_y, 3 * width, 1), total)
            both = times(rows, groups(box_z, depth, 0))
            return (both * jnp.float32(1.0 / 27.0)).reshape(3, box_y, box_z)

        def boundary(b, sub, j=1):
            weight = jnp.float32((sub + 1) / 3.0)
            before, after = U.at[b % 2, j], U.at[(b + 1) % 2, j]
            return [before[c] + weight * (after[c] - before[c]) for c in range(3)]

        def inject(ref, index, p, values):
            for c in range(3):
                ref[(*index, c)] = jnp.where(rims[p], values[c], ref[(*index, c)])

        def open_block(first_slot):
            oscillate(0, step, true)
            e = electric(0, true)
            put(AE, (), e)
            tell_left(first_slot, e)

        set_coefficients(step)
        wait_loads((0, 0), (1, 0), (2, 0), (3, 0), (1, 2))
        prepare()

        @pl.when(outer & jnp.logical_not(borrows))
        def _():
            near_recv[...] = jnp.zeros_like(near_recv)

        @pl.when(jnp.logical_not(has_seam))
        def _():
            kp_recv[...] = jnp.zeros_like(kp_recv)
            rim_recv[...] = jnp.zeros_like(rim_recv)

        @pl.when(jnp.logical_not(has_left))
        def _():
            f_recv[0] = jnp.zeros_like(f_recv[0])
            d_recv[0] = jnp.zeros_like(d_recv[0])
            for index in range(STEPS):
                pack_recv[index, 0] = jnp.zeros_like(pack_recv[index, 0])

        @pl.when(jnp.logical_not(has_right))
        def _():
            f_recv[1] = jnp.zeros_like(f_recv[1])
            d_recv[1] = jnp.zeros_like(d_recv[1])
            for index in range(STEPS):
                pack_recv[index, 2] = jnp.zeros_like(pack_recv[index, 2])

        pl.semaphore_wait(barrier, count(has_left, has_right))
        tell_right(0, H[2, 1], H[2, 2])
        open_block(0)
        go(has_left, m_to_left)
        go(has_right, m_to_right)
        wait_loads(*[(k, p) for k in range(4) for p in (1, 2) if (k, p) != (1, 2)])

        def fill(slot, packs, section):
            for j, plane in enumerate(unpack(packs, width, depth)):
                for c in range(3):
                    U[slot, j, c] = plane[c]

            @pl.when(outer)
            def _():
                whole = upsampled(section())
                for c in range(3):
                    U[slot, 1, c] = whole[c]

        def rim_values(b):
            heard(True, pack_copy(b, 0, 1))
            heard(has_left, pack_copy(b, 0, 2))
            heard(has_right, pack_copy(b, 0, 0))
            heard(has_seam, rim_copy(b, 0))
            heard(outer, section_copy(b, 0))
            heard(borrows, near_copy(b))

            @pl.when(b == 0)
            def _():
                heard(has_seam, kp_copy(0))
                heard(True, table_copy(0))
                fill(0, [pack_recv[0, j, 1] for j in range(3)], lambda: table_recv[0:3])

            seamed = kp_recv[...] * rim_recv[b]
            packs = [pack_recv[b, j, 0] + seamed * (seam == j).astype(jnp.float32) for j in range(3)]

            def section(extra=None):
                k_c = table_recv[3]
                base = sec_recv[b]
                parts = [
                    base[0], base[1] + k_c * near_recv[b, 1], base[2] - k_c * near_recv[b, 0],
                ]
                if extra is not None:
                    parts = [part + extra[c] for c, part in enumerate(parts)]
                return jnp.stack(parts)

            @pl.when(b < STEPS - 1)
            def _():
                fill((b + 1) % 2, packs, section)

            @pl.when(b == STEPS - 1)
            def _():
                heard(has_left, d_copy(0))
                heard(has_right, d_copy(1))
                extras = (d_recv[0], d_send[...], d_recv[1])
                fill((b + 1) % 2, [p + e for p, e in zip(packs, extras)], lambda: section(D))

            first = [boundary(b, 0, 0)]
            second = [None]
            for p in range(PLANES):
                first.append([jnp.where(rims[p], v, 0.0) for v in boundary(b, 0)])
                second.append([jnp.where(rims[p], v, 0.0) for v in boundary(b, 1)])
            first += [boundary(b, 0, 2)] * 2
            second.append(boundary(b, 1, 2))
            d_e = [[GA[q] * v for v in first[q]] for q in range(6)]
            d_h = []
            for q in range(5):
                curl = curl_e(d_e[q], (d_e[q + 1][1], d_e[q + 1][2]))
                d_h.append([-COURANT * u for u in curl])
            there = has_left.astype(jnp.float32)
            d_h[0] = [there * u for u in d_h[0]]
            for p in range(PLANES):
                put(DH, (p,), d_h[p + 1])
            for p in (1, 2):
                d_j = [CO[2, p] * v for v in first[p + 1]]
                put(DJ, (p,), d_j)
                put(DQ, (p,), [step * v for v in d_j])
            for q, at in ((1, 0), (4, 1)):
                a_j, a_p, a_e, k_c, k_j = [CO[k, 0] for k in range(5)] if at == 0 else [CR[k] for k in range(5)]
                curl = curl_h(d_h[q], (d_h[q - 1][1], d_h[q - 1][2]))
                for c in range(3):
                    early = a_e * first[q][c]
                    late = (a_j + step * a_p) * early + a_e * second[q][c]
                    DE[at, c] = second[q][c] - k_j * late + k_c * curl[c]
                    if at == 0:
                        DJ[0, c] = late
                        DQ[0, c] = step * (early + late)

        def feedback_response():
            heard(has_left, f_copy(0))
            heard(has_right, f_copy(1))
            here, before, after = f_send, f_recv.at[0], f_recv.at[1]
            curl = curl_e((here[0], here[1], here[2]), (after[1], after[2]))
            back_x = (up_z(before[0]) - before[0], up_y(before[0]) - before[0])
            back_y = back_x[0] - (here[2] - before[2])
            back_z = (here[1] - before[1]) - back_x[1]
            twice = curl_h(curl, (back_y, back_z))
            return [-COURANT * table_recv[3] * t for t in twice]

        def block(b, carry):
            s0 = 3 * b
            for p in (1, 2):
                oscillate(p, step, true)
            electric_whole(2, true)
            electric_whole(1, true)
            h = magnetic(2, true)
            put(BH, (), h)
            tell_right(s0 + 1, h[1], h[2])
            magnetic_whole(1, true)
            curl = curl_e(get(AE), (E[1, 1], E[1, 2]))
            put(AH, (), [H[0, c] - COURANT * curl[c] for c in range(3)])

            nothing = [jnp.zeros((width, depth), jnp.float32)] * 3
            inject(AE, (), 0, nothing)
            inject(E, (1,), 1, nothing)
            inject(E, (2,), 2, nothing)
            a_j, a_p, a_e, k_c, k_j = (CO[k, 0] for k in range(5))
            for c in range(3):
                current = a_j * J[0, c] + a_p * Q[0, c] + a_e * AE[c]
                AJ[c] = current
                AQ[c] = Q[0, c] + step * current
            curl = curl_h(get(AH))
            e_0 = tuple(AE[c] - k_j * AJ[c] + k_c * curl[c] for c in range(3))
            put(AE, (), e_0)
            tell_left(s0 + 1, e_0)
            for p in (1, 2):
                oscillate(p, step, true)
            curl = curl_h(get(BH), (H[1, 1], H[1, 2]))
            e_2 = tuple(E[2, c] - CO[4, 2] * J[2, c] + CO[3, 2] * curl[c] for c in range(3))
            put(BE, (), e_2)
            curl = curl_e(e_2)
            h = tuple(BH[c] - COURANT * curl[c] for c in range(3))
            put(BH, (), h)
            tell_right(s0 + 2, h[1], h[2])
            curl = curl_h(get(H, 1), (AH[1], AH[2]))
            e_1 = tuple(E[1, c] - CO[4, 1] * J[1, c] + CO[3, 1] * curl[c] for c in range(3))
            put(A1, (), e_1)
            curl = curl_e(get(AE), (A1[1], A1[2]))
            put(AH, (), [AH[c] - COURANT * curl[c] for c in range(3)])
            inject(AE, (), 0, nothing)
            for c in range(3):
                current = a_j * AJ[c] + a_p * AQ[c] + a_e * AE[c]
                AJ[c] = current
                AQ[c] = AQ[c] + step * current
            curl = curl_h(get(AH))
            e_0 = tuple(AE[c] - k_j * AJ[c] + k_c * curl[c] for c in range(3))
            put(AE, (), e_0)
            tell_left(s0 + 2, e_0)

            @pl.when(b == 0)
            def _():
                learn_neighbours(step)

            @pl.when(b == 1)
            def _():
                extra = feedback_response()
                for c in range(3):
                    D[c] = extra[c]
                d_send[...] = pack(extra)
                go(has_right, d_copy(0))
                go(has_left, d_copy(1))

            @pl.when(b > 0)
            def _():
                rim_values(b)

            def face(coefficients, k_near, k_back, there, h_own, e_own, hear):
                a_j, a_p, a_e, k_c, k_j = coefficients
                side = COURANT * there.astype(jnp.float32)

                def kept(u):
                    return jnp.where(edge, 0.0, u)

                hear(0)
                h_y, h_z = h_own(0)
                e_y, e_z = e_own(0)
                d_y, d_z = k_c * h_z, -k_c * h_y
                e_y, e_z = e_y + d_y, e_z + d_z
                l_y, l_z = side * e_z, -side * e_y
                d_h = tuple(-COURANT * u for u in curl_e((None, d_y, d_z)))
                d_y, d_z = kept(d_y), kept(d_z)
                j_y, j_z = a_e * d_y, a_e * d_z
                p_y, p_z = step * j_y, step * j_z
                hear(1)
                h_y, h_z = h_own(1)
                e_y, e_z = e_own(1)
                h_y, h_z = h_y + l_y, h_z + l_z
                curl = curl_h(d_h, (h_y, h_z))
                d_x = k_c * curl[0]
                d_y = d_y - k_j * j_y + k_c * curl[1]
                d_z = d_z - k_j * j_z + k_c * curl[2]
                e_y, e_z = e_y + d_y, e_z + d_z
                l_e = tuple(k_back * u for u in curl_h((None, l_y, l_z)))
                curl = curl_e(l_e)
                l_h = (
                    -COURANT * curl[0],
                    l_y - COURANT * curl[1] + side * e_z,
                    l_z - COURANT * curl[2] - side * e_y,
                )
                f_y, f_z = k_near * d_h[2], -k_near * d_h[1]
                curl = curl_e((d_x, d_y, d_z), (f_y, f_z))
                d_h = tuple(d_h[c] - COURANT * curl[c] for c in range(3))
                d_e = kept(d_x), kept(d_y), kept(d_z)
                d_j = (a_e * d_e[0], a_j * j_y + a_p * p_y + a_e * d_e[1], a_j * j_z + a_p * p_z + a_e * d_e[2])
                d_p = (step * d_j[0], p_y + step * d_j[1], p_z + step * d_j[2])
                curl = curl_h(d_h, (l_h[1], l_h[2]))
                d_e = tuple(d_e[c] - k_j * d_j[c] + k_c * curl[c] for c in range(3))
                return d_e, d_j, d_p, d_h, (f_y, f_z), l_e, l_h

            def hear_left(m):
                heard(has_left, h_copy(s0 + m))

            def hear_right(m):
                heard(has_right, b_copy(s0 + m))

            d_e, _, _, _, _, l_e, l_h = face(
                [CR[k] for k in range(5)], CR[5], CO[3, 2], has_right,
                lambda m: (h_send[s0 + m, 0], h_send[s0 + m, 1]),
                lambda m: (b_recv[s0 + m, 0], b_recv[s0 + m, 1]),
                hear_right,
            )
            k_c = CR[3]
            next_y = d_e[1] + k_c * h_send[s0 + 2, 1]
            next_z = d_e[2] - k_c * h_send[s0 + 2, 0]
            put(H, (2,), [BH[c] + l_h[c] for c in range(3)])
            put(E, (2,), [BE[c] + l_e[c] for c in range(3)])
            d_e, d_j, d_p, d_h, near, _, _ = face(
                [CO[k, 0] for k in range(5)], CO[3, 1], CL[...], has_left,
                lambda m: (h_recv[s0 + m, 0], h_recv[s0 + m, 1]),
                lambda m: (b_send[s0 + m, 0], b_send[s0 + m, 1]),
                hear_left,
            )
            put(H, (0,), [AH[c] + d_h[c] for c in range(3)])
            put(J, (0,), [AJ[c] + d_j[c] for c in range(3)])
            put(Q, (0,), [AQ[c] + d_p[c] for c in range(3)])
            put(AE, (), [AE[c] + d_e[c] for c in range(3)])
            put(E, (1,), [A1[0], A1[1] + near[0], A1[2] + near[1]])

            magnetic_whole(1, true)

            @pl.when(b == 0)
            def _():
                rim_values(b)

            next_y = next_y + DE[1, 1]
            next_z = next_z + DE[1, 2]
            values = boundary(b, 1)
            for c in range(3):
                for p in range(PLANES):
                    H[p, c] = H[p, c] + DH[p, c]
                    J[p, c] = J[p, c] + DJ[p, c]
                    Q[p, c] = Q[p, c] + DQ[p, c]
                AE[c] = AE[c] + DE[0, c]
            for p in (1, 2):
                inject(E, (p,), p, values)
                oscillate(p, step, true)
            electric_whole(2, true)
            electric_whole(1, true)
            magnetic_whole(1, true)
            values = boundary(b, 2)
            put(H, (2,), magnetic(2, true))
            near_y, near_z = E[1, 1], E[1, 2]
            for p in (1, 2):
                inject(E, (p,), p, values)
            for c in range(3):
                partial[c] = E[1, c] + E[2, c]

            def close_right():
                hear_right(2)
                H[2, 1] = H[2, 1] + COURANT * (next_z + b_recv[s0 + 2, 1])
                H[2, 2] = H[2, 2] - COURANT * (next_y + b_recv[s0 + 2, 0])

            @pl.when(b < STEPS - 1)
            def _():
                close_right()
                tell_right(s0 + 3, H[2, 1], H[2, 2])

            hear_left(2)
            k_c = CO[3, 0]
            E[0, 0] = AE[0]
            E[0, 1] = AE[1] + k_c * h_recv[s0 + 2, 1]
            E[0, 2] = AE[2] - k_c * h_recv[s0 + 2, 0]
            put(H, (0,), magnetic(0, true, (near_y, near_z)))
            inject(E, (0,), 0, values)

            @pl.when(b < STEPS - 1)
            def _():
                open_block(s0 + 3)

            mean = average()
            mean_send[b] = mean
            for index in range(STEPS):

                @pl.when(b == index)
                def _(index=index):
                    mean_copy(index).start()

            pl.when(b == STEPS - 1)(close_right)

            @pl.when(b == 0)
            def _():
                g = table_recv[4]
                for c in range(3):
                    f_send[c] = jnp.where(f_cells, g * mean[c], 0.0)
                go(has_right, f_copy(0))
                go(has_left, f_copy(1))

            return carry

        lax.fori_loop(0, STEPS, block, 0)
        for k in range(4):
            write(k)
        for slot in range(STEPS * SUBS):
            sent(has_right, h_copy(slot))
            sent(has_left, b_copy(slot))
        sent(has_right, f_copy(0), d_copy(0))
        sent(has_left, f_copy(1), d_copy(1))
        for index in range(STEPS):
            mean_copy(index).wait_send()
        written()

    @pl.when(is_coarse)
    def _():
        step = STEP_COARSE
        load_off = pltpu.make_async_copy(off_in, off_ref, off_sem)
        load_off.start()
        load_off.wait()
        corner_y = off_ref[0]
        guess = (TE, TH, TQ, TJ)

        def cut(value):
            return pltpu.roll(value[:, depth - box_z : depth], width - corner_y, 0)[:box_y]

        row, column = iota((width, box_z), 0), iota((width, box_z), 1)
        interior = (row >= corner_y + 1) & (row <= corner_y + box_y - 2) & (column >= 1) & (column <= box_z - 2)

        def inside(p):
            return interior & (fine_at[p] >= 1) & (fine_at[p] <= n_slab - 2)

        def place(index):
            for p in range(PLANES):

                @pl.when(in_box[p])
                def _(p=p):
                    mean_arrival(index, p).wait_recv()
                    for c in range(3):
                        tall = jnp.concatenate([mean_recv[index, p, c]] * (width // box_y), axis=0)
                        placed = pltpu.roll(tall, corner_y, 0)
                        kept = E[p, c, :, depth - box_z : depth]
                        E[p, c, :, depth - box_z : depth] = jnp.where(inside(p), placed, kept)

        def take(index, p, values):
            for c in range(3):
                sec_send[index, p, c] = cut(values[c])

        def take_near(index, state):
            for c in range(2):
                near_send[index, c] = cut(state[1][2, 1 + c])

        def get_section(index, p):
            return [sec_send[index, p, c] for c in range(3)]

        def take_rim(index):
            zero = jnp.zeros((box_y, box_z), jnp.float32)
            rim_send[index] = pack([zero, near_send[index, 1], -near_send[index, 0]])

        def send(index):
            for p in range(PLANES):
                for k in (1, 0, 2):
                    go(reaches(p, k), pack_copy(index, p, k))
                if p == 0:
                    for k in range(3):
                        go(reaches(PLANES, k), rim_copy(index, k))
            for p in range(PLANES):
                go(in_box[p] & full_at[p], section_copy(index, p))
            go(in_box[PLANES] & full_at[PLANES], near_copy(index))

        def first_half(state, slot_h, slot_b):
            e, h, _, _ = state
            for p in (1, 2):
                oscillate(p, step, state)
            electric_whole(2, state)
            electric_whole(1, state)
            k_c = CO[3, 0]
            e[0, 0] = b_send[slot_b, 2]
            e[0, 1] = b_send[slot_b, 0] + k_c * h_recv[slot_h, 1]
            e[0, 2] = b_send[slot_b, 1] - k_c * h_recv[slot_h, 0]
            magnetic_whole(1, state)
            magnetic_whole(0, state)

        def second_half(state, slot_h, slot_b):
            heard(has_right, b_copy(slot_b))
            k_c = CR[3]
            ahead = (
                b_recv[slot_b, 0] + k_c * h_send[slot_h, 1],
                b_recv[slot_b, 1] - k_c * h_send[slot_h, 0],
            )
            put(state[1], (2,), magnetic(2, state, ahead))

        set_coefficients(step)
        wait_loads(*[(k, p) for k in range(4) for p in range(PLANES)])
        for p in range(PLANES):
            for c in range(3):
                table_send[p, c] = cut(E[p, c])
            table_send[p, 3] = cut(CO[3, p])
            table_send[p, 4] = 1.0 - cut(CO[4, p]) * cut(CO[2, p])
        h_send[0, 0], h_send[0, 1] = H[2, 1], H[2, 2]
        take_near(0, true)
        for p in range(PLANES):
            oscillate(p, step, true)
        start = electric(0, true)
        set_b(0, start)
        take(0, 0, start)
        electric_whole(2, true)
        electric_whole(1, true)
        for p in (1, 2):
            take(0, p, get(E, p))
        for p in range(PLANES):
            pack_send[0, p, 0] = pack(get_section(0, p))
            pack_send[0, p, 1] = pack([table_send[p, c] for c in range(3)])
        kp_send[...] = pack([jnp.zeros((box_y, box_z), jnp.float32)] + [table_send[0, 3]] * 2)
        take_rim(0)
        prepare()
        pl.semaphore_wait(barrier, count(has_left, has_right, *listens))
        for k in range(3):
            go(reaches(0, k), kp_copy(k))
        send(0)
        go(has_right, h_copy(0), m_to_right)
        go(has_left, b_copy(0), m_to_left)
        for p in range(PLANES):
            go(in_box[p], table_copy(p))

        magnetic_whole(1, true)
        learn_neighbours(step)
        heard(has_left, h_copy(0))
        k_c = CO[3, 0]
        E[0, 0] = start[0]
        E[0, 1] = b_send[0, 0] + k_c * h_recv[0, 1]
        E[0, 2] = b_send[0, 1] - k_c * h_recv[0, 0]
        magnetic_whole(0, true)
        second_half(true, 0, 0)
        tell_right(1, H[2, 1], H[2, 2])

        take_near(1, true)
        for p in range(PLANES):
            for c in range(3):
                value = E[p, c]
                TE[p, c] = value
                kept = value[:, depth - box_z : depth]
                TE[p, c, :, depth - box_z : depth] = jnp.where(inside(p) & in_box[p], 0.0, kept)
                TH[p, c] = H[p, c]
                TQ[p, c] = Q[p, c]
                TJ[p, c] = J[p, c]
        oscillate(0, step, guess)
        start = electric(0, guess)
        tell_left(1, start)
        take(1, 0, start)
        for p in (1, 2):
            oscillate(p, step, guess)
        electric_whole(2, guess)
        electric_whole(1, guess)
        for p in (1, 2):
            take(1, p, get(TE, p))
        take_rim(1)
        for p in range(PLANES):
            pack_send[1, p, 0] = pack(get_section(1, p))
            pack_send[1, p, 1] = jnp.zeros((8, box_z), jnp.float32)
        send(1)
        heard(has_left, h_copy(1))
        k_c = CO[3, 0]
        TE[0, 0] = b_send[1, 2]
        TE[0, 1] = b_send[1, 0] + k_c * h_recv[1, 1]
        TE[0, 2] = b_send[1, 1] - k_c * h_recv[1, 0]
        magnetic_whole(1, guess)
        magnetic_whole(0, guess)
        second_half(guess, 1, 1)
        take_near(2, guess)
        for p in range(PLANES):
            oscillate(p, step, guess)
            back = None if p == 0 else (TH[p - 1, 1], TH[p - 1, 2])
            take(2, p, electric(p, guess, back))
            pack_send[2, p, 0] = pack(get_section(2, p))
            pack_send[2, p, 1] = jnp.zeros((8, box_z), jnp.float32)
        take_rim(2)
        send(2)

        place(0)
        oscillate(0, step, true)
        tell_left(2, electric(0, true))
        first_half(true, 1, 2)
        second_half(true, 1, 2)
        tell_right(2, H[2, 1], H[2, 2])
        place(1)
        oscillate(0, step, true)
        tell_left(3, electric(0, true))
        heard(has_left, h_copy(2))
        first_half(true, 2, 3)
        write(2)
        write(3)
        write(0)
        second_half(true, 2, 3)
        write(1)
        for slot in range(3):
            sent(has_right, h_copy(slot))
        for slot in range(4):
            sent(has_left, b_copy(slot))
        for p in range(PLANES):
            sent(in_box[p], table_copy(p))
            sent(in_box[p] & full_at[p], *[section_copy(index, p) for index in range(STEPS)])
            for k in range(3):
                sent(reaches(p, k), *[pack_copy(index, p, k) for index in range(STEPS)])
        for k in range(3):
            sent(reaches(0, k), kp_copy(k))
            sent(reaches(PLANES, k), *[rim_copy(index, k) for index in range(STEPS)])
        sent(in_box[PLANES] & full_at[PLANES], *[near_copy(index) for index in range(STEPS)])
        written()
        for p in range(PLANES):
            heard(in_box[p], mean_arrival(STEPS - 1, p))


def hand_over(n_slab, width, depth, off_in, mean_in, *refs):
    sources, targets = refs[:4], refs[4:8]
    off_ref, mean, held, load_sem, out_sem = refs[8:]
    loads = [pltpu.make_async_copy(sources[k].at[0], held.at[k], load_sem.at[k]) for k in range(4)]
    stores = [pltpu.make_async_copy(held.at[k], targets[k].at[0], out_sem.at[k]) for k in range(4)]
    load_off = pltpu.make_async_copy(off_in, off_ref, load_sem.at[4])
    load_mean = pltpu.make_async_copy(mean_in, mean, load_sem.at[5])
    load_off.start()
    load_mean.start()
    for load in loads:
        load.start()
    slab = lax.axis_index("slab")
    is_coarse = lax.axis_index("grid") == 0
    box_y, box_z = width // 3, depth // 3
    load_off.wait()
    load_mean.wait()
    corner_y = off_ref[0]
    row, column = iota((width, box_z), 0), iota((width, box_z), 1)
    interior = (row >= corner_y + 1) & (row <= corner_y + box_y - 2) & (column >= 1) & (column <= box_z - 2)
    loads[0].wait()
    for p in range(PLANES):
        fine = 3 * (slab - n_slab // 8) + p

        @pl.when(is_coarse & (fine >= 1) & (fine <= n_slab - 2))
        def _(p=p):
            for c in range(3):
                tall = jnp.concatenate([mean[p, c]] * (width // box_y), axis=0)
                placed = pltpu.roll(tall, corner_y, 0)
                kept = held[0, c, p, :, depth - box_z : depth]
                held[0, c, p, :, depth - box_z : depth] = jnp.where(interior, placed, kept)

    stores[0].start()
    for k in (1, 2, 3):
        loads[k].wait()
        stores[k].start()
    for store in stores:
        store.wait()


def on_device(n_slab, efield, hfield, polar, current, material, box_offset):
    planes, width, depth = efield.shape[2:]
    box = (width // 3, depth // 3)
    plane = (width, depth)
    f32 = jnp.float32
    dma = pltpu.SemaphoreType.DMA
    slots = STEPS * SUBS

    def room(*shape, dtype=f32):
        return pltpu.VMEM(shape, dtype)

    state = room(planes, 3, *plane)
    triple = room(3, *plane)
    scratch = [pltpu.SMEM((2,), jnp.int32)] + [state] * 8 + [
        room(planes, *plane, dtype=jnp.int32),
        room(5, planes, *plane),
        room(*plane, dtype=jnp.int32),
        room(2, *plane, dtype=jnp.int32),
        room(*plane),
        room(6, *plane),
    ]
    scratch += [triple] * 8
    scratch += [room(slots, 2, *plane), room(slots, 2, *plane), room(slots, 3, *plane), room(slots, 2, *plane)]
    scratch += [
        room(STEPS, planes, 3, *box),
        room(STEPS, 3, *box),
        room(planes, 5, *box),
        room(5, *box),
        room(STEPS, 2, *box),
        room(STEPS, 2, *box),
        room(2, 3, 3, *plane),
        room(6, *plane),
        state,
        state,
        state,
        room(2, 3, *plane),
        room(STEPS, 3, *box),
        room(STEPS - 1, planes, 3, *box),
        room(3, *box),
        room(2, 3, *box),
        room(STEPS, planes, 2, 8, box[1]),
        room(STEPS, 3, 2, 8, box[1]),
        room(8, box[1]),
        room(8, box[1]),
        room(STEPS, 8, box[1]),
        room(STEPS, 8, box[1]),
        room(3, *box),
        room(8, box[1]),
        room(2, 8, box[1]),
    ]
    scratch += [dma, dma((5, planes)), dma((4, planes)), dma((4,))]
    scratch += [dma((slots,))] * 4
    scratch += [dma((STEPS, planes)), dma((STEPS,)), dma((planes,)), dma, dma((STEPS,)), dma((STEPS,))]
    scratch += [dma((STEPS,)), dma((STEPS, planes)), dma((2,)), dma((2,))]
    scratch += [dma((STEPS, planes, 3)), dma((STEPS, 3)), dma((3,)), dma, dma((STEPS, 3)), dma((STEPS,))]
    scratch += [dma((2,)), dma((2,))]
    whole = pl.BlockSpec(memory_space=pl.ANY)
    fields = [jax.ShapeDtypeStruct(efield.shape, f32)] * 4
    state = pl.pallas_call(
        functools.partial(kernel, n_slab, width, depth),
        out_shape=fields + [jax.ShapeDtypeStruct((planes, 3, *box), f32)],
        in_specs=[whole] * 6,
        out_specs=[whole] * 5,
        scratch_shapes=scratch,
        compiler_params=pltpu.CompilerParams(
            collective_id=1, has_side_effects=True, vmem_limit_bytes=60 * 1024 * 1024
        ),
    )(box_offset, efield, hfield, polar, current, material)
    *state, mean = state
    return pl.pallas_call(
        functools.partial(hand_over, n_slab, width, depth),
        out_shape=fields,
        in_specs=[whole] * 6,
        out_specs=[whole] * 4,
        scratch_shapes=[
            pltpu.SMEM((2,), jnp.int32),
            room(planes, 3, *box),
            room(4, 3, planes, *plane),
            dma((6,)),
            dma((4,)),
        ],
        compiler_params=pltpu.CompilerParams(vmem_limit_bytes=60 * 1024 * 1024),
    )(box_offset, mean, *state)


def solution(mesh):
    field = P("grid", "angle", "slab", None, None)
    return jax.shard_map(
        functools.partial(on_device, mesh.shape["slab"]),
        mesh=mesh,
        in_specs=(field, field, field, field, P("grid", "slab", None, None), P()),
        out_specs=(field, field, field, field),
        check_vma=False,
    )
```

```python
import functools

import jax
import jax.numpy as jnp
from jax import lax
from jax.experimental import pallas as pl
from jax.experimental.pallas import tpu as pltpu
from jax.sharding import PartitionSpec as P

STEPS = 3
SUBS = 3
PERMITTIVITY = (1.0, 1.5, 1.2, 2.0)
STRENGTH = (0.4, 0.9, 0.3, 1.1)
RESONANCE = (0.6, 0.5, 0.8, 0.3)
DAMPING_RATE = (0.3, 0.2, 0.05, 0.4)
COURANT = 0.5
STEP_COARSE = 0.5
STEP_FINE = STEP_COARSE / 3.0
PLANES = 3
MESH = pl.DeviceIdType.MESH
EXACT = lax.Precision.HIGHEST


def tables(step):
    rows = zip(PERMITTIVITY, STRENGTH, RESONANCE, DAMPING_RATE)
    return [
        (1.0 - step * d, -step * r, step * s * r, COURANT / e, step / e) for e, s, r, d in rows
    ]


def pick(material, values):
    out = jnp.full(material.shape, values[0], jnp.float32)
    for index in range(1, 4):
        out = jnp.where(material == index, jnp.float32(values[index]), out)
    return out


def iota(shape, dim):
    return lax.broadcasted_iota(jnp.int32, shape, dim)


def down_y(u):
    return jnp.where(iota(u.shape, 0) == 0, 0.0, pltpu.roll(u, 1, 0))


def up_y(u):
    last = u.shape[0] - 1
    return jnp.where(iota(u.shape, 0) == last, 0.0, pltpu.roll(u, last, 0))


def down_z(u):
    return jnp.where(iota(u.shape, 1) == 0, 0.0, pltpu.roll(u, 1, 1))


def up_z(u):
    last = u.shape[1] - 1
    return jnp.where(iota(u.shape, 1) == last, 0.0, pltpu.roll(u, last, 1))


def curl_h(h, back=None):
    x, y, z = h
    c_x = (z - down_y(z)) - (y - down_z(y))
    c_y, c_z = -z, y
    if x is not None:
        c_y, c_z = (x - down_z(x)) - z, y - (x - down_y(x))
    if back is not None:
        c_y, c_z = c_y + back[1], c_z - back[0]
    return c_x, c_y, c_z


def curl_e(e, ahead=None):
    x, y, z = e
    c_x = (up_y(z) - z) - (up_z(y) - y)
    c_y, c_z = z, -y
    if x is not None:
        c_y, c_z = (up_z(x) - x) + z, -y - (up_y(x) - x)
    if ahead is not None:
        c_y, c_z = c_y - ahead[1], c_z + ahead[0]
    return c_x, c_y, c_z


def groups(few, many, many_dim):
    shape = (few, many) if many_dim == 1 else (many, few)
    return ones_where(iota(shape, many_dim) // 3 == iota(shape, 1 - many_dim))


def ones_where(condition):
    return jnp.where(condition, 1.0, 0.0).astype(jnp.bfloat16)


def terms(value):
    out = []
    for _ in range(3):
        out.append(value.astype(jnp.bfloat16))
        value = value - out[-1].astype(jnp.float32)
    return out


def times(wide, matrix):
    rows = wide.shape[0]
    parts = jnp.dot(jnp.concatenate(terms(wide), axis=0), matrix, preferred_element_type=jnp.float32)
    return parts[:rows] + parts[rows : 2 * rows] + parts[2 * rows :]


def times_left(matrix, wide):
    tall = jnp.concatenate(terms(wide), axis=0)
    return jnp.dot(jnp.concatenate([matrix] * 3, axis=1), tall, preferred_element_type=jnp.float32)


def ends(values, first):
    shape = next(v for v in values if v is not None).shape
    row, lane = iota(shape, 0), iota(shape, 1)
    flat = (8, shape[1])
    flat_row = iota(flat, 0)
    rows, columns = jnp.zeros(flat, jnp.float32), jnp.zeros(shape, jnp.float32)
    for c, value in enumerate(values):
        if value is not None:
            for side, at, column in ((0, first, 0), (1, first + 7, shape[1] - 1)):
                if isinstance(first, int):
                    taken = value[at : at + 1]
                else:
                    taken = jnp.sum(jnp.where(row == at, value, 0.0), axis=0, keepdims=True)
                rows = jnp.where(flat_row == 2 * c + side, taken, rows)
                columns = jnp.where(lane == 2 * c + side, value[:, column : column + 1], columns)
    return rows, columns


def fold(rows, columns):
    columns = jnp.where(iota(columns.shape, 1) < 8, columns, 0.0)
    line = jnp.sum(pltpu.roll(columns, 0, 1, stride=8, stride_axis=0), axis=0, keepdims=True)
    return jnp.where(iota(rows.shape, 0) == 6, line, rows)


def unfold(packed):
    line = jnp.broadcast_to(packed[6:7], packed.shape)
    out, row = line, iota(packed.shape, 0)
    for y in range(1, 8):
        out = jnp.where(row == y, pltpu.roll(line, packed.shape[1] - 8 * y, 1), out)
    return out


def unpack(rows, columns, width, depth):
    box_y, box_z = width // 3, depth // 3
    wide = times(jnp.concatenate(rows, axis=0), groups(box_z, depth, 1))
    spread = times_left(groups(3 * box_y, 3 * width, 0), jnp.concatenate(columns, axis=0))
    row, column = iota((width, depth), 0), iota((width, depth), 1)
    planes = []
    for j in range(3):
        plane = []
        for c in range(3):
            at, k = 8 * j + 2 * c, 2 * c
            side = spread[j * width : (j + 1) * width]
            value = jnp.where(column == 0, side[:, k : k + 1], 0.0)
            value = jnp.where(column == depth - 1, side[:, k + 1 : k + 2], value)
            value = jnp.where(row == 0, wide[at : at + 1], value)
            plane.append(jnp.where(row == width - 1, wide[at + 1 : at + 2], value))
        planes.append(plane)
    return planes


def kernel(
    n_slab, width, depth,
    off_in, e_in, h_in, p_in, j_in, m_in,
    e_out, h_out, p_out, j_out, mean_out,
    off_ref, E, H, Q, J, TE, TH, TQ, TJ, M, CO, m_left, m_right, CL, CR,
    AE, AH, AQ, AJ, A1, BE, BH, partial,
    h_send, h_recv, b_send, b_recv,
    sec_send, sec_recv, table_send, table_recv, near_send, near_recv,
    U, GA, DH, DJ, DQ, DE, mean_send, mean_recv, f_send, f_recv,
    pack_send, pack_recv, rim_send, rim_recv, D, d_send, d_recv,
    off_sem, load_sem, out_sem, m_sem,
    hs_sem, hr_sem, bs_sem, br_sem, ss_sem, sr_sem, ts_sem, tr_sem, ns_sem, nr_sem,
    ms_sem, mr_sem, fs_sem, fr_sem,
    ps_sem, pr_sem, es_sem, er_sem, ds_sem, dr_sem,
):
    slab = lax.axis_index("slab")
    level = lax.axis_index("grid")
    box_y, box_z = width // 3, depth // 3
    first_slab = n_slab // 8
    is_fine = level == 1
    is_coarse = level == 0
    has_left = slab > 0
    has_right = slab < n_slab - 1
    partner_slab = first_slab + slab // 3
    partner_plane = slab % 3
    outer = (slab == 0) | (slab == n_slab - 1)
    borrows = outer & (partner_plane == 0)
    seam = jnp.where(partner_plane == 0, 1, jnp.where(partner_plane == 1, 0, 2))
    has_seam = slab + seam - 1 < n_slab
    near_fines = [3 * (slab - first_slab) + k for k in range(-1, PLANES + 2)]
    listens = [(f >= 0) & (f < n_slab) for f in near_fines]
    listens[0] = listens[0] & (near_fines[1] < n_slab)
    fine_at = [3 * (slab - first_slab) + p for p in range(PLANES + 1)]
    in_box = [(f >= 0) & (f < n_slab) for f in fine_at]
    full_at = [(f == 0) | (f == n_slab - 1) for f in fine_at]

    fields = ((e_in, E, e_out), (h_in, H, h_out), (p_in, Q, p_out), (j_in, J, j_out))
    loads = [
        [pltpu.make_async_copy(src.at[0, :, p], dst.at[p], load_sem.at[k, p]) for p in range(PLANES)]
        for k, (src, dst, _) in enumerate(fields)
    ]
    load_m = pltpu.make_async_copy(m_in.at[0], M, load_sem.at[4, 0])

    barrier = pltpu.get_barrier_semaphore()

    def greet(condition, target):
        @pl.when(condition)
        def _():
            pl.semaphore_signal(barrier, inc=1, device_id=target, device_id_type=MESH)

    def count(*conditions):
        return sum(c.astype(jnp.int32) for c in conditions)

    greet(is_fine, {"grid": 0, "slab": partner_slab})
    greet(is_fine & (partner_plane < 2), {"grid": 0, "slab": partner_slab - 1})
    greet(is_fine & (partner_plane == 2) & has_right, {"grid": 0, "slab": partner_slab + 1})
    greet(has_left, {"slab": slab - 1})
    greet(has_right, {"slab": slab + 1})

    load_off = pltpu.make_async_copy(off_in, off_ref, off_sem)
    pl.when(is_coarse)(load_off.start)
    load_m.start()
    for p in range(PLANES):
        for k in range(4):
            loads[k][p].start()

    def remote(src, dst, send, recv, target):
        return pltpu.make_async_remote_copy(
            src_ref=src, dst_ref=dst, send_sem=send, recv_sem=recv, device_id=target, device_id_type=MESH
        )

    left, right = {"slab": slab - 1}, {"slab": slab + 1}

    def h_copy(slot):
        return remote(h_send.at[slot], h_recv.at[slot], hs_sem.at[slot], hr_sem.at[slot], right)

    def b_copy(slot):
        return remote(b_send.at[slot, 0:2], b_recv.at[slot], bs_sem.at[slot], br_sem.at[slot], left)

    m_next = remote(m_in.at[0, 0:1], m_right.at[0:1], m_sem.at[0], m_sem.at[1], left)
    m_to_left = remote(m_in.at[0, 0:2], m_right, m_sem.at[0], m_sem.at[1], left)
    m_to_right = remote(m_in.at[0, 2], m_left, m_sem.at[2], m_sem.at[3], right)

    def section_copy(index, p):
        return remote(
            sec_send.at[index, p], sec_recv.at[index], ss_sem.at[index, p], sr_sem.at[index],
            {"grid": 1, "slab": fine_at[p]},
        )

    def table_copy(p):
        return remote(
            table_send.at[p], table_recv, ts_sem.at[p], tr_sem, {"grid": 1, "slab": fine_at[p]}
        )

    def gain_copy(p):
        return remote(
            table_send.at[p, 3:5], table_recv.at[3:5], ts_sem.at[p], tr_sem, {"grid": 1, "slab": fine_at[p]}
        )

    def near_copy(index):
        return remote(
            near_send.at[index], near_recv.at[index], ns_sem.at[index], nr_sem.at[index],
            {"grid": 1, "slab": fine_at[PLANES]},
        )

    def mean_copy(index):
        room = mean_out if index == STEPS - 1 else mean_recv.at[index]
        return remote(
            mean_send.at[index], room.at[partner_plane], ms_sem.at[index],
            mr_sem.at[index, partner_plane], {"grid": 0, "slab": partner_slab},
        )

    def mean_arrival(index, p):
        room = mean_out if index == STEPS - 1 else mean_recv.at[index]
        return remote(
            mean_send.at[index], room.at[p], ms_sem.at[index], mr_sem.at[index, p],
            {"grid": 1, "slab": fine_at[p]},
        )

    def f_copy(side):
        return remote(f_send, f_recv.at[side], fs_sem.at[side], fr_sem.at[side], right if side == 0 else left)

    def pack_copy(index, p, k):
        size = 2 if isinstance(index, int) and index == 0 else 1
        return remote(
            pack_send.at[index, p, 0:size], pack_recv.at[index, 2 - k, 0:size],
            ps_sem.at[index, p, k], pr_sem.at[index, 2 - k],
            {"grid": 1, "slab": fine_at[p] + k - 1},
        )

    def rim_copy(index, k):
        return remote(
            rim_send.at[index], rim_recv.at[index], es_sem.at[index, k], er_sem.at[index],
            {"grid": 1, "slab": fine_at[PLANES] + k - 1},
        )

    def d_copy(side):
        return remote(d_send, d_recv.at[side], ds_sem.at[side], dr_sem.at[side], right if side == 0 else left)

    def reaches(p, k):
        target = fine_at[p] + k - 1
        return in_box[p] & (target >= 0) & (target < n_slab)

    def go(condition, *copies):
        @pl.when(condition)
        def _():
            for copy in copies:
                copy.start()

    def heard(condition, *copies):
        @pl.when(condition)
        def _():
            for copy in copies:
                copy.wait_recv()

    def sent(condition, *copies):
        @pl.when(condition)
        def _():
            for copy in copies:
                copy.wait_send()

    def get(ref, *index):
        return tuple(ref[(*index, c)] for c in range(3))

    def put(ref, index, values):
        for c, value in enumerate(values):
            if value is not None:
                ref[(*index, c)] = value

    def oscillate(p, step, state):
        e, _, q, j = state
        a_j, a_p, a_e = CO[0, p], CO[1, p], CO[2, p]
        for c in range(3):
            current = a_j * j[p, c] + a_p * q[p, c] + a_e * e[p, c]
            j[p, c] = current
            q[p, c] = q[p, c] + step * current

    def electric(p, state, back=None):
        e, h, _, j = state
        k_c, k_j = CO[3, p], CO[4, p]
        curl = curl_h(get(h, p), back)
        return tuple(e[p, c] - k_j * j[p, c] + k_c * curl[c] for c in range(3))

    def electric_whole(p, state):
        put(state[0], (p,), electric(p, state, (state[1][p - 1, 1], state[1][p - 1, 2])))

    def magnetic(p, state, ahead=None):
        e, h, _, _ = state
        curl = curl_e(get(e, p), ahead)
        return tuple(h[p, c] - COURANT * curl[c] for c in range(3))

    def magnetic_whole(p, state):
        put(state[1], (p,), magnetic(p, state, (state[0][p + 1, 1], state[0][p + 1, 2])))

    def set_coefficients(step):
        load_m.wait()
        values = tables(step)
        for p in range(PLANES):
            material = M[p]
            for k in range(5):
                CO[k, p] = pick(material, [row[k] for row in values])

    def learn_neighbours(step):
        heard(has_right, m_to_left)
        heard(has_left, m_to_right)
        sent(has_left, m_to_left)
        sent(has_right, m_to_right)
        values = tables(step)
        near, far = m_right[0], m_right[1]
        is_there = has_right.astype(jnp.float32)
        for k in range(5):
            scale = is_there if k == 3 else 1.0
            CR[k] = pick(near, [row[k] for row in values]) * scale
        CR[5] = pick(far, [row[3] for row in values]) * is_there
        before = m_left[...]
        CL[...] = pick(before, [row[3] for row in values]) * has_left.astype(jnp.float32)
        gains = [1.0 - row[4] * row[2] for row in values]
        for q, material in enumerate((before, M[0], M[1], M[2], near, far)):
            GA[q] = pick(material, gains)

    def prepare():
        @pl.when(jnp.logical_not(has_left))
        def _():
            h_recv[...] = jnp.zeros_like(h_recv)
            m_left[...] = jnp.zeros_like(m_left)

        @pl.when(jnp.logical_not(has_right))
        def _():
            b_recv[...] = jnp.zeros_like(b_recv)
            m_right[...] = jnp.zeros_like(m_right)

    def tell_right(slot, y, z):
        h_send[slot, 0], h_send[slot, 1] = y, z
        go(has_right, h_copy(slot))

    def set_b(slot, b):
        b_send[slot, 0], b_send[slot, 1], b_send[slot, 2] = b[1], b[2], b[0]

    def tell_left(slot, b):
        set_b(slot, b)
        go(has_left, b_copy(slot))

    def wait_loads(*which):
        for k, p in which:
            loads[k][p].wait()

    def write(k):
        for p in range(PLANES):
            pltpu.make_async_copy(fields[k][1].at[p], fields[k][2].at[0, :, p], out_sem.at[k, p]).start()

    def written():
        for k in range(4):
            for p in range(PLANES):
                pltpu.make_async_copy(fields[k][1].at[p], fields[k][2].at[0, :, p], out_sem.at[k, p]).wait()

    true = (E, H, Q, J)

    @pl.when(is_fine)
    def _():
        step = STEP_FINE
        row, column = iota((width, depth), 0), iota((width, depth), 1)
        edge = (row == 0) | (row == width - 1) | (column == 0) | (column == depth - 1)
        rims = [edge | (slab == 0), edge, edge | (slab == n_slab - 1)]
        small_row, small_column = iota((box_y, box_z), 0), iota((box_y, box_z), 1)
        f_cells = (
            (small_row >= 1) & (small_row <= box_y - 2) & (small_column >= 1) & (small_column <= box_z - 2)
            & (slab >= 1) & (slab <= n_slab - 2)
        )

        def upsampled(section):
            section = section.reshape(3 * box_y, box_z)
            wide = times(section, groups(box_z, depth, 1))
            return times_left(groups(3 * box_y, 3 * width, 0), wide).reshape(3, width, depth)

        def average():
            total = jnp.concatenate([E[0, c] + partial[c] for c in range(3)], axis=0)
            rows = times_left(groups(3 * box_y, 3 * width, 1), total)
            both = times(rows, groups(box_z, depth, 0))
            return (both * jnp.float32(1.0 / 27.0)).reshape(3, box_y, box_z)

        def boundary(b, sub, j=1):
            weight = jnp.float32((sub + 1) / 3.0)
            before, after = U.at[b % 2, j], U.at[(b + 1) % 2, j]
            return [before[c] + weight * (after[c] - before[c]) for c in range(3)]

        def inject(ref, index, p, values):
            for c in range(3):
                ref[(*index, c)] = jnp.where(rims[p], values[c], ref[(*index, c)])

        def open_block(first_slot):
            oscillate(0, step, true)
            e = electric(0, true)
            put(AE, (), e)
            tell_left(first_slot, e)

        set_coefficients(step)
        wait_loads((0, 0), (1, 0), (2, 0), (3, 0), (1, 2))
        prepare()

        @pl.when(outer & jnp.logical_not(borrows))
        def _():
            near_recv[...] = jnp.zeros_like(near_recv)

        @pl.when(jnp.logical_not(has_seam))
        def _():
            rim_recv[...] = jnp.zeros_like(rim_recv)

        @pl.when(jnp.logical_not(has_left))
        def _():
            f_recv[0] = jnp.zeros_like(f_recv[0])
            d_recv[0] = jnp.zeros_like(d_recv[0])
            for index in range(STEPS):
                pack_recv[index, 0] = jnp.zeros_like(pack_recv[index, 0])

        @pl.when(jnp.logical_not(has_right))
        def _():
            f_recv[1] = jnp.zeros_like(f_recv[1])
            d_recv[1] = jnp.zeros_like(d_recv[1])
            for index in range(STEPS):
                pack_recv[index, 2] = jnp.zeros_like(pack_recv[index, 2])

        pl.semaphore_wait(barrier, count(has_left, has_right))
        tell_right(0, H[2, 1], H[2, 2])
        open_block(0)
        go(has_left, m_to_left)
        go(has_right, m_to_right)
        wait_loads(*[(k, p) for k in range(4) for p in (1, 2) if (k, p) != (1, 2)])

        def fill(slot, rows, columns, section):
            for j, plane in enumerate(unpack(rows, columns, width, depth)):
                for c in range(3):
                    U[slot, j, c] = plane[c]

            @pl.when(outer)
            def _():
                whole = upsampled(section())
                for c in range(3):
                    U[slot, 1, c] = whole[c]

        def rim_values(b):
            for index, now in ((0, b == 0), (b, b > 0)):
                heard(now, pack_copy(index, 0, 1))
                heard(now & has_left, pack_copy(index, 0, 2))
                heard(now & has_right, pack_copy(index, 0, 0))

            heard(has_seam, rim_copy(b, 0))
            heard(outer, section_copy(b, 0))
            heard(borrows, near_copy(b))

            @pl.when(b == 0)
            def _():
                heard(outer, table_copy(0))
                before = [pack_recv[0, j, 1] for j in range(3)]
                fill(0, before, [unfold(v) for v in before], lambda: table_recv[0:3])

            near = rim_recv[b]
            near_columns = unfold(near)
            flat_row, lane = iota(near.shape, 0), iota(near.shape, 1)
            rows, columns = [], []
            for j in range(3):
                here, origin = pack_recv[b, j, 0], pack_recv[0, j, 0]
                sides = unfold(origin)
                k_rows = jnp.where((flat_row == 2) | (flat_row == 4), origin[7:8], pack_recv[0, j, 1][7:8])
                k_sides = jnp.where((lane == 2) | (lane == 4), sides[:, 6:7], sides[:, 7:8])
                rows.append(here + jnp.where((flat_row >= 2) & (flat_row <= 5), k_rows * near, 0.0))
                columns.append(unfold(here) + jnp.where((lane >= 2) & (lane <= 5), k_sides * near_columns, 0.0))

            def section(extra=None):
                k_c = table_recv[3]
                base = sec_recv[b]
                parts = [
                    base[0], base[1] + k_c * near_recv[b, 1], base[2] - k_c * near_recv[b, 0],
                ]
                if extra is not None:
                    parts = [part + extra[c] for c, part in enumerate(parts)]
                return jnp.stack(parts)

            @pl.when(b < STEPS - 1)
            def _():
                fill((b + 1) % 2, rows, columns, section)

            @pl.when(b == STEPS - 1)
            def _():
                heard(has_left, d_copy(0))
                heard(has_right, d_copy(1))
                extras = (d_recv[0], d_send[...], d_recv[1])
                fill(
                    (b + 1) % 2, [r + e for r, e in zip(rows, extras)],
                    [k + unfold(e) for k, e in zip(columns, extras)], lambda: section(D),
                )

            first = [boundary(b, 0, 0)]
            second = [None]
            for p in range(PLANES):
                first.append([jnp.where(rims[p], v, 0.0) for v in boundary(b, 0)])
                second.append([jnp.where(rims[p], v, 0.0) for v in boundary(b, 1)])
            first += [boundary(b, 0, 2)] * 2
            second.append(boundary(b, 1, 2))
            d_e = [[GA[q] * v for v in first[q]] for q in range(6)]
            d_h = []
            for q in range(5):
                curl = curl_e(d_e[q], (d_e[q + 1][1], d_e[q + 1][2]))
                d_h.append([-COURANT * u for u in curl])
            there = has_left.astype(jnp.float32)
            d_h[0] = [there * u for u in d_h[0]]
            for p in range(PLANES):
                put(DH, (p,), d_h[p + 1])
            for p in (1, 2):
                d_j = [CO[2, p] * v for v in first[p + 1]]
                put(DJ, (p,), d_j)
                put(DQ, (p,), [step * v for v in d_j])
            for q, at in ((1, 0), (4, 1)):
                a_j, a_p, a_e, k_c, k_j = [CO[k, 0] for k in range(5)] if at == 0 else [CR[k] for k in range(5)]
                curl = curl_h(d_h[q], (d_h[q - 1][1], d_h[q - 1][2]))
                for c in range(3):
                    early = a_e * first[q][c]
                    late = (a_j + step * a_p) * early + a_e * second[q][c]
                    DE[at, c] = second[q][c] - k_j * late + k_c * curl[c]
                    if at == 0:
                        DJ[0, c] = late
                        DQ[0, c] = step * (early + late)

        def feedback_response():
            heard(has_left, f_copy(0))
            heard(has_right, f_copy(1))
            here, before, after = f_send, f_recv.at[0], f_recv.at[1]
            curl = curl_e((here[0], here[1], here[2]), (after[1], after[2]))
            back_x = (up_z(before[0]) - before[0], up_y(before[0]) - before[0])
            back_y = back_x[0] - (here[2] - before[2])
            back_z = (here[1] - before[1]) - back_x[1]
            twice = curl_h(curl, (back_y, back_z))
            return [-COURANT * table_recv[3] * t for t in twice]

        def block(b, carry):
            s0 = 3 * b
            for p in (1, 2):
                oscillate(p, step, true)
            electric_whole(2, true)
            electric_whole(1, true)
            h = magnetic(2, true)
            put(BH, (), h)
            tell_right(s0 + 1, h[1], h[2])
            magnetic_whole(1, true)
            curl = curl_e(get(AE), (E[1, 1], E[1, 2]))
            put(AH, (), [H[0, c] - COURANT * curl[c] for c in range(3)])

            nothing = [jnp.zeros((width, depth), jnp.float32)] * 3
            inject(AE, (), 0, nothing)
            inject(E, (1,), 1, nothing)
            inject(E, (2,), 2, nothing)
            a_j, a_p, a_e, k_c, k_j = (CO[k, 0] for k in range(5))
            for c in range(3):
                current = a_j * J[0, c] + a_p * Q[0, c] + a_e * AE[c]
                AJ[c] = current
                AQ[c] = Q[0, c] + step * current
            curl = curl_h(get(AH))
            e_0 = tuple(AE[c] - k_j * AJ[c] + k_c * curl[c] for c in range(3))
            put(AE, (), e_0)
            tell_left(s0 + 1, e_0)
            for p in (1, 2):
                oscillate(p, step, true)
            curl = curl_h(get(BH), (H[1, 1], H[1, 2]))
            e_2 = tuple(E[2, c] - CO[4, 2] * J[2, c] + CO[3, 2] * curl[c] for c in range(3))
            put(BE, (), e_2)
            curl = curl_e(e_2)
            h = tuple(BH[c] - COURANT * curl[c] for c in range(3))
            put(BH, (), h)
            tell_right(s0 + 2, h[1], h[2])
            curl = curl_h(get(H, 1), (AH[1], AH[2]))
            e_1 = tuple(E[1, c] - CO[4, 1] * J[1, c] + CO[3, 1] * curl[c] for c in range(3))
            put(A1, (), e_1)
            curl = curl_e(get(AE), (A1[1], A1[2]))
            put(AH, (), [AH[c] - COURANT * curl[c] for c in range(3)])
            inject(AE, (), 0, nothing)
            for c in range(3):
                current = a_j * AJ[c] + a_p * AQ[c] + a_e * AE[c]
                AJ[c] = current
                AQ[c] = AQ[c] + step * current
            curl = curl_h(get(AH))
            e_0 = tuple(AE[c] - k_j * AJ[c] + k_c * curl[c] for c in range(3))
            put(AE, (), e_0)
            tell_left(s0 + 2, e_0)

            @pl.when(b == 0)
            def _():
                learn_neighbours(step)

            @pl.when(b == 1)
            def _():
                extra = feedback_response()
                for c in range(3):
                    D[c] = extra[c]
                d_send[...] = fold(*ends(extra, 0))
                go(has_right, d_copy(0))
                go(has_left, d_copy(1))

            @pl.when(b > 0)
            def _():
                rim_values(b)

            def face(coefficients, k_near, k_back, there, h_own, e_own, hear):
                a_j, a_p, a_e, k_c, k_j = coefficients
                side = COURANT * there.astype(jnp.float32)

                def kept(u):
                    return jnp.where(edge, 0.0, u)

                hear(0)
                h_y, h_z = h_own(0)
                e_y, e_z = e_own(0)
                d_y, d_z = k_c * h_z, -k_c * h_y
                e_y, e_z = e_y + d_y, e_z + d_z
                l_y, l_z = side * e_z, -side * e_y
                d_h = tuple(-COURANT * u for u in curl_e((None, d_y, d_z)))
                d_y, d_z = kept(d_y), kept(d_z)
                j_y, j_z = a_e * d_y, a_e * d_z
                p_y, p_z = step * j_y, step * j_z
                hear(1)
                h_y, h_z = h_own(1)
                e_y, e_z = e_own(1)
                h_y, h_z = h_y + l_y, h_z + l_z
                curl = curl_h(d_h, (h_y, h_z))
                d_x = k_c * curl[0]
                d_y = d_y - k_j * j_y + k_c * curl[1]
                d_z = d_z - k_j * j_z + k_c * curl[2]
                e_y, e_z = e_y + d_y, e_z + d_z
                l_e = tuple(k_back * u for u in curl_h((None, l_y, l_z)))
                curl = curl_e(l_e)
                l_h = (
                    -COURANT * curl[0],
                    l_y - COURANT * curl[1] + side * e_z,
                    l_z - COURANT * curl[2] - side * e_y,
                )
                f_y, f_z = k_near * d_h[2], -k_near * d_h[1]
                curl = curl_e((d_x, d_y, d_z), (f_y, f_z))
                d_h = tuple(d_h[c] - COURANT * curl[c] for c in range(3))
                d_e = kept(d_x), kept(d_y), kept(d_z)
                d_j = (a_e * d_e[0], a_j * j_y + a_p * p_y + a_e * d_e[1], a_j * j_z + a_p * p_z + a_e * d_e[2])
                d_p = (step * d_j[0], p_y + step * d_j[1], p_z + step * d_j[2])
                curl = curl_h(d_h, (l_h[1], l_h[2]))
                d_e = tuple(d_e[c] - k_j * d_j[c] + k_c * curl[c] for c in range(3))
                return d_e, d_j, d_p, d_h, (f_y, f_z), l_e, l_h

            def hear_left(m):
                heard(has_left, h_copy(s0 + m))

            def hear_right(m):
                heard(has_right, b_copy(s0 + m))

            d_e, _, _, _, _, l_e, l_h = face(
                [CR[k] for k in range(5)], CR[5], CO[3, 2], has_right,
                lambda m: (h_send[s0 + m, 0], h_send[s0 + m, 1]),
                lambda m: (b_recv[s0 + m, 0], b_recv[s0 + m, 1]),
                hear_right,
            )
            k_c = CR[3]
            next_y = d_e[1] + k_c * h_send[s0 + 2, 1]
            next_z = d_e[2] - k_c * h_send[s0 + 2, 0]
            put(H, (2,), [BH[c] + l_h[c] for c in range(3)])
            put(E, (2,), [BE[c] + l_e[c] for c in range(3)])
            d_e, d_j, d_p, d_h, near, _, _ = face(
                [CO[k, 0] for k in range(5)], CO[3, 1], CL[...], has_left,
                lambda m: (h_recv[s0 + m, 0], h_recv[s0 + m, 1]),
                lambda m: (b_send[s0 + m, 0], b_send[s0 + m, 1]),
                hear_left,
            )
            put(H, (0,), [AH[c] + d_h[c] for c in range(3)])
            put(J, (0,), [AJ[c] + d_j[c] for c in range(3)])
            put(Q, (0,), [AQ[c] + d_p[c] for c in range(3)])
            put(AE, (), [AE[c] + d_e[c] for c in range(3)])
            put(E, (1,), [A1[0], A1[1] + near[0], A1[2] + near[1]])

            magnetic_whole(1, true)

            @pl.when(b == 0)
            def _():
                rim_values(b)

            next_y = next_y + DE[1, 1]
            next_z = next_z + DE[1, 2]
            values = boundary(b, 1)
            for c in range(3):
                for p in range(PLANES):
                    H[p, c] = H[p, c] + DH[p, c]
                    J[p, c] = J[p, c] + DJ[p, c]
                    Q[p, c] = Q[p, c] + DQ[p, c]
                AE[c] = AE[c] + DE[0, c]
            for p in (1, 2):
                inject(E, (p,), p, values)
                oscillate(p, step, true)
            electric_whole(2, true)
            electric_whole(1, true)
            magnetic_whole(1, true)
            values = boundary(b, 2)
            put(H, (2,), magnetic(2, true))
            near_y, near_z = E[1, 1], E[1, 2]
            for p in (1, 2):
                inject(E, (p,), p, values)
            for c in range(3):
                partial[c] = E[1, c] + E[2, c]

            def close_right():
                hear_right(2)
                H[2, 1] = H[2, 1] + COURANT * (next_z + b_recv[s0 + 2, 1])
                H[2, 2] = H[2, 2] - COURANT * (next_y + b_recv[s0 + 2, 0])

            @pl.when(b < STEPS - 1)
            def _():
                close_right()
                tell_right(s0 + 3, H[2, 1], H[2, 2])

            hear_left(2)
            k_c = CO[3, 0]
            E[0, 0] = AE[0]
            E[0, 1] = AE[1] + k_c * h_recv[s0 + 2, 1]
            E[0, 2] = AE[2] - k_c * h_recv[s0 + 2, 0]
            put(H, (0,), magnetic(0, true, (near_y, near_z)))
            inject(E, (0,), 0, values)

            @pl.when(b < STEPS - 1)
            def _():
                open_block(s0 + 3)

            mean = average()
            mean_send[b] = mean
            for index in range(STEPS):

                @pl.when(b == index)
                def _(index=index):
                    mean_copy(index).start()

            pl.when(b == STEPS - 1)(close_right)

            @pl.when(b == 0)
            def _():
                heard(jnp.logical_not(outer), gain_copy(0))
                g = table_recv[4]
                for c in range(3):
                    f_send[c] = jnp.where(f_cells, g * mean[c], 0.0)
                go(has_right, f_copy(0))
                go(has_left, f_copy(1))

            return carry

        lax.fori_loop(0, STEPS, block, 0)
        for k in range(4):
            write(k)
        for slot in range(STEPS * SUBS):
            sent(has_right, h_copy(slot))
            sent(has_left, b_copy(slot))
        sent(has_right, f_copy(0), d_copy(0))
        sent(has_left, f_copy(1), d_copy(1))
        for index in range(STEPS):
            mean_copy(index).wait_send()
        written()

    @pl.when(is_coarse)
    def _():
        step = STEP_COARSE
        load_off.wait()
        corner_y = off_ref[0]
        guess = (TE, TH, TQ, TJ)

        def cut(value):
            return pltpu.roll(value[:, depth - box_z : depth], width - corner_y, 0)[:box_y]

        row, column = iota((width, box_z), 0), iota((width, box_z), 1)
        interior = (row >= corner_y + 1) & (row <= corner_y + box_y - 2) & (column >= 1) & (column <= box_z - 2)

        def inside(p):
            return interior & (fine_at[p] >= 1) & (fine_at[p] <= n_slab - 2)

        def place(index):
            for p in range(PLANES):

                @pl.when(in_box[p])
                def _(p=p):
                    mean_arrival(index, p).wait_recv()
                    for c in range(3):
                        tall = jnp.concatenate([mean_recv[index, p, c]] * (width // box_y), axis=0)
                        placed = pltpu.roll(tall, corner_y, 0)
                        kept = E[p, c, :, depth - box_z : depth]
                        E[p, c, :, depth - box_z : depth] = jnp.where(inside(p), placed, kept)

        def box_part(value):
            return value[:, depth - box_z : depth]

        def with_row(rows, value, at):
            taken = jnp.sum(jnp.where(iota(value.shape, 0) == at, value, 0.0), axis=0, keepdims=True)
            return jnp.where(iota(rows.shape, 0) == 7, taken, rows)

        def packed(rows, columns):
            return fold(rows, pltpu.roll(columns, width - corner_y, 0)[:box_y])

        def emit(index, p, values, scale=None):
            rows, columns = ends([box_part(v) for v in values], corner_y)
            if scale is not None:
                lane = iota(columns.shape, 1)
                columns = jnp.where(lane == 6, scale[:, 0:1], columns)
                columns = jnp.where(lane == 7, scale[:, box_z - 1 : box_z], columns)
                rows = with_row(rows, scale, corner_y)
            pack_send[index, p, 0] = packed(rows, columns)

            @pl.when(in_box[p] & full_at[p])
            def _():
                for c in range(3):
                    sec_send[index, p, c] = cut(values[c])

        def emit_near(index, y, z):
            rim_send[index] = packed(*ends([None, box_part(z), -box_part(y)], corner_y))

            @pl.when(in_box[PLANES] & full_at[PLANES])
            def _():
                near_send[index, 0], near_send[index, 1] = cut(y), cut(z)

        def send(index):
            for p in range(PLANES):
                for k in (1, 0, 2):
                    go(reaches(p, k), pack_copy(index, p, k))
                if p == 0:
                    for k in range(3):
                        go(reaches(PLANES, k), rim_copy(index, k))
            for p in range(PLANES):
                go(in_box[p] & full_at[p], section_copy(index, p))
            go(in_box[PLANES] & full_at[PLANES], near_copy(index))

        def first_half(state, slot_h, slot_b):
            e, h, _, _ = state
            for p in (1, 2):
                oscillate(p, step, state)
            electric_whole(2, state)
            electric_whole(1, state)
            k_c = CO[3, 0]
            e[0, 0] = b_send[slot_b, 2]
            e[0, 1] = b_send[slot_b, 0] + k_c * h_recv[slot_h, 1]
            e[0, 2] = b_send[slot_b, 1] - k_c * h_recv[slot_h, 0]
            magnetic_whole(1, state)
            magnetic_whole(0, state)

        def second_half(state, slot_h, slot_b):
            heard(has_right, b_copy(slot_b))
            k_c = CR[3]
            ahead = (
                b_recv[slot_b, 0] + k_c * h_send[slot_h, 1],
                b_recv[slot_b, 1] - k_c * h_send[slot_h, 0],
            )
            put(state[1], (2,), magnetic(2, state, ahead))

        def guess_from(p):
            for c in range(3):
                value = E[p, c]
                TE[p, c] = value
                TE[p, c, :, depth - box_z : depth] = jnp.where(inside(p) & in_box[p], 0.0, box_part(value))
                TQ[p, c] = Q[p, c]
                TJ[p, c] = J[p, c]

        set_coefficients(step)
        wait_loads(*[(k, p) for k in range(4) for p in range(PLANES)])
        h_send[0, 0], h_send[0, 1] = H[2, 1], H[2, 2]
        oscillate(0, step, true)
        start = electric(0, true)
        set_b(0, start)
        emit_near(0, H[2, 1], H[2, 2])
        scale = box_part(CO[3, 0])
        for p in range(PLANES):
            rows, columns = ends([box_part(E[p, c]) for c in range(3)], corner_y)
            if p == 0:
                rows = with_row(rows, scale, corner_y + box_y - 1)
            pack_send[0, p, 1] = packed(rows, columns)

            @pl.when(in_box[p] & full_at[p])
            def _(p=p):
                for c in range(3):
                    table_send[p, c] = cut(E[p, c])

        emit(0, 0, start, scale)
        for p in (2, 1):
            oscillate(p, step, true)
            electric_whole(p, true)
            emit(0, p, get(E, p))
        prepare()
        pl.semaphore_wait(barrier, count(has_left, has_right, *listens))
        send(0)
        go(has_right, h_copy(0))
        go(has_left, b_copy(0), m_next)
        for p in range(PLANES):

            @pl.when(in_box[p])
            def _(p=p):
                table_send[p, 3] = cut(CO[3, p])
                table_send[p, 4] = 1.0 - cut(CO[4, p]) * cut(CO[2, p])
                go(full_at[p], table_copy(p))
                go(jnp.logical_not(full_at[p]), gain_copy(p))

        magnetic_whole(1, true)
        for p in (1, 2):
            guess_from(p)
            oscillate(p, step, guess)
        for c in range(3):
            TH[1, c] = H[1, c]
        heard(has_left, h_copy(0))
        k_c = CO[3, 0]
        E[0, 0] = start[0]
        E[0, 1] = b_send[0, 0] + k_c * h_recv[0, 1]
        E[0, 2] = b_send[0, 1] - k_c * h_recv[0, 0]
        magnetic_whole(0, true)
        guess_from(0)
        for c in range(3):
            TH[0, c] = H[0, c]
        oscillate(0, step, guess)
        start = electric(0, guess)
        tell_left(1, start)
        emit(1, 0, start)
        electric_whole(1, guess)
        emit(1, 1, get(TE, 1))
        heard(has_right, m_next)
        sent(has_left, m_next)
        CR[3] = pick(m_right[0], [row[3] for row in tables(step)]) * has_right.astype(jnp.float32)
        second_half(true, 0, 0)
        tell_right(1, H[2, 1], H[2, 2])
        emit_near(1, H[2, 1], H[2, 2])
        for c in range(3):
            TH[2, c] = H[2, c]
        electric_whole(2, guess)
        emit(1, 2, get(TE, 2))
        send(1)
        magnetic_whole(1, guess)
        for p in (1, 2):
            oscillate(p, step, guess)
        heard(has_left, h_copy(1))
        TE[0, 0] = b_send[1, 2]
        TE[0, 1] = b_send[1, 0] + k_c * h_recv[1, 1]
        TE[0, 2] = b_send[1, 1] - k_c * h_recv[1, 0]
        magnetic_whole(0, guess)
        oscillate(0, step, guess)
        emit(2, 0, electric(0, guess))
        emit(2, 1, electric(1, guess, (TH[0, 1], TH[0, 2])))
        second_half(guess, 1, 1)
        emit_near(2, TH[2, 1], TH[2, 2])
        emit(2, 2, electric(2, guess, (TH[1, 1], TH[1, 2])))
        send(2)

        place(0)
        oscillate(0, step, true)
        tell_left(2, electric(0, true))
        first_half(true, 1, 2)
        second_half(true, 1, 2)
        tell_right(2, H[2, 1], H[2, 2])
        place(1)
        oscillate(0, step, true)
        tell_left(3, electric(0, true))
        heard(has_left, h_copy(2))
        first_half(true, 2, 3)
        write(2)
        write(3)
        write(0)
        second_half(true, 2, 3)
        write(1)
        for slot in range(3):
            sent(has_right, h_copy(slot))
        for slot in range(4):
            sent(has_left, b_copy(slot))
        for p in range(PLANES):
            sent(in_box[p] & full_at[p], table_copy(p))
            sent(in_box[p] & jnp.logical_not(full_at[p]), gain_copy(p))
            sent(in_box[p] & full_at[p], *[section_copy(index, p) for index in range(STEPS)])
            for k in range(3):
                sent(reaches(p, k), *[pack_copy(index, p, k) for index in range(STEPS)])
        for k in range(3):
            sent(reaches(PLANES, k), *[rim_copy(index, k) for index in range(STEPS)])
        sent(in_box[PLANES] & full_at[PLANES], *[near_copy(index) for index in range(STEPS)])
        written()
        for p in range(PLANES):
            heard(in_box[p], mean_arrival(STEPS - 1, p))


def hand_over(n_slab, width, depth, off_in, mean_in, *refs):
    sources, targets = refs[:4], refs[4:8]
    off_ref, mean, held, load_sem, out_sem = refs[8:]
    loads = [pltpu.make_async_copy(sources[k].at[0], held.at[k], load_sem.at[k]) for k in range(4)]
    stores = [pltpu.make_async_copy(held.at[k], targets[k].at[0], out_sem.at[k]) for k in range(4)]
    load_off = pltpu.make_async_copy(off_in, off_ref, load_sem.at[4])
    load_mean = pltpu.make_async_copy(mean_in, mean, load_sem.at[5])
    load_off.start()
    load_mean.start()
    for load in loads:
        load.start()
    slab = lax.axis_index("slab")
    is_coarse = lax.axis_index("grid") == 0
    box_y, box_z = width // 3, depth // 3
    load_off.wait()
    load_mean.wait()
    corner_y = off_ref[0]
    row, column = iota((width, box_z), 0), iota((width, box_z), 1)
    interior = (row >= corner_y + 1) & (row <= corner_y + box_y - 2) & (column >= 1) & (column <= box_z - 2)
    loads[0].wait()
    for p in range(PLANES):
        fine = 3 * (slab - n_slab // 8) + p

        @pl.when(is_coarse & (fine >= 1) & (fine <= n_slab - 2))
        def _(p=p):
            for c in range(3):
                tall = jnp.concatenate([mean[p, c]] * (width // box_y), axis=0)
                placed = pltpu.roll(tall, corner_y, 0)
                kept = held[0, c, p, :, depth - box_z : depth]
                held[0, c, p, :, depth - box_z : depth] = jnp.where(interior, placed, kept)

    stores[0].start()
    for k in (1, 2, 3):
        loads[k].wait()
        stores[k].start()
    for store in stores:
        store.wait()


def on_device(n_slab, efield, hfield, polar, current, material, box_offset):
    planes, width, depth = efield.shape[2:]
    box = (width // 3, depth // 3)
    plane = (width, depth)
    f32 = jnp.float32
    dma = pltpu.SemaphoreType.DMA
    slots = STEPS * SUBS

    def room(*shape, dtype=f32):
        return pltpu.VMEM(shape, dtype)

    state = room(planes, 3, *plane)
    triple = room(3, *plane)
    scratch = [pltpu.SMEM((2,), jnp.int32)] + [state] * 8 + [
        room(planes, *plane, dtype=jnp.int32),
        room(5, planes, *plane),
        room(*plane, dtype=jnp.int32),
        room(2, *plane, dtype=jnp.int32),
        room(*plane),
        room(6, *plane),
    ]
    scratch += [triple] * 8
    scratch += [room(slots, 2, *plane), room(slots, 2, *plane), room(slots, 3, *plane), room(slots, 2, *plane)]
    scratch += [
        room(STEPS, planes, 3, *box),
        room(STEPS, 3, *box),
        room(planes, 5, *box),
        room(5, *box),
        room(STEPS, 2, *box),
        room(STEPS, 2, *box),
        room(2, 3, 3, *plane),
        room(6, *plane),
        state,
        state,
        state,
        room(2, 3, *plane),
        room(STEPS, 3, *box),
        room(STEPS - 1, planes, 3, *box),
        room(3, *box),
        room(2, 3, *box),
        room(STEPS, planes, 2, 8, box[1]),
        room(STEPS, 3, 2, 8, box[1]),
        room(STEPS, 8, box[1]),
        room(STEPS, 8, box[1]),
        room(3, *box),
        room(8, box[1]),
        room(2, 8, box[1]),
    ]
    scratch += [dma, dma((5, planes)), dma((4, planes)), dma((4,))]
    scratch += [dma((slots,))] * 4
    scratch += [dma((STEPS, planes)), dma((STEPS,)), dma((planes,)), dma, dma((STEPS,)), dma((STEPS,))]
    scratch += [dma((STEPS,)), dma((STEPS, planes)), dma((2,)), dma((2,))]
    scratch += [dma((STEPS, planes, 3)), dma((STEPS, 3)), dma((STEPS, 3)), dma((STEPS,))]
    scratch += [dma((2,)), dma((2,))]
    whole = pl.BlockSpec(memory_space=pl.ANY)
    fields = [jax.ShapeDtypeStruct(efield.shape, f32)] * 4
    state = pl.pallas_call(
        functools.partial(kernel, n_slab, width, depth),
        out_shape=fields + [jax.ShapeDtypeStruct((planes, 3, *box), f32)],
        in_specs=[whole] * 6,
        out_specs=[whole] * 5,
        scratch_shapes=scratch,
        compiler_params=pltpu.CompilerParams(
            collective_id=1, has_side_effects=True, vmem_limit_bytes=60 * 1024 * 1024
        ),
    )(box_offset, efield, hfield, polar, current, material)
    *state, mean = state
    return pl.pallas_call(
        functools.partial(hand_over, n_slab, width, depth),
        out_shape=fields,
        in_specs=[whole] * 6,
        out_specs=[whole] * 4,
        scratch_shapes=[
            pltpu.SMEM((2,), jnp.int32),
            room(planes, 3, *box),
            room(4, 3, planes, *plane),
            dma((6,)),
            dma((4,)),
        ],
        compiler_params=pltpu.CompilerParams(vmem_limit_bytes=60 * 1024 * 1024),
    )(box_offset, mean, *state)


def solution(mesh):
    field = P("grid", "angle", "slab", None, None)
    return jax.shard_map(
        functools.partial(on_device, mesh.shape["slab"]),
        mesh=mesh,
        in_specs=(field, field, field, field, P("grid", "slab", None, None), P()),
        out_specs=(field, field, field, field),
        check_vma=False,
    )
```

```python
import functools

import jax
import jax.numpy as jnp
from jax import lax
from jax.experimental import pallas as pl
from jax.experimental.pallas import tpu as pltpu
from jax.sharding import PartitionSpec as P

STEPS = 3
SUBS = 3
PERMITTIVITY = (1.0, 1.5, 1.2, 2.0)
STRENGTH = (0.4, 0.9, 0.3, 1.1)
RESONANCE = (0.6, 0.5, 0.8, 0.3)
DAMPING_RATE = (0.3, 0.2, 0.05, 0.4)
COURANT = 0.5
STEP_COARSE = 0.5
STEP_FINE = STEP_COARSE / 3.0
PLANES = 3
MESH = pl.DeviceIdType.MESH
EXACT = lax.Precision.HIGHEST


def tables(step):
    rows = zip(PERMITTIVITY, STRENGTH, RESONANCE, DAMPING_RATE)
    return [
        (1.0 - step * d, -step * r, step * s * r, COURANT / e, step / e) for e, s, r, d in rows
    ]


def pick(material, values):
    out = jnp.full(material.shape, values[0], jnp.float32)
    for index in range(1, 4):
        out = jnp.where(material == index, jnp.float32(values[index]), out)
    return out


def iota(shape, dim):
    return lax.broadcasted_iota(jnp.int32, shape, dim)


def down_y(u):
    return jnp.where(iota(u.shape, 0) == 0, 0.0, pltpu.roll(u, 1, 0))


def up_y(u):
    last = u.shape[0] - 1
    return jnp.where(iota(u.shape, 0) == last, 0.0, pltpu.roll(u, last, 0))


def down_z(u):
    return jnp.where(iota(u.shape, 1) == 0, 0.0, pltpu.roll(u, 1, 1))


def up_z(u):
    last = u.shape[1] - 1
    return jnp.where(iota(u.shape, 1) == last, 0.0, pltpu.roll(u, last, 1))


def curl_h(h, back=None):
    x, y, z = h
    c_x = (z - down_y(z)) - (y - down_z(y))
    c_y, c_z = -z, y
    if x is not None:
        c_y, c_z = (x - down_z(x)) - z, y - (x - down_y(x))
    if back is not None:
        c_y, c_z = c_y + back[1], c_z - back[0]
    return c_x, c_y, c_z


def curl_e(e, ahead=None):
    x, y, z = e
    c_x = (up_y(z) - z) - (up_z(y) - y)
    c_y, c_z = z, -y
    if x is not None:
        c_y, c_z = (up_z(x) - x) + z, -y - (up_y(x) - x)
    if ahead is not None:
        c_y, c_z = c_y - ahead[1], c_z + ahead[0]
    return c_x, c_y, c_z


def groups(few, many, many_dim):
    shape = (few, many) if many_dim == 1 else (many, few)
    return ones_where(iota(shape, many_dim) // 3 == iota(shape, 1 - many_dim))


def ones_where(condition):
    return jnp.where(condition, 1.0, 0.0).astype(jnp.bfloat16)


def terms(value):
    out = []
    for _ in range(3):
        out.append(value.astype(jnp.bfloat16))
        value = value - out[-1].astype(jnp.float32)
    return out


def times(wide, matrix):
    rows = wide.shape[0]
    parts = jnp.dot(jnp.concatenate(terms(wide), axis=0), matrix, preferred_element_type=jnp.float32)
    return parts[:rows] + parts[rows : 2 * rows] + parts[2 * rows :]


def times_left(matrix, wide):
    tall = jnp.concatenate(terms(wide), axis=0)
    return jnp.dot(jnp.concatenate([matrix] * 3, axis=1), tall, preferred_element_type=jnp.float32)


def ends(values, first):
    shape = next(v for v in values if v is not None).shape
    row, lane = iota(shape, 0), iota(shape, 1)
    flat = (8, shape[1])
    flat_row = iota(flat, 0)
    rows, columns = jnp.zeros(flat, jnp.float32), jnp.zeros(shape, jnp.float32)
    for c, value in enumerate(values):
        if value is not None:
            for side, at, column in ((0, first, 0), (1, first + 7, shape[1] - 1)):
                if isinstance(first, int):
                    taken = value[at : at + 1]
                else:
                    taken = jnp.sum(jnp.where(row == at, value, 0.0), axis=0, keepdims=True)
                rows = jnp.where(flat_row == 2 * c + side, taken, rows)
                columns = jnp.where(lane == 2 * c + side, value[:, column : column + 1], columns)
    return rows, columns


def fold(rows, columns):
    columns = jnp.where(iota(columns.shape, 1) < 8, columns, 0.0)
    line = jnp.sum(pltpu.roll(columns, 0, 1, stride=8, stride_axis=0), axis=0, keepdims=True)
    return jnp.where(iota(rows.shape, 0) == 6, line, rows)


def unfold(packed):
    line = jnp.broadcast_to(packed[6:7], packed.shape)
    out, row = line, iota(packed.shape, 0)
    for y in range(1, 8):
        out = jnp.where(row == y, pltpu.roll(line, packed.shape[1] - 8 * y, 1), out)
    return out


def unpack(rows, columns, width, depth):
    box_y, box_z = width // 3, depth // 3
    wide = times(jnp.concatenate(rows, axis=0), groups(box_z, depth, 1))
    spread = times_left(groups(3 * box_y, 3 * width, 0), jnp.concatenate(columns, axis=0))
    row, column = iota((width, depth), 0), iota((width, depth), 1)
    planes = []
    for j in range(3):
        plane = []
        for c in range(3):
            at, k = 8 * j + 2 * c, 2 * c
            side = spread[j * width : (j + 1) * width]
            value = jnp.where(column == 0, side[:, k : k + 1], 0.0)
            value = jnp.where(column == depth - 1, side[:, k + 1 : k + 2], value)
            value = jnp.where(row == 0, wide[at : at + 1], value)
            plane.append(jnp.where(row == width - 1, wide[at + 1 : at + 2], value))
        planes.append(plane)
    return planes


def kernel(
    n_slab, width, depth,
    off_in, e_in, h_in, p_in, j_in, m_in,
    e_out, h_out, p_out, j_out, mean_out,
    off_ref, E, H, Q, J, TE, TH, TQ, TJ, M, CO, m_left, m_right, CL, CR,
    AE, AH, AQ, AJ, A1, BE, BH, partial,
    h_send, h_recv, b_send, b_recv,
    sec_send, sec_recv, table_send, table_recv, near_send, near_recv,
    U, GA, DH, DJ, DQ, DE, mean_send, mean_recv, f_send, f_recv,
    pack_send, pack_recv, rim_send, rim_recv, D, d_send, d_recv,
    off_sem, load_sem, out_sem, m_sem,
    hs_sem, hr_sem, bs_sem, br_sem, ss_sem, sr_sem, ts_sem, tr_sem, ns_sem, nr_sem,
    ms_sem, mr_sem, fs_sem, fr_sem,
    ps_sem, pr_sem, es_sem, er_sem, ds_sem, dr_sem,
):
    slab = lax.axis_index("slab")
    level = lax.axis_index("grid")
    box_y, box_z = width // 3, depth // 3
    first_slab = n_slab // 8
    is_fine = level == 1
    is_coarse = level == 0
    has_left = slab > 0
    has_right = slab < n_slab - 1
    partner_slab = first_slab + slab // 3
    partner_plane = slab % 3
    outer = (slab == 0) | (slab == n_slab - 1)
    borrows = outer & (partner_plane == 0)
    seam = jnp.where(partner_plane == 0, 1, jnp.where(partner_plane == 1, 0, 2))
    has_seam = slab + seam - 1 < n_slab
    near_fines = [3 * (slab - first_slab) + k for k in range(-1, PLANES + 2)]
    listens = [(f >= 0) & (f < n_slab) for f in near_fines]
    listens[0] = listens[0] & (near_fines[1] < n_slab)
    fine_at = [3 * (slab - first_slab) + p for p in range(PLANES + 1)]
    in_box = [(f >= 0) & (f < n_slab) for f in fine_at]
    full_at = [(f == 0) | (f == n_slab - 1) for f in fine_at]

    fields = ((e_in, E, e_out), (h_in, H, h_out), (p_in, Q, p_out), (j_in, J, j_out))
    loads = [
        [pltpu.make_async_copy(src.at[0, :, p], dst.at[p], load_sem.at[k, p]) for p in range(PLANES)]
        for k, (src, dst, _) in enumerate(fields)
    ]
    load_m = pltpu.make_async_copy(m_in.at[0], M, load_sem.at[4, 0])

    barrier = pltpu.get_barrier_semaphore()

    def greet(condition, target):
        @pl.when(condition)
        def _():
            pl.semaphore_signal(barrier, inc=1, device_id=target, device_id_type=MESH)

    def count(*conditions):
        return sum(c.astype(jnp.int32) for c in conditions)

    greet(is_fine, {"grid": 0, "slab": partner_slab})
    greet(is_fine & (partner_plane < 2), {"grid": 0, "slab": partner_slab - 1})
    greet(is_fine & (partner_plane == 2) & has_right, {"grid": 0, "slab": partner_slab + 1})
    greet(has_left, {"slab": slab - 1})
    greet(has_right, {"slab": slab + 1})

    load_off = pltpu.make_async_copy(off_in, off_ref, off_sem)
    pl.when(is_coarse)(load_off.start)
    load_m.start()
    for p in range(PLANES):
        for k in range(4):
            loads[k][p].start()

    def remote(src, dst, send, recv, target):
        return pltpu.make_async_remote_copy(
            src_ref=src, dst_ref=dst, send_sem=send, recv_sem=recv, device_id=target, device_id_type=MESH
        )

    left, right = {"slab": slab - 1}, {"slab": slab + 1}

    def h_copy(slot):
        return remote(h_send.at[slot], h_recv.at[slot], hs_sem.at[slot], hr_sem.at[slot], right)

    def b_copy(slot):
        return remote(b_send.at[slot, 0:2], b_recv.at[slot], bs_sem.at[slot], br_sem.at[slot], left)

    m_next = remote(m_in.at[0, 0:1], m_right.at[0:1], m_sem.at[0], m_sem.at[1], left)
    m_to_left = remote(m_in.at[0, 0:2], m_right, m_sem.at[0], m_sem.at[1], left)
    m_to_right = remote(m_in.at[0, 2], m_left, m_sem.at[2], m_sem.at[3], right)

    def section_copy(index, p):
        return remote(
            sec_send.at[index, p], sec_recv.at[index], ss_sem.at[index, p], sr_sem.at[index],
            {"grid": 1, "slab": fine_at[p]},
        )

    def table_copy(p):
        return remote(
            table_send.at[p], table_recv, ts_sem.at[p], tr_sem, {"grid": 1, "slab": fine_at[p]}
        )

    def gain_copy(p):
        return remote(
            table_send.at[p, 3:5], table_recv.at[3:5], ts_sem.at[p], tr_sem, {"grid": 1, "slab": fine_at[p]}
        )

    def near_copy(index):
        return remote(
            near_send.at[index], near_recv.at[index], ns_sem.at[index], nr_sem.at[index],
            {"grid": 1, "slab": fine_at[PLANES]},
        )

    def mean_copy(index):
        room = mean_out if index == STEPS - 1 else mean_recv.at[index]
        return remote(
            mean_send.at[index], room.at[partner_plane], ms_sem.at[index],
            mr_sem.at[index, partner_plane], {"grid": 0, "slab": partner_slab},
        )

    def mean_arrival(index, p):
        room = mean_out if index == STEPS - 1 else mean_recv.at[index]
        return remote(
            mean_send.at[index], room.at[p], ms_sem.at[index], mr_sem.at[index, p],
            {"grid": 1, "slab": fine_at[p]},
        )

    def f_copy(side):
        return remote(f_send, f_recv.at[side], fs_sem.at[side], fr_sem.at[side], right if side == 0 else left)

    def pack_copy(index, p, k):
        size = 2 if isinstance(index, int) and index == 0 else 1
        return remote(
            pack_send.at[index, p, 0:size], pack_recv.at[index, 2 - k, 0:size],
            ps_sem.at[index, p, k], pr_sem.at[index, 2 - k],
            {"grid": 1, "slab": fine_at[p] + k - 1},
        )

    def rim_copy(index, k):
        return remote(
            rim_send.at[index], rim_recv.at[index], es_sem.at[index, k], er_sem.at[index],
            {"grid": 1, "slab": fine_at[PLANES] + k - 1},
        )

    def d_copy(side):
        return remote(d_send, d_recv.at[side], ds_sem.at[side], dr_sem.at[side], right if side == 0 else left)

    def reaches(p, k):
        target = fine_at[p] + k - 1
        return in_box[p] & (target >= 0) & (target < n_slab)

    def go(condition, *copies):
        @pl.when(condition)
        def _():
            for copy in copies:
                copy.start()

    def heard(condition, *copies):
        @pl.when(condition)
        def _():
            for copy in copies:
                copy.wait_recv()

    def sent(condition, *copies):
        @pl.when(condition)
        def _():
            for copy in copies:
                copy.wait_send()

    def get(ref, *index):
        return tuple(ref[(*index, c)] for c in range(3))

    def put(ref, index, values):
        for c, value in enumerate(values):
            if value is not None:
                ref[(*index, c)] = value

    def oscillate(p, step, state):
        e, _, q, j = state
        a_j, a_p, a_e = CO[0, p], CO[1, p], CO[2, p]
        for c in range(3):
            current = a_j * j[p, c] + a_p * q[p, c] + a_e * e[p, c]
            j[p, c] = current
            q[p, c] = q[p, c] + step * current

    def electric(p, state, back=None):
        e, h, _, j = state
        k_c, k_j = CO[3, p], CO[4, p]
        curl = curl_h(get(h, p), back)
        return tuple(e[p, c] - k_j * j[p, c] + k_c * curl[c] for c in range(3))

    def electric_whole(p, state):
        put(state[0], (p,), electric(p, state, (state[1][p - 1, 1], state[1][p - 1, 2])))

    def magnetic(p, state, ahead=None):
        e, h, _, _ = state
        curl = curl_e(get(e, p), ahead)
        return tuple(h[p, c] - COURANT * curl[c] for c in range(3))

    def magnetic_whole(p, state):
        put(state[1], (p,), magnetic(p, state, (state[0][p + 1, 1], state[0][p + 1, 2])))

    def set_coefficients(step):
        load_m.wait()
        values = tables(step)
        for p in range(PLANES):
            material = M[p]
            for k in range(5):
                CO[k, p] = pick(material, [row[k] for row in values])

    def learn_neighbours(step):
        heard(has_right, m_to_left)
        heard(has_left, m_to_right)
        sent(has_left, m_to_left)
        sent(has_right, m_to_right)
        values = tables(step)
        near, far = m_right[0], m_right[1]
        is_there = has_right.astype(jnp.float32)
        for k in range(5):
            scale = is_there if k == 3 else 1.0
            CR[k] = pick(near, [row[k] for row in values]) * scale
        CR[5] = pick(far, [row[3] for row in values]) * is_there
        before = m_left[...]
        CL[...] = pick(before, [row[3] for row in values]) * has_left.astype(jnp.float32)
        gains = [1.0 - row[4] * row[2] for row in values]
        for q, material in enumerate((before, M[0], M[1], M[2], near, far)):
            GA[q] = pick(material, gains)

    def prepare():
        @pl.when(jnp.logical_not(has_left))
        def _():
            h_recv[...] = jnp.zeros_like(h_recv)
            m_left[...] = jnp.zeros_like(m_left)

        @pl.when(jnp.logical_not(has_right))
        def _():
            b_recv[...] = jnp.zeros_like(b_recv)
            m_right[...] = jnp.zeros_like(m_right)

    def tell_right(slot, y, z):
        h_send[slot, 0], h_send[slot, 1] = y, z
        go(has_right, h_copy(slot))

    def set_b(slot, b):
        b_send[slot, 0], b_send[slot, 1], b_send[slot, 2] = b[1], b[2], b[0]

    def tell_left(slot, b):
        set_b(slot, b)
        go(has_left, b_copy(slot))

    def wait_loads(*which):
        for k, p in which:
            loads[k][p].wait()

    def write(k):
        for p in range(PLANES):
            pltpu.make_async_copy(fields[k][1].at[p], fields[k][2].at[0, :, p], out_sem.at[k, p]).start()

    def written():
        for k in range(4):
            for p in range(PLANES):
                pltpu.make_async_copy(fields[k][1].at[p], fields[k][2].at[0, :, p], out_sem.at[k, p]).wait()

    true = (E, H, Q, J)

    @pl.when(is_fine)
    def _():
        step = STEP_FINE
        row, column = iota((width, depth), 0), iota((width, depth), 1)
        edge = (row == 0) | (row == width - 1) | (column == 0) | (column == depth - 1)
        rims = [edge | (slab == 0), edge, edge | (slab == n_slab - 1)]
        small_row, small_column = iota((box_y, box_z), 0), iota((box_y, box_z), 1)
        f_cells = (
            (small_row >= 1) & (small_row <= box_y - 2) & (small_column >= 1) & (small_column <= box_z - 2)
            & (slab >= 1) & (slab <= n_slab - 2)
        )

        def upsampled(section):
            section = section.reshape(3 * box_y, box_z)
            wide = times(section, groups(box_z, depth, 1))
            return times_left(groups(3 * box_y, 3 * width, 0), wide).reshape(3, width, depth)

        def average():
            total = jnp.concatenate([E[0, c] + partial[c] for c in range(3)], axis=0)
            rows = times_left(groups(3 * box_y, 3 * width, 1), total)
            both = times(rows, groups(box_z, depth, 0))
            return (both * jnp.float32(1.0 / 27.0)).reshape(3, box_y, box_z)

        def boundary(b, sub, j=1):
            weight = jnp.float32((sub + 1) / 3.0)
            before, after = U.at[b % 2, j], U.at[(b + 1) % 2, j]
            return [before[c] + weight * (after[c] - before[c]) for c in range(3)]

        def inject(ref, index, p, values):
            for c in range(3):
                ref[(*index, c)] = jnp.where(rims[p], values[c], ref[(*index, c)])

        def open_block(first_slot):
            oscillate(0, step, true)
            e = electric(0, true)
            put(AE, (), e)
            tell_left(first_slot, e)

        set_coefficients(step)
        wait_loads((0, 0), (1, 0), (2, 0), (3, 0), (1, 2))
        prepare()

        @pl.when(outer & jnp.logical_not(borrows))
        def _():
            near_recv[...] = jnp.zeros_like(near_recv)

        @pl.when(jnp.logical_not(has_seam))
        def _():
            rim_recv[...] = jnp.zeros_like(rim_recv)

        @pl.when(jnp.logical_not(has_left))
        def _():
            f_recv[0] = jnp.zeros_like(f_recv[0])
            d_recv[0] = jnp.zeros_like(d_recv[0])
            for index in range(STEPS):
                pack_recv[index, 0] = jnp.zeros_like(pack_recv[index, 0])

        @pl.when(jnp.logical_not(has_right))
        def _():
            f_recv[1] = jnp.zeros_like(f_recv[1])
            d_recv[1] = jnp.zeros_like(d_recv[1])
            for index in range(STEPS):
                pack_recv[index, 2] = jnp.zeros_like(pack_recv[index, 2])

        pl.semaphore_wait(barrier, count(has_left, has_right))
        tell_right(0, H[2, 1], H[2, 2])
        open_block(0)
        go(has_left, m_to_left)
        go(has_right, m_to_right)
        wait_loads(*[(k, p) for k in range(4) for p in (1, 2) if (k, p) != (1, 2)])

        def fill(slot, rows, columns, section):
            for j, plane in enumerate(unpack(rows, columns, width, depth)):
                for c in range(3):
                    U[slot, j, c] = plane[c]

            @pl.when(outer)
            def _():
                whole = upsampled(section())
                for c in range(3):
                    U[slot, 1, c] = whole[c]

        def rim_values(b):
            for index, now in ((0, b == 0), (b, b > 0)):
                heard(now, pack_copy(index, 0, 1))
                heard(now & has_left, pack_copy(index, 0, 2))
                heard(now & has_right, pack_copy(index, 0, 0))

            heard(has_seam, rim_copy(b, 0))
            heard(outer, section_copy(b, 0))
            heard(borrows, near_copy(b))

            @pl.when(b == 0)
            def _():
                heard(outer, table_copy(0))
                before = [pack_recv[0, j, 1] for j in range(3)]
                fill(0, before, [unfold(v) for v in before], lambda: table_recv[0:3])

            near = rim_recv[b]
            near_columns = unfold(near)
            flat_row, lane = iota(near.shape, 0), iota(near.shape, 1)
            rows, columns = [], []
            for j in range(3):
                here, origin = pack_recv[b, j, 0], pack_recv[0, j, 0]
                sides = unfold(origin)
                k_rows = jnp.where((flat_row == 2) | (flat_row == 4), origin[7:8], pack_recv[0, j, 1][7:8])
                k_sides = jnp.where((lane == 2) | (lane == 4), sides[:, 6:7], sides[:, 7:8])
                rows.append(here + jnp.where((flat_row >= 2) & (flat_row <= 5), k_rows * near, 0.0))
                columns.append(unfold(here) + jnp.where((lane >= 2) & (lane <= 5), k_sides * near_columns, 0.0))

            def section(extra=None):
                k_c = table_recv[3]
                base = sec_recv[b]
                parts = [
                    base[0], base[1] + k_c * near_recv[b, 1], base[2] - k_c * near_recv[b, 0],
                ]
                if extra is not None:
                    parts = [part + extra[c] for c, part in enumerate(parts)]
                return jnp.stack(parts)

            @pl.when(b < STEPS - 1)
            def _():
                fill((b + 1) % 2, rows, columns, section)

            @pl.when(b == STEPS - 1)
            def _():
                heard(has_left, d_copy(0))
                heard(has_right, d_copy(1))
                extras = (d_recv[0], d_send[...], d_recv[1])
                fill(
                    (b + 1) % 2, [r + e for r, e in zip(rows, extras)],
                    [k + unfold(e) for k, e in zip(columns, extras)], lambda: section(D),
                )

            first = [boundary(b, 0, 0)]
            second = [None]
            for p in range(PLANES):
                first.append([jnp.where(rims[p], v, 0.0) for v in boundary(b, 0)])
                second.append([jnp.where(rims[p], v, 0.0) for v in boundary(b, 1)])
            first += [boundary(b, 0, 2)] * 2
            second.append(boundary(b, 1, 2))
            d_e = [[GA[q] * v for v in first[q]] for q in range(6)]
            d_h = []
            for q in range(5):
                curl = curl_e(d_e[q], (d_e[q + 1][1], d_e[q + 1][2]))
                d_h.append([-COURANT * u for u in curl])
            there = has_left.astype(jnp.float32)
            d_h[0] = [there * u for u in d_h[0]]
            for p in range(PLANES):
                put(DH, (p,), d_h[p + 1])
            for p in (1, 2):
                d_j = [CO[2, p] * v for v in first[p + 1]]
                put(DJ, (p,), d_j)
                put(DQ, (p,), [step * v for v in d_j])
            for q, at in ((1, 0), (4, 1)):
                a_j, a_p, a_e, k_c, k_j = [CO[k, 0] for k in range(5)] if at == 0 else [CR[k] for k in range(5)]
                curl = curl_h(d_h[q], (d_h[q - 1][1], d_h[q - 1][2]))
                for c in range(3):
                    early = a_e * first[q][c]
                    late = (a_j + step * a_p) * early + a_e * second[q][c]
                    DE[at, c] = second[q][c] - k_j * late + k_c * curl[c]
                    if at == 0:
                        DJ[0, c] = late
                        DQ[0, c] = step * (early + late)

        def feedback_response():
            heard(has_left, f_copy(0))
            heard(has_right, f_copy(1))
            here, before, after = f_send, f_recv.at[0], f_recv.at[1]
            curl = curl_e((here[0], here[1], here[2]), (after[1], after[2]))
            back_x = (up_z(before[0]) - before[0], up_y(before[0]) - before[0])
            back_y = back_x[0] - (here[2] - before[2])
            back_z = (here[1] - before[1]) - back_x[1]
            twice = curl_h(curl, (back_y, back_z))
            return [-COURANT * table_recv[3] * t for t in twice]

        def block(b, carry):
            s0 = 3 * b
            for p in (1, 2):
                oscillate(p, step, true)
            electric_whole(2, true)
            electric_whole(1, true)
            h = magnetic(2, true)
            put(BH, (), h)
            tell_right(s0 + 1, h[1], h[2])
            magnetic_whole(1, true)
            curl = curl_e(get(AE), (E[1, 1], E[1, 2]))
            put(AH, (), [H[0, c] - COURANT * curl[c] for c in range(3)])

            nothing = [jnp.zeros((width, depth), jnp.float32)] * 3
            inject(AE, (), 0, nothing)
            inject(E, (1,), 1, nothing)
            inject(E, (2,), 2, nothing)
            a_j, a_p, a_e, k_c, k_j = (CO[k, 0] for k in range(5))
            for c in range(3):
                current = a_j * J[0, c] + a_p * Q[0, c] + a_e * AE[c]
                AJ[c] = current
                AQ[c] = Q[0, c] + step * current
            curl = curl_h(get(AH))
            e_0 = tuple(AE[c] - k_j * AJ[c] + k_c * curl[c] for c in range(3))
            put(AE, (), e_0)
            tell_left(s0 + 1, e_0)
            for p in (1, 2):
                oscillate(p, step, true)
            curl = curl_h(get(BH), (H[1, 1], H[1, 2]))
            e_2 = tuple(E[2, c] - CO[4, 2] * J[2, c] + CO[3, 2] * curl[c] for c in range(3))
            put(BE, (), e_2)
            curl = curl_e(e_2)
            h = tuple(BH[c] - COURANT * curl[c] for c in range(3))
            put(BH, (), h)
            tell_right(s0 + 2, h[1], h[2])
            curl = curl_h(get(H, 1), (AH[1], AH[2]))
            e_1 = tuple(E[1, c] - CO[4, 1] * J[1, c] + CO[3, 1] * curl[c] for c in range(3))
            put(A1, (), e_1)
            curl = curl_e(get(AE), (A1[1], A1[2]))
            put(AH, (), [AH[c] - COURANT * curl[c] for c in range(3)])
            inject(AE, (), 0, nothing)
            for c in range(3):
                current = a_j * AJ[c] + a_p * AQ[c] + a_e * AE[c]
                AJ[c] = current
                AQ[c] = AQ[c] + step * current
            curl = curl_h(get(AH))
            e_0 = tuple(AE[c] - k_j * AJ[c] + k_c * curl[c] for c in range(3))
            put(AE, (), e_0)
            tell_left(s0 + 2, e_0)

            @pl.when(b == 0)
            def _():
                learn_neighbours(step)

            @pl.when(b == 1)
            def _():
                extra = feedback_response()
                for c in range(3):
                    D[c] = extra[c]
                d_send[...] = fold(*ends(extra, 0))
                go(has_right, d_copy(0))
                go(has_left, d_copy(1))

            @pl.when(b > 0)
            def _():
                rim_values(b)

            def face(coefficients, k_near, k_back, there, h_own, e_own, hear):
                a_j, a_p, a_e, k_c, k_j = coefficients
                side = COURANT * there.astype(jnp.float32)

                def kept(u):
                    return jnp.where(edge, 0.0, u)

                hear(0)
                h_y, h_z = h_own(0)
                e_y, e_z = e_own(0)
                d_y, d_z = k_c * h_z, -k_c * h_y
                e_y, e_z = e_y + d_y, e_z + d_z
                l_y, l_z = side * e_z, -side * e_y
                d_h = tuple(-COURANT * u for u in curl_e((None, d_y, d_z)))
                d_y, d_z = kept(d_y), kept(d_z)
                j_y, j_z = a_e * d_y, a_e * d_z
                p_y, p_z = step * j_y, step * j_z
                hear(1)
                h_y, h_z = h_own(1)
                e_y, e_z = e_own(1)
                h_y, h_z = h_y + l_y, h_z + l_z
                curl = curl_h(d_h, (h_y, h_z))
                d_x = k_c * curl[0]
                d_y = d_y - k_j * j_y + k_c * curl[1]
                d_z = d_z - k_j * j_z + k_c * curl[2]
                e_y, e_z = e_y + d_y, e_z + d_z
                l_e = tuple(k_back * u for u in curl_h((None, l_y, l_z)))
                curl = curl_e(l_e)
                l_h = (
                    -COURANT * curl[0],
                    l_y - COURANT * curl[1] + side * e_z,
                    l_z - COURANT * curl[2] - side * e_y,
                )
                f_y, f_z = k_near * d_h[2], -k_near * d_h[1]
                curl = curl_e((d_x, d_y, d_z), (f_y, f_z))
                d_h = tuple(d_h[c] - COURANT * curl[c] for c in range(3))
                d_e = kept(d_x), kept(d_y), kept(d_z)
                d_j = (a_e * d_e[0], a_j * j_y + a_p * p_y + a_e * d_e[1], a_j * j_z + a_p * p_z + a_e * d_e[2])
                d_p = (step * d_j[0], p_y + step * d_j[1], p_z + step * d_j[2])
                curl = curl_h(d_h, (l_h[1], l_h[2]))
                d_e = tuple(d_e[c] - k_j * d_j[c] + k_c * curl[c] for c in range(3))
                return d_e, d_j, d_p, d_h, (f_y, f_z), l_e, l_h

            def hear_left(m):
                heard(has_left, h_copy(s0 + m))

            def hear_right(m):
                heard(has_right, b_copy(s0 + m))

            d_e, _, _, _, _, l_e, l_h = face(
                [CR[k] for k in range(5)], CR[5], CO[3, 2], has_right,
                lambda m: (h_send[s0 + m, 0], h_send[s0 + m, 1]),
                lambda m: (b_recv[s0 + m, 0], b_recv[s0 + m, 1]),
                hear_right,
            )
            k_c = CR[3]
            next_y = d_e[1] + k_c * h_send[s0 + 2, 1]
            next_z = d_e[2] - k_c * h_send[s0 + 2, 0]
            put(H, (2,), [BH[c] + l_h[c] for c in range(3)])
            put(E, (2,), [BE[c] + l_e[c] for c in range(3)])
            d_e, d_j, d_p, d_h, near, _, _ = face(
                [CO[k, 0] for k in range(5)], CO[3, 1], CL[...], has_left,
                lambda m: (h_recv[s0 + m, 0], h_recv[s0 + m, 1]),
                lambda m: (b_send[s0 + m, 0], b_send[s0 + m, 1]),
                hear_left,
            )
            put(H, (0,), [AH[c] + d_h[c] for c in range(3)])
            put(J, (0,), [AJ[c] + d_j[c] for c in range(3)])
            put(Q, (0,), [AQ[c] + d_p[c] for c in range(3)])
            put(AE, (), [AE[c] + d_e[c] for c in range(3)])
            put(E, (1,), [A1[0], A1[1] + near[0], A1[2] + near[1]])

            magnetic_whole(1, true)

            @pl.when(b == 0)
            def _():
                rim_values(b)

            next_y = next_y + DE[1, 1]
            next_z = next_z + DE[1, 2]
            values = boundary(b, 1)
            for c in range(3):
                for p in range(PLANES):
                    H[p, c] = H[p, c] + DH[p, c]
                    J[p, c] = J[p, c] + DJ[p, c]
                    Q[p, c] = Q[p, c] + DQ[p, c]
                AE[c] = AE[c] + DE[0, c]
            for p in (1, 2):
                inject(E, (p,), p, values)
                oscillate(p, step, true)
            electric_whole(2, true)
            electric_whole(1, true)
            magnetic_whole(1, true)
            values = boundary(b, 2)
            put(H, (2,), magnetic(2, true))
            near_y, near_z = E[1, 1], E[1, 2]
            for p in (1, 2):
                inject(E, (p,), p, values)
            for c in range(3):
                partial[c] = E[1, c] + E[2, c]

            def close_right():
                hear_right(2)
                H[2, 1] = H[2, 1] + COURANT * (next_z + b_recv[s0 + 2, 1])
                H[2, 2] = H[2, 2] - COURANT * (next_y + b_recv[s0 + 2, 0])

            @pl.when(b < STEPS - 1)
            def _():
                close_right()
                tell_right(s0 + 3, H[2, 1], H[2, 2])

            hear_left(2)
            k_c = CO[3, 0]
            E[0, 0] = AE[0]
            E[0, 1] = AE[1] + k_c * h_recv[s0 + 2, 1]
            E[0, 2] = AE[2] - k_c * h_recv[s0 + 2, 0]
            put(H, (0,), magnetic(0, true, (near_y, near_z)))
            inject(E, (0,), 0, values)

            @pl.when(b < STEPS - 1)
            def _():
                open_block(s0 + 3)

            mean = average()
            mean_send[b] = mean
            for index in range(STEPS):

                @pl.when(b == index)
                def _(index=index):
                    mean_copy(index).start()

            pl.when(b == STEPS - 1)(close_right)

            @pl.when(b == 0)
            def _():
                heard(jnp.logical_not(outer), gain_copy(0))
                g = table_recv[4]
                for c in range(3):
                    f_send[c] = jnp.where(f_cells, g * mean[c], 0.0)
                go(has_right, f_copy(0))
                go(has_left, f_copy(1))

            return carry

        lax.fori_loop(0, STEPS, block, 0)
        for k in range(4):
            write(k)
        for slot in range(STEPS * SUBS):
            sent(has_right, h_copy(slot))
            sent(has_left, b_copy(slot))
        sent(has_right, f_copy(0), d_copy(0))
        sent(has_left, f_copy(1), d_copy(1))
        for index in range(STEPS):
            mean_copy(index).wait_send()
        written()

    @pl.when(is_coarse)
    def _():
        step = STEP_COARSE
        load_off.wait()
        corner_y = off_ref[0]
        guess = (TE, TH, TQ, TJ)

        def cut(value):
            return pltpu.roll(value[:, depth - box_z : depth], width - corner_y, 0)[:box_y]

        row, column = iota((width, box_z), 0), iota((width, box_z), 1)
        interior = (row >= corner_y + 1) & (row <= corner_y + box_y - 2) & (column >= 1) & (column <= box_z - 2)

        def inside(p):
            return interior & (fine_at[p] >= 1) & (fine_at[p] <= n_slab - 2)

        def place(index):
            for p in range(PLANES):

                @pl.when(in_box[p])
                def _(p=p):
                    mean_arrival(index, p).wait_recv()
                    for c in range(3):
                        tall = jnp.concatenate([mean_recv[index, p, c]] * (width // box_y), axis=0)
                        placed = pltpu.roll(tall, corner_y, 0)
                        kept = E[p, c, :, depth - box_z : depth]
                        E[p, c, :, depth - box_z : depth] = jnp.where(inside(p), placed, kept)

        def box_part(value):
            return value[:, depth - box_z : depth]

        def with_row(rows, value, at):
            taken = jnp.sum(jnp.where(iota(value.shape, 0) == at, value, 0.0), axis=0, keepdims=True)
            return jnp.where(iota(rows.shape, 0) == 7, taken, rows)

        def packed(rows, columns):
            return fold(rows, pltpu.roll(columns, width - corner_y, 0)[:box_y])

        def emit(index, p, values, scale=None):
            rows, columns = ends([box_part(v) for v in values], corner_y)
            if scale is not None:
                lane = iota(columns.shape, 1)
                columns = jnp.where(lane == 6, scale[:, 0:1], columns)
                columns = jnp.where(lane == 7, scale[:, box_z - 1 : box_z], columns)
                rows = with_row(rows, scale, corner_y)
            pack_send[index, p, 0] = packed(rows, columns)

            @pl.when(in_box[p] & full_at[p])
            def _():
                for c in range(3):
                    sec_send[index, p, c] = cut(values[c])

        def emit_near(index, y, z):
            rim_send[index] = packed(*ends([None, box_part(z), -box_part(y)], corner_y))

            @pl.when(in_box[PLANES] & full_at[PLANES])
            def _():
                near_send[index, 0], near_send[index, 1] = cut(y), cut(z)

        def send(index):
            for p in range(PLANES):
                for k in (1, 0, 2):
                    go(reaches(p, k), pack_copy(index, p, k))
                if p == 0:
                    for k in range(3):
                        go(reaches(PLANES, k), rim_copy(index, k))
            for p in range(PLANES):
                go(in_box[p] & full_at[p], section_copy(index, p))
            go(in_box[PLANES] & full_at[PLANES], near_copy(index))

        def first_half(state, slot_h, slot_b):
            e, h, _, _ = state
            for p in (1, 2):
                oscillate(p, step, state)
            electric_whole(2, state)
            electric_whole(1, state)
            k_c = CO[3, 0]
            e[0, 0] = b_send[slot_b, 2]
            e[0, 1] = b_send[slot_b, 0] + k_c * h_recv[slot_h, 1]
            e[0, 2] = b_send[slot_b, 1] - k_c * h_recv[slot_h, 0]
            magnetic_whole(1, state)
            magnetic_whole(0, state)

        def second_half(state, slot_h, slot_b):
            heard(has_right, b_copy(slot_b))
            k_c = CR[3]
            ahead = (
                b_recv[slot_b, 0] + k_c * h_send[slot_h, 1],
                b_recv[slot_b, 1] - k_c * h_send[slot_h, 0],
            )
            put(state[1], (2,), magnetic(2, state, ahead))

        def guess_from(p):
            for c in range(3):
                value = E[p, c]
                TE[p, c] = value
                TE[p, c, :, depth - box_z : depth] = jnp.where(inside(p) & in_box[p], 0.0, box_part(value))
                TQ[p, c] = Q[p, c]
                TJ[p, c] = J[p, c]

        set_coefficients(step)
        wait_loads(*[(k, p) for k in range(4) for p in range(PLANES)])
        h_send[0, 0], h_send[0, 1] = H[2, 1], H[2, 2]
        oscillate(0, step, true)
        start = electric(0, true)
        set_b(0, start)
        emit_near(0, H[2, 1], H[2, 2])
        scale = box_part(CO[3, 0])
        for p in range(PLANES):
            rows, columns = ends([box_part(E[p, c]) for c in range(3)], corner_y)
            if p == 0:
                rows = with_row(rows, scale, corner_y + box_y - 1)
            pack_send[0, p, 1] = packed(rows, columns)

            @pl.when(in_box[p] & full_at[p])
            def _(p=p):
                for c in range(3):
                    table_send[p, c] = cut(E[p, c])

        emit(0, 0, start, scale)
        for p in (2, 1):
            oscillate(p, step, true)
            electric_whole(p, true)
            emit(0, p, get(E, p))
        prepare()
        pl.semaphore_wait(barrier, count(has_left, has_right, *listens))
        go(has_right, h_copy(0))
        go(has_left, b_copy(0), m_next)
        send(0)
        for p in range(PLANES):

            @pl.when(in_box[p])
            def _(p=p):
                table_send[p, 3] = cut(CO[3, p])
                table_send[p, 4] = 1.0 - cut(CO[4, p]) * cut(CO[2, p])
                go(full_at[p], table_copy(p))
                go(jnp.logical_not(full_at[p]), gain_copy(p))

        magnetic_whole(1, true)
        for p in (1, 2):
            guess_from(p)
            oscillate(p, step, guess)
        for c in range(3):
            TH[1, c] = H[1, c]
        heard(has_left, h_copy(0))
        k_c = CO[3, 0]
        E[0, 0] = start[0]
        E[0, 1] = b_send[0, 0] + k_c * h_recv[0, 1]
        E[0, 2] = b_send[0, 1] - k_c * h_recv[0, 0]
        magnetic_whole(0, true)
        guess_from(0)
        for c in range(3):
            TH[0, c] = H[0, c]
        oscillate(0, step, guess)
        start = electric(0, guess)
        tell_left(1, start)
        emit(1, 0, start)
        electric_whole(1, guess)
        emit(1, 1, get(TE, 1))
        heard(has_right, m_next)
        sent(has_left, m_next)
        CR[3] = pick(m_right[0], [row[3] for row in tables(step)]) * has_right.astype(jnp.float32)
        second_half(true, 0, 0)
        tell_right(1, H[2, 1], H[2, 2])
        emit_near(1, H[2, 1], H[2, 2])
        for c in range(3):
            TH[2, c] = H[2, c]
        electric_whole(2, guess)
        emit(1, 2, get(TE, 2))
        send(1)
        magnetic_whole(1, guess)
        for p in (1, 2):
            oscillate(p, step, guess)
        heard(has_left, h_copy(1))
        TE[0, 0] = b_send[1, 2]
        TE[0, 1] = b_send[1, 0] + k_c * h_recv[1, 1]
        TE[0, 2] = b_send[1, 1] - k_c * h_recv[1, 0]
        magnetic_whole(0, guess)
        oscillate(0, step, guess)
        emit(2, 0, electric(0, guess))
        emit(2, 1, electric(1, guess, (TH[0, 1], TH[0, 2])))
        second_half(guess, 1, 1)
        emit_near(2, TH[2, 1], TH[2, 2])
        emit(2, 2, electric(2, guess, (TH[1, 1], TH[1, 2])))
        send(2)

        place(0)
        oscillate(0, step, true)
        tell_left(2, electric(0, true))
        first_half(true, 1, 2)
        second_half(true, 1, 2)
        tell_right(2, H[2, 1], H[2, 2])
        place(1)
        oscillate(0, step, true)
        tell_left(3, electric(0, true))
        heard(has_left, h_copy(2))
        first_half(true, 2, 3)
        write(2)
        write(3)
        write(0)
        second_half(true, 2, 3)
        write(1)
        for slot in range(3):
            sent(has_right, h_copy(slot))
        for slot in range(4):
            sent(has_left, b_copy(slot))
        for p in range(PLANES):
            sent(in_box[p] & full_at[p], table_copy(p))
            sent(in_box[p] & jnp.logical_not(full_at[p]), gain_copy(p))
            sent(in_box[p] & full_at[p], *[section_copy(index, p) for index in range(STEPS)])
            for k in range(3):
                sent(reaches(p, k), *[pack_copy(index, p, k) for index in range(STEPS)])
        for k in range(3):
            sent(reaches(PLANES, k), *[rim_copy(index, k) for index in range(STEPS)])
        sent(in_box[PLANES] & full_at[PLANES], *[near_copy(index) for index in range(STEPS)])
        written()
        for p in range(PLANES):
            heard(in_box[p], mean_arrival(STEPS - 1, p))


def hand_over(n_slab, width, depth, off_in, mean_in, *refs):
    sources, targets = refs[:4], refs[4:8]
    off_ref, mean, held, load_sem, out_sem = refs[8:]
    loads = [pltpu.make_async_copy(sources[k].at[0], held.at[k], load_sem.at[k]) for k in range(4)]
    stores = [pltpu.make_async_copy(held.at[k], targets[k].at[0], out_sem.at[k]) for k in range(4)]
    load_off = pltpu.make_async_copy(off_in, off_ref, load_sem.at[4])
    load_mean = pltpu.make_async_copy(mean_in, mean, load_sem.at[5])
    load_off.start()
    load_mean.start()
    for load in loads:
        load.start()
    slab = lax.axis_index("slab")
    is_coarse = lax.axis_index("grid") == 0
    box_y, box_z = width // 3, depth // 3
    load_off.wait()
    load_mean.wait()
    corner_y = off_ref[0]
    row, column = iota((width, box_z), 0), iota((width, box_z), 1)
    interior = (row >= corner_y + 1) & (row <= corner_y + box_y - 2) & (column >= 1) & (column <= box_z - 2)
    loads[0].wait()
    for p in range(PLANES):
        fine = 3 * (slab - n_slab // 8) + p

        @pl.when(is_coarse & (fine >= 1) & (fine <= n_slab - 2))
        def _(p=p):
            for c in range(3):
                tall = jnp.concatenate([mean[p, c]] * (width // box_y), axis=0)
                placed = pltpu.roll(tall, corner_y, 0)
                kept = held[0, c, p, :, depth - box_z : depth]
                held[0, c, p, :, depth - box_z : depth] = jnp.where(interior, placed, kept)

    stores[0].start()
    for k in (1, 2, 3):
        loads[k].wait()
        stores[k].start()
    for store in stores:
        store.wait()


def on_device(n_slab, efield, hfield, polar, current, material, box_offset):
    planes, width, depth = efield.shape[2:]
    box = (width // 3, depth // 3)
    plane = (width, depth)
    f32 = jnp.float32
    dma = pltpu.SemaphoreType.DMA
    slots = STEPS * SUBS

    def room(*shape, dtype=f32):
        return pltpu.VMEM(shape, dtype)

    state = room(planes, 3, *plane)
    triple = room(3, *plane)
    scratch = [pltpu.SMEM((2,), jnp.int32)] + [state] * 8 + [
        room(planes, *plane, dtype=jnp.int32),
        room(5, planes, *plane),
        room(*plane, dtype=jnp.int32),
        room(2, *plane, dtype=jnp.int32),
        room(*plane),
        room(6, *plane),
    ]
    scratch += [triple] * 8
    scratch += [room(slots, 2, *plane), room(slots, 2, *plane), room(slots, 3, *plane), room(slots, 2, *plane)]
    scratch += [
        room(STEPS, planes, 3, *box),
        room(STEPS, 3, *box),
        room(planes, 5, *box),
        room(5, *box),
        room(STEPS, 2, *box),
        room(STEPS, 2, *box),
        room(2, 3, 3, *plane),
        room(6, *plane),
        state,
        state,
        state,
        room(2, 3, *plane),
        room(STEPS, 3, *box),
        room(STEPS - 1, planes, 3, *box),
        room(3, *box),
        room(2, 3, *box),
        room(STEPS, planes, 2, 8, box[1]),
        room(STEPS, 3, 2, 8, box[1]),
        room(STEPS, 8, box[1]),
        room(STEPS, 8, box[1]),
        room(3, *box),
        room(8, box[1]),
        room(2, 8, box[1]),
    ]
    scratch += [dma, dma((5, planes)), dma((4, planes)), dma((4,))]
    scratch += [dma((slots,))] * 4
    scratch += [dma((STEPS, planes)), dma((STEPS,)), dma((planes,)), dma, dma((STEPS,)), dma((STEPS,))]
    scratch += [dma((STEPS,)), dma((STEPS, planes)), dma((2,)), dma((2,))]
    scratch += [dma((STEPS, planes, 3)), dma((STEPS, 3)), dma((STEPS, 3)), dma((STEPS,))]
    scratch += [dma((2,)), dma((2,))]
    whole = pl.BlockSpec(memory_space=pl.ANY)
    fields = [jax.ShapeDtypeStruct(efield.shape, f32)] * 4
    state = pl.pallas_call(
        functools.partial(kernel, n_slab, width, depth),
        out_shape=fields + [jax.ShapeDtypeStruct((planes, 3, *box), f32)],
        in_specs=[whole] * 6,
        out_specs=[whole] * 5,
        scratch_shapes=scratch,
        compiler_params=pltpu.CompilerParams(
            collective_id=1, has_side_effects=True, vmem_limit_bytes=60 * 1024 * 1024
        ),
    )(box_offset, efield, hfield, polar, current, material)
    *state, mean = state
    return pl.pallas_call(
        functools.partial(hand_over, n_slab, width, depth),
        out_shape=fields,
        in_specs=[whole] * 6,
        out_specs=[whole] * 4,
        scratch_shapes=[
            pltpu.SMEM((2,), jnp.int32),
            room(planes, 3, *box),
            room(4, 3, planes, *plane),
            dma((6,)),
            dma((4,)),
        ],
        compiler_params=pltpu.CompilerParams(vmem_limit_bytes=60 * 1024 * 1024),
    )(box_offset, mean, *state)


def solution(mesh):
    field = P("grid", "angle", "slab", None, None)
    return jax.shard_map(
        functools.partial(on_device, mesh.shape["slab"]),
        mesh=mesh,
        in_specs=(field, field, field, field, P("grid", "slab", None, None), P()),
        out_specs=(field, field, field, field),
        check_vma=False,
    )
```

```python
import functools

import jax
import jax.numpy as jnp
from jax import lax
from jax.experimental import pallas as pl
from jax.experimental.pallas import tpu as pltpu
from jax.sharding import PartitionSpec as P

STEPS = 3
SUBS = 3
PERMITTIVITY = (1.0, 1.5, 1.2, 2.0)
STRENGTH = (0.4, 0.9, 0.3, 1.1)
RESONANCE = (0.6, 0.5, 0.8, 0.3)
DAMPING_RATE = (0.3, 0.2, 0.05, 0.4)
COURANT = 0.5
STEP_COARSE = 0.5
STEP_FINE = STEP_COARSE / 3.0
PLANES = 3
MESH = pl.DeviceIdType.MESH
EXACT = lax.Precision.HIGHEST


def tables(step):
    rows = zip(PERMITTIVITY, STRENGTH, RESONANCE, DAMPING_RATE)
    return [
        (1.0 - step * d, -step * r, step * s * r, COURANT / e, step / e) for e, s, r, d in rows
    ]


def pick(material, values):
    out = jnp.full(material.shape, values[0], jnp.float32)
    for index in range(1, 4):
        out = jnp.where(material == index, jnp.float32(values[index]), out)
    return out


def iota(shape, dim):
    return lax.broadcasted_iota(jnp.int32, shape, dim)


def down_y(u):
    return jnp.where(iota(u.shape, 0) == 0, 0.0, pltpu.roll(u, 1, 0))


def up_y(u):
    last = u.shape[0] - 1
    return jnp.where(iota(u.shape, 0) == last, 0.0, pltpu.roll(u, last, 0))


def down_z(u):
    return jnp.where(iota(u.shape, 1) == 0, 0.0, pltpu.roll(u, 1, 1))


def up_z(u):
    last = u.shape[1] - 1
    return jnp.where(iota(u.shape, 1) == last, 0.0, pltpu.roll(u, last, 1))


def curl_h(h, back=None):
    x, y, z = h
    c_x = (z - down_y(z)) - (y - down_z(y))
    c_y, c_z = -z, y
    if x is not None:
        c_y, c_z = (x - down_z(x)) - z, y - (x - down_y(x))
    if back is not None:
        c_y, c_z = c_y + back[1], c_z - back[0]
    return c_x, c_y, c_z


def curl_e(e, ahead=None):
    x, y, z = e
    c_x = (up_y(z) - z) - (up_z(y) - y)
    c_y, c_z = z, -y
    if x is not None:
        c_y, c_z = (up_z(x) - x) + z, -y - (up_y(x) - x)
    if ahead is not None:
        c_y, c_z = c_y - ahead[1], c_z + ahead[0]
    return c_x, c_y, c_z


def groups(few, many, many_dim):
    shape = (few, many) if many_dim == 1 else (many, few)
    return ones_where(iota(shape, many_dim) // 3 == iota(shape, 1 - many_dim))


def ones_where(condition):
    return jnp.where(condition, 1.0, 0.0).astype(jnp.bfloat16)


def terms(value):
    out = []
    for _ in range(3):
        out.append(value.astype(jnp.bfloat16))
        value = value - out[-1].astype(jnp.float32)
    return out


def times(wide, matrix):
    rows = wide.shape[0]
    parts = jnp.dot(jnp.concatenate(terms(wide), axis=0), matrix, preferred_element_type=jnp.float32)
    return parts[:rows] + parts[rows : 2 * rows] + parts[2 * rows :]


def times_left(matrix, wide):
    tall = jnp.concatenate(terms(wide), axis=0)
    return jnp.dot(jnp.concatenate([matrix] * 3, axis=1), tall, preferred_element_type=jnp.float32)


def ends(values, first):
    shape = next(v for v in values if v is not None).shape
    row, lane = iota(shape, 0), iota(shape, 1)
    flat = (8, shape[1])
    flat_row = iota(flat, 0)
    rows, columns = jnp.zeros(flat, jnp.float32), jnp.zeros(shape, jnp.float32)
    for c, value in enumerate(values):
        if value is not None:
            for side, at, column in ((0, first, 0), (1, first + 7, shape[1] - 1)):
                if isinstance(first, int):
                    taken = value[at : at + 1]
                else:
                    taken = jnp.sum(jnp.where(row == at, value, 0.0), axis=0, keepdims=True)
                rows = jnp.where(flat_row == 2 * c + side, taken, rows)
                columns = jnp.where(lane == 2 * c + side, value[:, column : column + 1], columns)
    return rows, columns


def fold(rows, columns):
    columns = jnp.where(iota(columns.shape, 1) < 8, columns, 0.0)
    line = jnp.sum(pltpu.roll(columns, 0, 1, stride=8, stride_axis=0), axis=0, keepdims=True)
    return jnp.where(iota(rows.shape, 0) == 6, line, rows)


def unfold(packed):
    line = jnp.broadcast_to(packed[6:7], packed.shape)
    out, row = line, iota(packed.shape, 0)
    for y in range(1, 8):
        out = jnp.where(row == y, pltpu.roll(line, packed.shape[1] - 8 * y, 1), out)
    return out


def unpack(rows, columns, width, depth):
    box_y, box_z = width // 3, depth // 3
    wide = times(jnp.concatenate(rows, axis=0), groups(box_z, depth, 1))
    spread = times_left(groups(3 * box_y, 3 * width, 0), jnp.concatenate(columns, axis=0))
    row, column = iota((width, depth), 0), iota((width, depth), 1)
    planes = []
    for j in range(3):
        plane = []
        for c in range(3):
            at, k = 8 * j + 2 * c, 2 * c
            side = spread[j * width : (j + 1) * width]
            value = jnp.where(column == 0, side[:, k : k + 1], 0.0)
            value = jnp.where(column == depth - 1, side[:, k + 1 : k + 2], value)
            value = jnp.where(row == 0, wide[at : at + 1], value)
            plane.append(jnp.where(row == width - 1, wide[at + 1 : at + 2], value))
        planes.append(plane)
    return planes


def kernel(
    n_slab, width, depth,
    off_in, e_in, h_in, p_in, j_in, m_in,
    e_out, h_out, p_out, j_out, mean_out,
    off_ref, E, H, Q, J, TE, TH, TQ, TJ, M, CO, m_left, m_right, CL, CR,
    AE, AH, AQ, AJ, A1, BE, BH, partial,
    h_send, h_recv, b_send, b_recv,
    sec_send, sec_recv, table_send, table_recv, near_send, near_recv,
    U, GA, DH, DJ, DQ, DE, mean_send, mean_recv, f_send, f_recv,
    pack_send, pack_recv, rim_send, rim_recv, D, d_send, d_recv,
    off_sem, load_sem, out_sem, m_sem,
    hs_sem, hr_sem, bs_sem, br_sem, ss_sem, sr_sem, ts_sem, tr_sem, ns_sem, nr_sem,
    ms_sem, mr_sem, fs_sem, fr_sem,
    ps_sem, pr_sem, es_sem, er_sem, ds_sem, dr_sem,
):
    slab = lax.axis_index("slab")
    level = lax.axis_index("grid")
    box_y, box_z = width // 3, depth // 3
    first_slab = n_slab // 8
    is_fine = level == 1
    is_coarse = level == 0
    has_left = slab > 0
    has_right = slab < n_slab - 1
    partner_slab = first_slab + slab // 3
    partner_plane = slab % 3
    outer = (slab == 0) | (slab == n_slab - 1)
    borrows = outer & (partner_plane == 0)
    seam = jnp.where(partner_plane == 0, 1, jnp.where(partner_plane == 1, 0, 2))
    has_seam = slab + seam - 1 < n_slab
    near_fines = [3 * (slab - first_slab) + k for k in range(-1, PLANES + 2)]
    listens = [(f >= 0) & (f < n_slab) for f in near_fines]
    listens[0] = listens[0] & (near_fines[1] < n_slab)
    fine_at = [3 * (slab - first_slab) + p for p in range(PLANES + 1)]
    in_box = [(f >= 0) & (f < n_slab) for f in fine_at]
    full_at = [(f == 0) | (f == n_slab - 1) for f in fine_at]

    fields = ((e_in, E, e_out), (h_in, H, h_out), (p_in, Q, p_out), (j_in, J, j_out))
    loads = [
        [pltpu.make_async_copy(src.at[0, :, p], dst.at[p], load_sem.at[k, p]) for p in range(PLANES)]
        for k, (src, dst, _) in enumerate(fields)
    ]
    load_m = pltpu.make_async_copy(m_in.at[0], M, load_sem.at[4, 0])

    barrier = pltpu.get_barrier_semaphore()

    def greet(condition, target):
        @pl.when(condition)
        def _():
            pl.semaphore_signal(barrier, inc=1, device_id=target, device_id_type=MESH)

    def count(*conditions):
        return sum(c.astype(jnp.int32) for c in conditions)

    greet(is_fine, {"grid": 0, "slab": partner_slab})
    greet(is_fine & (partner_plane < 2), {"grid": 0, "slab": partner_slab - 1})
    greet(is_fine & (partner_plane == 2) & has_right, {"grid": 0, "slab": partner_slab + 1})
    greet(has_left, {"slab": slab - 1})
    greet(has_right, {"slab": slab + 1})

    load_off = pltpu.make_async_copy(off_in, off_ref, off_sem)
    pl.when(is_coarse)(load_off.start)
    load_m.start()
    for p in range(PLANES):
        for k in range(4):
            loads[k][p].start()

    def remote(src, dst, send, recv, target):
        return pltpu.make_async_remote_copy(
            src_ref=src, dst_ref=dst, send_sem=send, recv_sem=recv, device_id=target, device_id_type=MESH
        )

    left, right = {"slab": slab - 1}, {"slab": slab + 1}

    def h_copy(slot):
        return remote(h_send.at[slot], h_recv.at[slot], hs_sem.at[slot], hr_sem.at[slot], right)

    def b_copy(slot):
        return remote(b_send.at[slot, 0:2], b_recv.at[slot], bs_sem.at[slot], br_sem.at[slot], left)

    m_next = remote(m_in.at[0, 0:1], m_right.at[0:1], m_sem.at[0], m_sem.at[1], left)
    m_to_left = remote(m_in.at[0, 0:2], m_right, m_sem.at[0], m_sem.at[1], left)
    m_to_right = remote(m_in.at[0, 2], m_left, m_sem.at[2], m_sem.at[3], right)

    def section_copy(index, p):
        return remote(
            sec_send.at[index, p], sec_recv.at[index], ss_sem.at[index, p], sr_sem.at[index],
            {"grid": 1, "slab": fine_at[p]},
        )

    def table_copy(p):
        return remote(
            table_send.at[p], table_recv, ts_sem.at[p], tr_sem, {"grid": 1, "slab": fine_at[p]}
        )

    def gain_copy(p):
        return remote(
            table_send.at[p, 3:5], table_recv.at[3:5], ts_sem.at[p], tr_sem, {"grid": 1, "slab": fine_at[p]}
        )

    def near_copy(index):
        return remote(
            near_send.at[index], near_recv.at[index], ns_sem.at[index], nr_sem.at[index],
            {"grid": 1, "slab": fine_at[PLANES]},
        )

    def mean_copy(index):
        room = mean_out if index == STEPS - 1 else mean_recv.at[index]
        return remote(
            mean_send.at[index], room.at[partner_plane], ms_sem.at[index],
            mr_sem.at[index, partner_plane], {"grid": 0, "slab": partner_slab},
        )

    def mean_arrival(index, p):
        room = mean_out if index == STEPS - 1 else mean_recv.at[index]
        return remote(
            mean_send.at[index], room.at[p], ms_sem.at[index], mr_sem.at[index, p],
            {"grid": 1, "slab": fine_at[p]},
        )

    def f_copy(side):
        return remote(f_send, f_recv.at[side], fs_sem.at[side], fr_sem.at[side], right if side == 0 else left)

    def pack_copy(index, p, k):
        size = 2 if isinstance(index, int) and index == 0 else 1
        return remote(
            pack_send.at[index, p, 0:size], pack_recv.at[index, 2 - k, 0:size],
            ps_sem.at[index, p, k], pr_sem.at[index, 2 - k],
            {"grid": 1, "slab": fine_at[p] + k - 1},
        )

    def rim_copy(index, k):
        return remote(
            rim_send.at[index], rim_recv.at[index], es_sem.at[index, k], er_sem.at[index],
            {"grid": 1, "slab": fine_at[PLANES] + k - 1},
        )

    def d_copy(side):
        return remote(d_send, d_recv.at[side], ds_sem.at[side], dr_sem.at[side], right if side == 0 else left)

    def reaches(p, k):
        target = fine_at[p] + k - 1
        return in_box[p] & (target >= 0) & (target < n_slab)

    def go(condition, *copies):
        @pl.when(condition)
        def _():
            for copy in copies:
                copy.start()

    def heard(condition, *copies):
        @pl.when(condition)
        def _():
            for copy in copies:
                copy.wait_recv()

    def sent(condition, *copies):
        @pl.when(condition)
        def _():
            for copy in copies:
                copy.wait_send()

    def get(ref, *index):
        return tuple(ref[(*index, c)] for c in range(3))

    def put(ref, index, values):
        for c, value in enumerate(values):
            if value is not None:
                ref[(*index, c)] = value

    def oscillate(p, step, state):
        e, _, q, j = state
        a_j, a_p, a_e = CO[0, p], CO[1, p], CO[2, p]
        for c in range(3):
            current = a_j * j[p, c] + a_p * q[p, c] + a_e * e[p, c]
            j[p, c] = current
            q[p, c] = q[p, c] + step * current

    def electric(p, state, back=None):
        e, h, _, j = state
        k_c, k_j = CO[3, p], CO[4, p]
        curl = curl_h(get(h, p), back)
        return tuple(e[p, c] - k_j * j[p, c] + k_c * curl[c] for c in range(3))

    def electric_whole(p, state):
        put(state[0], (p,), electric(p, state, (state[1][p - 1, 1], state[1][p - 1, 2])))

    def magnetic(p, state, ahead=None):
        e, h, _, _ = state
        curl = curl_e(get(e, p), ahead)
        return tuple(h[p, c] - COURANT * curl[c] for c in range(3))

    def magnetic_whole(p, state):
        put(state[1], (p,), magnetic(p, state, (state[0][p + 1, 1], state[0][p + 1, 2])))

    def set_coefficients(step):
        load_m.wait()
        values = tables(step)
        for p in range(PLANES):
            material = M[p]
            for k in range(5):
                CO[k, p] = pick(material, [row[k] for row in values])

    def learn_neighbours(step):
        heard(has_right, m_to_left)
        heard(has_left, m_to_right)
        sent(has_left, m_to_left)
        sent(has_right, m_to_right)
        values = tables(step)
        near, far = m_right[0], m_right[1]
        is_there = has_right.astype(jnp.float32)
        for k in range(5):
            scale = is_there if k == 3 else 1.0
            CR[k] = pick(near, [row[k] for row in values]) * scale
        CR[5] = pick(far, [row[3] for row in values]) * is_there
        before = m_left[...]
        CL[...] = pick(before, [row[3] for row in values]) * has_left.astype(jnp.float32)
        gains = [1.0 - row[4] * row[2] for row in values]
        for q, material in enumerate((before, M[0], M[1], M[2], near, far)):
            GA[q] = pick(material, gains)

    def prepare():
        @pl.when(jnp.logical_not(has_left))
        def _():
            h_recv[...] = jnp.zeros_like(h_recv)
            m_left[...] = jnp.zeros_like(m_left)

        @pl.when(jnp.logical_not(has_right))
        def _():
            b_recv[...] = jnp.zeros_like(b_recv)
            m_right[...] = jnp.zeros_like(m_right)

    def tell_right(slot, y, z):
        h_send[slot, 0], h_send[slot, 1] = y, z
        go(has_right, h_copy(slot))

    def set_b(slot, b):
        b_send[slot, 0], b_send[slot, 1], b_send[slot, 2] = b[1], b[2], b[0]

    def tell_left(slot, b):
        set_b(slot, b)
        go(has_left, b_copy(slot))

    def wait_loads(*which):
        for k, p in which:
            loads[k][p].wait()

    def write(k):
        for p in range(PLANES):
            pltpu.make_async_copy(fields[k][1].at[p], fields[k][2].at[0, :, p], out_sem.at[k, p]).start()

    def written():
        for k in range(4):
            for p in range(PLANES):
                pltpu.make_async_copy(fields[k][1].at[p], fields[k][2].at[0, :, p], out_sem.at[k, p]).wait()

    true = (E, H, Q, J)

    @pl.when(is_fine)
    def _():
        step = STEP_FINE
        row, column = iota((width, depth), 0), iota((width, depth), 1)
        edge = (row == 0) | (row == width - 1) | (column == 0) | (column == depth - 1)
        rims = [edge | (slab == 0), edge, edge | (slab == n_slab - 1)]
        small_row, small_column = iota((box_y, box_z), 0), iota((box_y, box_z), 1)
        f_cells = (
            (small_row >= 1) & (small_row <= box_y - 2) & (small_column >= 1) & (small_column <= box_z - 2)
            & (slab >= 1) & (slab <= n_slab - 2)
        )

        def upsampled(section):
            section = section.reshape(3 * box_y, box_z)
            wide = times(section, groups(box_z, depth, 1))
            return times_left(groups(3 * box_y, 3 * width, 0), wide).reshape(3, width, depth)

        def average():
            total = jnp.concatenate([E[0, c] + partial[c] for c in range(3)], axis=0)
            rows = times_left(groups(3 * box_y, 3 * width, 1), total)
            both = times(rows, groups(box_z, depth, 0))
            return (both * jnp.float32(1.0 / 27.0)).reshape(3, box_y, box_z)

        def boundary(b, sub, j=1):
            weight = jnp.float32((sub + 1) / 3.0)
            before, after = U.at[b % 2, j], U.at[(b + 1) % 2, j]
            return [before[c] + weight * (after[c] - before[c]) for c in range(3)]

        def inject(ref, index, p, values):
            for c in range(3):
                ref[(*index, c)] = jnp.where(rims[p], values[c], ref[(*index, c)])

        def open_block(first_slot):
            oscillate(0, step, true)
            e = electric(0, true)
            put(AE, (), e)
            tell_left(first_slot, e)

        set_coefficients(step)
        wait_loads((0, 0), (1, 0), (2, 0), (3, 0), (1, 2))
        prepare()

        @pl.when(outer & jnp.logical_not(borrows))
        def _():
            near_recv[...] = jnp.zeros_like(near_recv)

        @pl.when(jnp.logical_not(has_seam))
        def _():
            rim_recv[...] = jnp.zeros_like(rim_recv)

        @pl.when(jnp.logical_not(has_left))
        def _():
            f_recv[0] = jnp.zeros_like(f_recv[0])
            d_recv[0] = jnp.zeros_like(d_recv[0])
            for index in range(STEPS):
                pack_recv[index, 0] = jnp.zeros_like(pack_recv[index, 0])

        @pl.when(jnp.logical_not(has_right))
        def _():
            f_recv[1] = jnp.zeros_like(f_recv[1])
            d_recv[1] = jnp.zeros_like(d_recv[1])
            for index in range(STEPS):
                pack_recv[index, 2] = jnp.zeros_like(pack_recv[index, 2])

        pl.semaphore_wait(barrier, count(has_left, has_right))
        tell_right(0, H[2, 1], H[2, 2])
        open_block(0)
        go(has_left, m_to_left)
        go(has_right, m_to_right)
        wait_loads(*[(k, p) for k in range(4) for p in (1, 2) if (k, p) != (1, 2)])

        def fill(slot, rows, columns, section):
            for j, plane in enumerate(unpack(rows, columns, width, depth)):
                for c in range(3):
                    U[slot, j, c] = plane[c]

            @pl.when(outer)
            def _():
                whole = upsampled(section())
                for c in range(3):
                    U[slot, 1, c] = whole[c]

        def rim_values(b):
            for index, now in ((0, b == 0), (b, b > 0)):
                heard(now, pack_copy(index, 0, 1))
                heard(now & has_left, pack_copy(index, 0, 2))
                heard(now & has_right, pack_copy(index, 0, 0))

            heard(has_seam, rim_copy(b, 0))
            heard(outer, section_copy(b, 0))
            heard(borrows, near_copy(b))

            @pl.when(b == 0)
            def _():
                heard(outer, table_copy(0))
                before = [pack_recv[0, j, 1] for j in range(3)]
                fill(0, before, [unfold(v) for v in before], lambda: table_recv[0:3])

            near = rim_recv[b]
            near_columns = unfold(near)
            flat_row, lane = iota(near.shape, 0), iota(near.shape, 1)
            rows, columns = [], []
            for j in range(3):
                here, origin = pack_recv[b, j, 0], pack_recv[0, j, 0]
                sides = unfold(origin)
                k_rows = jnp.where((flat_row == 2) | (flat_row == 4), origin[7:8], pack_recv[0, j, 1][7:8])
                k_sides = jnp.where((lane == 2) | (lane == 4), sides[:, 6:7], sides[:, 7:8])
                rows.append(here + jnp.where((flat_row >= 2) & (flat_row <= 5), k_rows * near, 0.0))
                columns.append(unfold(here) + jnp.where((lane >= 2) & (lane <= 5), k_sides * near_columns, 0.0))

            def section(extra=None):
                k_c = table_recv[3]
                base = sec_recv[b]
                parts = [
                    base[0], base[1] + k_c * near_recv[b, 1], base[2] - k_c * near_recv[b, 0],
                ]
                if extra is not None:
                    parts = [part + extra[c] for c, part in enumerate(parts)]
                return jnp.stack(parts)

            @pl.when(b < STEPS - 1)
            def _():
                fill((b + 1) % 2, rows, columns, section)

            @pl.when(b == STEPS - 1)
            def _():
                heard(has_left, d_copy(0))
                heard(has_right, d_copy(1))
                extras = (d_recv[0], d_send[...], d_recv[1])
                fill(
                    (b + 1) % 2, [r + e for r, e in zip(rows, extras)],
                    [k + unfold(e) for k, e in zip(columns, extras)], lambda: section(D),
                )

            first = [boundary(b, 0, 0)]
            second = [None]
            for p in range(PLANES):
                first.append([jnp.where(rims[p], v, 0.0) for v in boundary(b, 0)])
                second.append([jnp.where(rims[p], v, 0.0) for v in boundary(b, 1)])
            first += [boundary(b, 0, 2)] * 2
            second.append(boundary(b, 1, 2))
            d_e = [[GA[q] * v for v in first[q]] for q in range(6)]
            d_h = []
            for q in range(5):
                curl = curl_e(d_e[q], (d_e[q + 1][1], d_e[q + 1][2]))
                d_h.append([-COURANT * u for u in curl])
            there = has_left.astype(jnp.float32)
            d_h[0] = [there * u for u in d_h[0]]
            for p in range(PLANES):
                put(DH, (p,), d_h[p + 1])
            for p in (1, 2):
                d_j = [CO[2, p] * v for v in first[p + 1]]
                put(DJ, (p,), d_j)
                put(DQ, (p,), [step * v for v in d_j])
            for q, at in ((1, 0), (4, 1)):
                a_j, a_p, a_e, k_c, k_j = [CO[k, 0] for k in range(5)] if at == 0 else [CR[k] for k in range(5)]
                curl = curl_h(d_h[q], (d_h[q - 1][1], d_h[q - 1][2]))
                for c in range(3):
                    early = a_e * first[q][c]
                    late = (a_j + step * a_p) * early + a_e * second[q][c]
                    DE[at, c] = second[q][c] - k_j * late + k_c * curl[c]
                    if at == 0:
                        DJ[0, c] = late
                        DQ[0, c] = step * (early + late)

        def feedback_response():
            heard(has_left, f_copy(0))
            heard(has_right, f_copy(1))
            here, before, after = f_send, f_recv.at[0], f_recv.at[1]
            curl = curl_e((here[0], here[1], here[2]), (after[1], after[2]))
            back_x = (up_z(before[0]) - before[0], up_y(before[0]) - before[0])
            back_y = back_x[0] - (here[2] - before[2])
            back_z = (here[1] - before[1]) - back_x[1]
            twice = curl_h(curl, (back_y, back_z))
            return [-COURANT * table_recv[3] * t for t in twice]

        def block(b, carry):
            s0 = 3 * b
            for p in (1, 2):
                oscillate(p, step, true)
            electric_whole(2, true)
            electric_whole(1, true)
            h = magnetic(2, true)
            put(BH, (), h)
            tell_right(s0 + 1, h[1], h[2])
            magnetic_whole(1, true)
            curl = curl_e(get(AE), (E[1, 1], E[1, 2]))
            put(AH, (), [H[0, c] - COURANT * curl[c] for c in range(3)])

            nothing = [jnp.zeros((width, depth), jnp.float32)] * 3
            inject(AE, (), 0, nothing)
            inject(E, (1,), 1, nothing)
            inject(E, (2,), 2, nothing)
            a_j, a_p, a_e, k_c, k_j = (CO[k, 0] for k in range(5))
            for c in range(3):
                current = a_j * J[0, c] + a_p * Q[0, c] + a_e * AE[c]
                AJ[c] = current
                AQ[c] = Q[0, c] + step * current
            curl = curl_h(get(AH))
            e_0 = tuple(AE[c] - k_j * AJ[c] + k_c * curl[c] for c in range(3))
            put(AE, (), e_0)
            tell_left(s0 + 1, e_0)
            for p in (1, 2):
                oscillate(p, step, true)
            curl = curl_h(get(BH), (H[1, 1], H[1, 2]))
            e_2 = tuple(E[2, c] - CO[4, 2] * J[2, c] + CO[3, 2] * curl[c] for c in range(3))
            put(BE, (), e_2)
            curl = curl_e(e_2)
            h = tuple(BH[c] - COURANT * curl[c] for c in range(3))
            put(BH, (), h)
            tell_right(s0 + 2, h[1], h[2])
            curl = curl_h(get(H, 1), (AH[1], AH[2]))
            e_1 = tuple(E[1, c] - CO[4, 1] * J[1, c] + CO[3, 1] * curl[c] for c in range(3))
            put(A1, (), e_1)
            curl = curl_e(get(AE), (A1[1], A1[2]))
            put(AH, (), [AH[c] - COURANT * curl[c] for c in range(3)])
            inject(AE, (), 0, nothing)
            for c in range(3):
                current = a_j * AJ[c] + a_p * AQ[c] + a_e * AE[c]
                AJ[c] = current
                AQ[c] = AQ[c] + step * current
            curl = curl_h(get(AH))
            e_0 = tuple(AE[c] - k_j * AJ[c] + k_c * curl[c] for c in range(3))
            put(AE, (), e_0)
            tell_left(s0 + 2, e_0)

            @pl.when(b == 0)
            def _():
                learn_neighbours(step)

            @pl.when(b == 1)
            def _():
                extra = feedback_response()
                for c in range(3):
                    D[c] = extra[c]
                d_send[...] = fold(*ends(extra, 0))
                go(has_right, d_copy(0))
                go(has_left, d_copy(1))

            @pl.when(b > 0)
            def _():
                rim_values(b)

            def face(coefficients, k_near, k_back, there, h_own, e_own, hear):
                a_j, a_p, a_e, k_c, k_j = coefficients
                side = COURANT * there.astype(jnp.float32)

                def kept(u):
                    return jnp.where(edge, 0.0, u)

                hear(0)
                h_y, h_z = h_own(0)
                e_y, e_z = e_own(0)
                d_y, d_z = k_c * h_z, -k_c * h_y
                e_y, e_z = e_y + d_y, e_z + d_z
                l_y, l_z = side * e_z, -side * e_y
                d_h = tuple(-COURANT * u for u in curl_e((None, d_y, d_z)))
                d_y, d_z = kept(d_y), kept(d_z)
                j_y, j_z = a_e * d_y, a_e * d_z
                p_y, p_z = step * j_y, step * j_z
                hear(1)
                h_y, h_z = h_own(1)
                e_y, e_z = e_own(1)
                h_y, h_z = h_y + l_y, h_z + l_z
                curl = curl_h(d_h, (h_y, h_z))
                d_x = k_c * curl[0]
                d_y = d_y - k_j * j_y + k_c * curl[1]
                d_z = d_z - k_j * j_z + k_c * curl[2]
                e_y, e_z = e_y + d_y, e_z + d_z
                l_e = tuple(k_back * u for u in curl_h((None, l_y, l_z)))
                curl = curl_e(l_e)
                l_h = (
                    -COURANT * curl[0],
                    l_y - COURANT * curl[1] + side * e_z,
                    l_z - COURANT * curl[2] - side * e_y,
                )
                f_y, f_z = k_near * d_h[2], -k_near * d_h[1]
                curl = curl_e((d_x, d_y, d_z), (f_y, f_z))
                d_h = tuple(d_h[c] - COURANT * curl[c] for c in range(3))
                d_e = kept(d_x), kept(d_y), kept(d_z)
                d_j = (a_e * d_e[0], a_j * j_y + a_p * p_y + a_e * d_e[1], a_j * j_z + a_p * p_z + a_e * d_e[2])
                d_p = (step * d_j[0], p_y + step * d_j[1], p_z + step * d_j[2])
                curl = curl_h(d_h, (l_h[1], l_h[2]))
                d_e = tuple(d_e[c] - k_j * d_j[c] + k_c * curl[c] for c in range(3))
                return d_e, d_j, d_p, d_h, (f_y, f_z), l_e, l_h

            def hear_left(m):
                heard(has_left, h_copy(s0 + m))

            def hear_right(m):
                heard(has_right, b_copy(s0 + m))

            d_e, _, _, _, _, l_e, l_h = face(
                [CR[k] for k in range(5)], CR[5], CO[3, 2], has_right,
                lambda m: (h_send[s0 + m, 0], h_send[s0 + m, 1]),
                lambda m: (b_recv[s0 + m, 0], b_recv[s0 + m, 1]),
                hear_right,
            )
            k_c = CR[3]
            next_y = d_e[1] + k_c * h_send[s0 + 2, 1]
            next_z = d_e[2] - k_c * h_send[s0 + 2, 0]
            put(H, (2,), [BH[c] + l_h[c] for c in range(3)])
            put(E, (2,), [BE[c] + l_e[c] for c in range(3)])
            d_e, d_j, d_p, d_h, near, _, _ = face(
                [CO[k, 0] for k in range(5)], CO[3, 1], CL[...], has_left,
                lambda m: (h_recv[s0 + m, 0], h_recv[s0 + m, 1]),
                lambda m: (b_send[s0 + m, 0], b_send[s0 + m, 1]),
                hear_left,
            )
            put(H, (0,), [AH[c] + d_h[c] for c in range(3)])
            put(J, (0,), [AJ[c] + d_j[c] for c in range(3)])
            put(Q, (0,), [AQ[c] + d_p[c] for c in range(3)])
            put(AE, (), [AE[c] + d_e[c] for c in range(3)])
            put(E, (1,), [A1[0], A1[1] + near[0], A1[2] + near[1]])

            magnetic_whole(1, true)

            @pl.when(b == 0)
            def _():
                rim_values(b)

            next_y = next_y + DE[1, 1]
            next_z = next_z + DE[1, 2]
            values = boundary(b, 1)
            for c in range(3):
                for p in range(PLANES):
                    H[p, c] = H[p, c] + DH[p, c]
                    J[p, c] = J[p, c] + DJ[p, c]
                    Q[p, c] = Q[p, c] + DQ[p, c]
                AE[c] = AE[c] + DE[0, c]
            for p in (1, 2):
                inject(E, (p,), p, values)
                oscillate(p, step, true)
            electric_whole(2, true)
            electric_whole(1, true)
            magnetic_whole(1, true)
            values = boundary(b, 2)
            put(H, (2,), magnetic(2, true))
            near_y, near_z = E[1, 1], E[1, 2]
            for p in (1, 2):
                inject(E, (p,), p, values)
            for c in range(3):
                partial[c] = E[1, c] + E[2, c]

            def close_right():
                hear_right(2)
                H[2, 1] = H[2, 1] + COURANT * (next_z + b_recv[s0 + 2, 1])
                H[2, 2] = H[2, 2] - COURANT * (next_y + b_recv[s0 + 2, 0])

            @pl.when(b < STEPS - 1)
            def _():
                close_right()
                tell_right(s0 + 3, H[2, 1], H[2, 2])

            hear_left(2)
            k_c = CO[3, 0]
            E[0, 0] = AE[0]
            E[0, 1] = AE[1] + k_c * h_recv[s0 + 2, 1]
            E[0, 2] = AE[2] - k_c * h_recv[s0 + 2, 0]
            put(H, (0,), magnetic(0, true, (near_y, near_z)))
            inject(E, (0,), 0, values)

            @pl.when(b < STEPS - 1)
            def _():
                open_block(s0 + 3)

            mean = average()
            mean_send[b] = mean
            for index in range(STEPS):

                @pl.when(b == index)
                def _(index=index):
                    mean_copy(index).start()

            pl.when(b == STEPS - 1)(close_right)

            @pl.when(b == 0)
            def _():
                heard(jnp.logical_not(outer), gain_copy(0))
                g = table_recv[4]
                for c in range(3):
                    f_send[c] = jnp.where(f_cells, g * mean[c], 0.0)
                go(has_right, f_copy(0))
                go(has_left, f_copy(1))

            return carry

        lax.fori_loop(0, STEPS, block, 0)
        for k in range(4):
            write(k)
        for slot in range(STEPS * SUBS):
            sent(has_right, h_copy(slot))
            sent(has_left, b_copy(slot))
        sent(has_right, f_copy(0), d_copy(0))
        sent(has_left, f_copy(1), d_copy(1))
        for index in range(STEPS):
            mean_copy(index).wait_send()
        written()

    @pl.when(is_coarse)
    def _():
        step = STEP_COARSE
        load_off.wait()
        corner_y = off_ref[0]
        guess = (TE, TH, TQ, TJ)

        def cut(value):
            return pltpu.roll(value[:, depth - box_z : depth], width - corner_y, 0)[:box_y]

        row, column = iota((width, box_z), 0), iota((width, box_z), 1)
        interior = (row >= corner_y + 1) & (row <= corner_y + box_y - 2) & (column >= 1) & (column <= box_z - 2)

        def inside(p):
            return interior & (fine_at[p] >= 1) & (fine_at[p] <= n_slab - 2)

        def place(index):
            for p in range(PLANES):

                @pl.when(in_box[p])
                def _(p=p):
                    mean_arrival(index, p).wait_recv()
                    for c in range(3):
                        tall = jnp.concatenate([mean_recv[index, p, c]] * (width // box_y), axis=0)
                        placed = pltpu.roll(tall, corner_y, 0)
                        kept = E[p, c, :, depth - box_z : depth]
                        E[p, c, :, depth - box_z : depth] = jnp.where(inside(p), placed, kept)

        def box_part(value):
            return value[:, depth - box_z : depth]

        def with_row(rows, value, at):
            taken = jnp.sum(jnp.where(iota(value.shape, 0) == at, value, 0.0), axis=0, keepdims=True)
            return jnp.where(iota(rows.shape, 0) == 7, taken, rows)

        def packed(rows, columns):
            return fold(rows, pltpu.roll(columns, width - corner_y, 0)[:box_y])

        def emit(index, p, values, scale=None):
            rows, columns = ends([box_part(v) for v in values], corner_y)
            if scale is not None:
                lane = iota(columns.shape, 1)
                columns = jnp.where(lane == 6, scale[:, 0:1], columns)
                columns = jnp.where(lane == 7, scale[:, box_z - 1 : box_z], columns)
                rows = with_row(rows, scale, corner_y)
            pack_send[index, p, 0] = packed(rows, columns)

            @pl.when(in_box[p] & full_at[p])
            def _():
                for c in range(3):
                    sec_send[index, p, c] = cut(values[c])

        def emit_near(index, y, z):
            rim_send[index] = packed(*ends([None, box_part(z), -box_part(y)], corner_y))

            @pl.when(in_box[PLANES] & full_at[PLANES])
            def _():
                near_send[index, 0], near_send[index, 1] = cut(y), cut(z)

        def send(index):
            for p in range(PLANES):
                for k in (1, 0, 2):
                    go(reaches(p, k), pack_copy(index, p, k))
                if p == 0:
                    for k in range(3):
                        go(reaches(PLANES, k), rim_copy(index, k))
            for p in range(PLANES):
                go(in_box[p] & full_at[p], section_copy(index, p))
            go(in_box[PLANES] & full_at[PLANES], near_copy(index))

        def first_half(state, slot_h, slot_b):
            e, h, _, _ = state
            for p in (1, 2):
                oscillate(p, step, state)
            electric_whole(2, state)
            electric_whole(1, state)
            k_c = CO[3, 0]
            e[0, 0] = b_send[slot_b, 2]
            e[0, 1] = b_send[slot_b, 0] + k_c * h_recv[slot_h, 1]
            e[0, 2] = b_send[slot_b, 1] - k_c * h_recv[slot_h, 0]
            magnetic_whole(1, state)
            magnetic_whole(0, state)

        def second_half(state, slot_h, slot_b):
            heard(has_right, b_copy(slot_b))
            k_c = CR[3]
            ahead = (
                b_recv[slot_b, 0] + k_c * h_send[slot_h, 1],
                b_recv[slot_b, 1] - k_c * h_send[slot_h, 0],
            )
            put(state[1], (2,), magnetic(2, state, ahead))

        def guess_from(p):
            for c in range(3):
                value = E[p, c]
                TE[p, c] = value
                TE[p, c, :, depth - box_z : depth] = jnp.where(inside(p) & in_box[p], 0.0, box_part(value))
                TQ[p, c] = Q[p, c]
                TJ[p, c] = J[p, c]

        set_coefficients(step)
        wait_loads(*[(k, p) for k in range(4) for p in range(PLANES)])
        h_send[0, 0], h_send[0, 1] = H[2, 1], H[2, 2]
        oscillate(0, step, true)
        start = electric(0, true)
        set_b(0, start)
        emit_near(0, H[2, 1], H[2, 2])
        scale = box_part(CO[3, 0])
        for p in range(PLANES):
            rows, columns = ends([box_part(E[p, c]) for c in range(3)], corner_y)
            if p == 0:
                rows = with_row(rows, scale, corner_y + box_y - 1)
            pack_send[0, p, 1] = packed(rows, columns)

            @pl.when(in_box[p] & full_at[p])
            def _(p=p):
                for c in range(3):
                    table_send[p, c] = cut(E[p, c])

        emit(0, 0, start, scale)
        for p in (2, 1):
            oscillate(p, step, true)
            electric_whole(p, true)
            emit(0, p, get(E, p))
        prepare()
        pl.semaphore_wait(barrier, count(has_left, has_right, *listens))
        go(has_right, h_copy(0))
        go(has_left, b_copy(0), m_next)
        send(0)
        for p in range(PLANES):

            @pl.when(in_box[p])
            def _(p=p):
                table_send[p, 3] = cut(CO[3, p])
                table_send[p, 4] = 1.0 - cut(CO[4, p]) * cut(CO[2, p])
                go(full_at[p], table_copy(p))
                go(jnp.logical_not(full_at[p]), gain_copy(p))

        magnetic_whole(1, true)
        for p in (1, 2):
            guess_from(p)
            oscillate(p, step, guess)
        for c in range(3):
            TH[1, c] = H[1, c]
        heard(has_left, h_copy(0))
        k_c = CO[3, 0]
        E[0, 0] = start[0]
        E[0, 1] = b_send[0, 0] + k_c * h_recv[0, 1]
        E[0, 2] = b_send[0, 1] - k_c * h_recv[0, 0]
        magnetic_whole(0, true)
        guess_from(0)
        for c in range(3):
            TH[0, c] = H[0, c]
        oscillate(0, step, guess)
        start = electric(0, guess)
        tell_left(1, start)
        heard(has_right, m_next)
        sent(has_left, m_next)
        CR[3] = pick(m_right[0], [row[3] for row in tables(step)]) * has_right.astype(jnp.float32)
        second_half(true, 0, 0)
        tell_right(1, H[2, 1], H[2, 2])
        emit(1, 0, start)
        electric_whole(1, guess)
        emit(1, 1, get(TE, 1))
        emit_near(1, H[2, 1], H[2, 2])
        for c in range(3):
            TH[2, c] = H[2, c]
        electric_whole(2, guess)
        emit(1, 2, get(TE, 2))
        send(1)
        magnetic_whole(1, guess)
        for p in (1, 2):
            oscillate(p, step, guess)
        heard(has_left, h_copy(1))
        TE[0, 0] = b_send[1, 2]
        TE[0, 1] = b_send[1, 0] + k_c * h_recv[1, 1]
        TE[0, 2] = b_send[1, 1] - k_c * h_recv[1, 0]
        magnetic_whole(0, guess)
        oscillate(0, step, guess)
        emit(2, 0, electric(0, guess))
        emit(2, 1, electric(1, guess, (TH[0, 1], TH[0, 2])))
        second_half(guess, 1, 1)
        emit_near(2, TH[2, 1], TH[2, 2])
        emit(2, 2, electric(2, guess, (TH[1, 1], TH[1, 2])))
        send(2)

        place(0)
        oscillate(0, step, true)
        tell_left(2, electric(0, true))
        first_half(true, 1, 2)
        second_half(true, 1, 2)
        tell_right(2, H[2, 1], H[2, 2])
        place(1)
        oscillate(0, step, true)
        tell_left(3, electric(0, true))
        heard(has_left, h_copy(2))
        first_half(true, 2, 3)
        write(2)
        write(3)
        write(0)
        second_half(true, 2, 3)
        write(1)
        for slot in range(3):
            sent(has_right, h_copy(slot))
        for slot in range(4):
            sent(has_left, b_copy(slot))
        for p in range(PLANES):
            sent(in_box[p] & full_at[p], table_copy(p))
            sent(in_box[p] & jnp.logical_not(full_at[p]), gain_copy(p))
            sent(in_box[p] & full_at[p], *[section_copy(index, p) for index in range(STEPS)])
            for k in range(3):
                sent(reaches(p, k), *[pack_copy(index, p, k) for index in range(STEPS)])
        for k in range(3):
            sent(reaches(PLANES, k), *[rim_copy(index, k) for index in range(STEPS)])
        sent(in_box[PLANES] & full_at[PLANES], *[near_copy(index) for index in range(STEPS)])
        written()
        for p in range(PLANES):
            heard(in_box[p], mean_arrival(STEPS - 1, p))


def hand_over(n_slab, width, depth, off_in, mean_in, *refs):
    sources, targets = refs[:4], refs[4:8]
    off_ref, mean, held, load_sem, out_sem = refs[8:]
    loads = [pltpu.make_async_copy(sources[k].at[0], held.at[k], load_sem.at[k]) for k in range(4)]
    stores = [pltpu.make_async_copy(held.at[k], targets[k].at[0], out_sem.at[k]) for k in range(4)]
    load_off = pltpu.make_async_copy(off_in, off_ref, load_sem.at[4])
    load_mean = pltpu.make_async_copy(mean_in, mean, load_sem.at[5])
    load_off.start()
    load_mean.start()
    for load in loads:
        load.start()
    slab = lax.axis_index("slab")
    is_coarse = lax.axis_index("grid") == 0
    box_y, box_z = width // 3, depth // 3
    load_off.wait()
    load_mean.wait()
    corner_y = off_ref[0]
    row, column = iota((width, box_z), 0), iota((width, box_z), 1)
    interior = (row >= corner_y + 1) & (row <= corner_y + box_y - 2) & (column >= 1) & (column <= box_z - 2)
    loads[0].wait()
    for p in range(PLANES):
        fine = 3 * (slab - n_slab // 8) + p

        @pl.when(is_coarse & (fine >= 1) & (fine <= n_slab - 2))
        def _(p=p):
            for c in range(3):
                tall = jnp.concatenate([mean[p, c]] * (width // box_y), axis=0)
                placed = pltpu.roll(tall, corner_y, 0)
                kept = held[0, c, p, :, depth - box_z : depth]
                held[0, c, p, :, depth - box_z : depth] = jnp.where(interior, placed, kept)

    stores[0].start()
    for k in (1, 2, 3):
        loads[k].wait()
        stores[k].start()
    for store in stores:
        store.wait()


def on_device(n_slab, efield, hfield, polar, current, material, box_offset):
    planes, width, depth = efield.shape[2:]
    box = (width // 3, depth // 3)
    plane = (width, depth)
    f32 = jnp.float32
    dma = pltpu.SemaphoreType.DMA
    slots = STEPS * SUBS

    def room(*shape, dtype=f32):
        return pltpu.VMEM(shape, dtype)

    state = room(planes, 3, *plane)
    triple = room(3, *plane)
    scratch = [pltpu.SMEM((2,), jnp.int32)] + [state] * 8 + [
        room(planes, *plane, dtype=jnp.int32),
        room(5, planes, *plane),
        room(*plane, dtype=jnp.int32),
        room(2, *plane, dtype=jnp.int32),
        room(*plane),
        room(6, *plane),
    ]
    scratch += [triple] * 8
    scratch += [room(slots, 2, *plane), room(slots, 2, *plane), room(slots, 3, *plane), room(slots, 2, *plane)]
    scratch += [
        room(STEPS, planes, 3, *box),
        room(STEPS, 3, *box),
        room(planes, 5, *box),
        room(5, *box),
        room(STEPS, 2, *box),
        room(STEPS, 2, *box),
        room(2, 3, 3, *plane),
        room(6, *plane),
        state,
        state,
        state,
        room(2, 3, *plane),
        room(STEPS, 3, *box),
        room(STEPS - 1, planes, 3, *box),
        room(3, *box),
        room(2, 3, *box),
        room(STEPS, planes, 2, 8, box[1]),
        room(STEPS, 3, 2, 8, box[1]),
        room(STEPS, 8, box[1]),
        room(STEPS, 8, box[1]),
        room(3, *box),
        room(8, box[1]),
        room(2, 8, box[1]),
    ]
    scratch += [dma, dma((5, planes)), dma((4, planes)), dma((4,))]
    scratch += [dma((slots,))] * 4
    scratch += [dma((STEPS, planes)), dma((STEPS,)), dma((planes,)), dma, dma((STEPS,)), dma((STEPS,))]
    scratch += [dma((STEPS,)), dma((STEPS, planes)), dma((2,)), dma((2,))]
    scratch += [dma((STEPS, planes, 3)), dma((STEPS, 3)), dma((STEPS, 3)), dma((STEPS,))]
    scratch += [dma((2,)), dma((2,))]
    whole = pl.BlockSpec(memory_space=pl.ANY)
    fields = [jax.ShapeDtypeStruct(efield.shape, f32)] * 4
    state = pl.pallas_call(
        functools.partial(kernel, n_slab, width, depth),
        out_shape=fields + [jax.ShapeDtypeStruct((planes, 3, *box), f32)],
        in_specs=[whole] * 6,
        out_specs=[whole] * 5,
        scratch_shapes=scratch,
        compiler_params=pltpu.CompilerParams(
            collective_id=1, has_side_effects=True, vmem_limit_bytes=60 * 1024 * 1024
        ),
    )(box_offset, efield, hfield, polar, current, material)
    *state, mean = state
    return pl.pallas_call(
        functools.partial(hand_over, n_slab, width, depth),
        out_shape=fields,
        in_specs=[whole] * 6,
        out_specs=[whole] * 4,
        scratch_shapes=[
            pltpu.SMEM((2,), jnp.int32),
            room(planes, 3, *box),
            room(4, 3, planes, *plane),
            dma((6,)),
            dma((4,)),
        ],
        compiler_params=pltpu.CompilerParams(vmem_limit_bytes=60 * 1024 * 1024),
    )(box_offset, mean, *state)


def solution(mesh):
    field = P("grid", "angle", "slab", None, None)
    return jax.shard_map(
        functools.partial(on_device, mesh.shape["slab"]),
        mesh=mesh,
        in_specs=(field, field, field, field, P("grid", "slab", None, None), P()),
        out_specs=(field, field, field, field),
        check_vma=False,
    )
```
